32 devices in a mesh: rep: 2 (over y), seq: 4 (over z), shot: 4 (over x, core).
Axes of the slice: x: 2, y: 2, z: 4, core: 2. Of those that a mesh axis runs over, the one named last changes fastest.
Arguments:
- queries: bfloat16 [8192, 1536], P(('rep', 'seq'), 'shot'), parts along dimension 0, may hold values from -6.5 to 6.5
- key_rows: bfloat16 [8192, 1536], P(('rep', 'seq'), 'shot'), parts along dimension 0, may hold values from -6.5 to 6.5
- value_rows: bfloat16 [8192, 1536], P(('rep', 'seq'), 'shot'), parts along dimension 0, may hold values from -6 to 6
- text_keys: bfloat16 [512, 1536], P('rep', 'shot'), parts along dimension 0, may hold values from -6 to 6
- text_values: bfloat16 [512, 1536], P('rep', 'shot'), parts along dimension 0, may hold values from -6 to 6
- shot_of_stretch: int32 [16], P('rep'), parts along dimension 0, may hold values from 0 to 3, never falling along the last dimension, each value on 1 to 4 neighbouring positions
- anchor_stretch: int32 [8], P('rep'), parts along dimension 0, may hold values from 0 to 7
- context_count: int32 [16], P('rep'), parts along dimension 0, may hold values from 0 to 4, as said below
- context_ids: int32 [16, 4], P('rep'), parts along dimension 0, may hold values from 0 to 7, as said below
Outputs:
- attended: bfloat16 [8192, 1536], P(('rep', 'seq'), 'shot'), parts along dimension 0
The draws below stay inside these ranges and needn't reach their ends.
There are 2 independent parts, one for each index of `rep`. The reference program is written for one: setup_inputs(seed, part) draws one part's arguments, and reference() takes and returns one part's arrays. A program takes and returns all parts, laid end to end along the dimension named above; each array names one. Nothing has to cross between parts.
Inputs may be any that keep to these rules, and one draw needn't show every extreme that they name: `context_count`: query stretch 0 has no live entries. Entries of context_ids[c] at positions at or beyond context_count[c] are never read. The live entries of stretch c are distinct, differ from c, and name stretches e with |e // 2 - c // 2| <= 2. Over all live entries of the query stretches g * 2 to (g + 1) * 2 - 1, at most one stretch of each other aligned block of 2 stretches is named. `shot_of_stretch`: shot numbers never fall from one stretch to the next.
All inputs are finite; a program needn't handle non-finite values.
Results may differ from the reference program's by a relative error of at most 0.0085.
Values may be sent and summed in bfloat16 or wider, within the bound.
No kernel may reach another device: no remote copies, remote signals or barrier semaphores. Data moves between devices by JAX's collectives and lax.ppermute only.
A program may use at most 128 MiB of HBM per device.

```python
import math
import jax
import jax.numpy as jnp
import numpy as np
from jax import lax

HEADS = 12
HD = 128
STRETCH = 512
TEXT = 256
REACH = 2
SHOTS = 4
STRETCH_DEV = 2
NCHUNK = 8
TOKENS = 4096
MAXCTX = 4


def draw_queries(key, part):
    key = jax.random.fold_in(key, 7)
    values = jnp.clip(jax.random.normal(key, (TOKENS, HEADS * HD), jnp.float32), -6.5, 6.5)
    return values.astype(jnp.bfloat16)


def draw_key_rows(key, part):
    key = jax.random.fold_in(key, 11)
    values = jnp.clip(jax.random.normal(key, (TOKENS, HEADS * HD), jnp.float32), -6.5, 6.5)
    return values.astype(jnp.bfloat16)


def routing(key):
    groups = NCHUNK // STRETCH_DEV
    span = 2 * REACH
    candidate_width = STRETCH_DEV - 1 + span
    subkeys = jax.random.split(key, 6)
    stretch_index = jnp.arange(NCHUNK, dtype=jnp.int32)
    reader = stretch_index // STRETCH_DEV
    place_in = stretch_index % STRETCH_DEV
    picked = jax.random.randint(subkeys[0], (groups, span), 0, STRETCH_DEV)
    own_step = jnp.arange(STRETCH_DEV - 1, dtype=jnp.int32) + 1
    own_ids = reader[:, None] * STRETCH_DEV + (place_in[:, None] + own_step[None, :]) % STRETCH_DEV
    offsets = jnp.concatenate([jnp.arange(-REACH, 0, dtype=jnp.int32), jnp.arange(1, REACH + 1, dtype=jnp.int32)])
    owners = reader[:, None] + offsets[None, :]
    near_ok = (owners >= 0) & (owners < groups)
    near_ids = owners * STRETCH_DEV + picked[reader]
    candidate = jnp.concatenate([own_ids, near_ids], axis=1)
    usable = jnp.concatenate([jnp.ones((NCHUNK, STRETCH_DEV - 1), dtype=bool), near_ok], axis=1)
    scores = jax.random.randint(subkeys[1], (NCHUNK, candidate_width), 0, 2 ** 20) * candidate_width
    scores = scores + jnp.arange(candidate_width, dtype=jnp.int32)[None, :]
    scores = scores + jnp.where(usable, 2 ** 20 * candidate_width, 0)
    ranking = jnp.argsort(-scores, axis=1)
    ordered = jnp.take_along_axis(candidate, ranking, axis=1)
    available = jnp.sum(usable.astype(jnp.int32), axis=1)
    heaviness = jax.random.randint(subkeys[2], (groups,), 2, MAXCTX + 1)
    ceiling = jnp.minimum(heaviness[reader], available)
    counts = jax.random.randint(subkeys[3], (NCHUNK,), 0, ceiling + 1)
    lowest = max(1, min(REACH, groups - 1 - REACH))
    highest = min(groups - 1, max(REACH, groups - 1 - REACH))
    forced = jax.random.randint(subkeys[4], (), lowest, highest + 1) * STRETCH_DEV
    counts = jnp.where(stretch_index == forced, MAXCTX, counts)
    counts = jnp.where(stretch_index == 0, 0, counts)
    filler = jax.random.randint(subkeys[5], (NCHUNK, MAXCTX), 0, NCHUNK)
    filler = filler.at[0, 0].set(0).at[0, 1].set(NCHUNK - 1)
    listed = jnp.where(jnp.arange(MAXCTX, dtype=jnp.int32)[None, :] < counts[:, None], ordered[:, :MAXCTX], filler)
    return (listed.astype(jnp.int32), counts.astype(jnp.int32))


def draw_context_ids(key, part):
    listed, counts = routing(key)
    return listed


def draw_context_count(key, part):
    listed, counts = routing(key)
    return counts


def place_ends(values, key, least, high):
    longest = values.shape.index(max(values.shape))
    spots = []
    for shift in (0, 1):
        where = [jax.random.randint(jax.random.fold_in(key, axis), (), 0, length) for axis, length in enumerate(values.shape)]
        where[longest] = (where[longest] + shift) % values.shape[longest]
        spots.append(tuple(where))
    return values.at[spots[0]].set(least).at[spots[1]].set(high)


def shard_levels(rng, extent, cuts, least, top_value):
    factor_of = 1.0
    for dim, parts in cuts:
        steps = jax.random.uniform(jax.random.fold_in(jax.random.fold_in(rng, 6), dim), (parts,), jnp.float32, least / len(cuts), top_value / len(cuts))
        factor_of = factor_of * jnp.repeat(jnp.exp(steps), extent[dim] // parts).reshape((-1,) + (1,) * (len(extent) - 1 - dim))
    return factor_of


def length_profile(count, total, limit, skew):
    loads = [(1 << 20) // math.isqrt(rank ** skew) + 1 for rank in range(2, count + 1)]
    rest, given = total - limit - (count - 1), [1] * (count - 1)
    while rest > 0:
        movable = [i for i in range(count - 1) if given[i] < limit]
        mass, remaining = sum([loads[i] for i in movable]), rest
        for i in movable:
            addition = min(limit - given[i], max(1, remaining * loads[i] // mass), rest)
            given[i] = given[i] + addition
            rest = rest - addition
    return np.array([limit] + given)


def uneven(stream_key, amount, total, bound, skew):
    if amount == 2:
        one = jax.random.randint(stream_key, (), max(1, total - bound), min(bound, total - 1) + 1)
        return jnp.stack([one, total - one])
    lengths = jnp.asarray(length_profile(amount, total, bound, skew), jnp.int32)
    twos = (amount - 1) // 2
    giver, receiver = lengths[1:1 + 2 * twos:2], lengths[2:2 + 2 * twos:2]
    room = jnp.minimum(giver - 1, bound - receiver)
    passed = jax.random.randint(jax.random.fold_in(stream_key, 1), (twos,), 0, 1 << 20) % (room + 1)
    lengths = lengths.at[1:1 + 2 * twos:2].set(giver - passed).at[2:2 + 2 * twos:2].set(receiver + passed)
    return lengths[jax.random.permutation(jax.random.fold_in(stream_key, 2), amount)]


def normal_values(rng, shape, width, bound, pieces=(), held_as=jnp.bfloat16):
    values = jax.random.normal(rng, shape, jnp.float32) * width
    if len(pieces) > 0:
        values = shard_levels(rng, shape, pieces, -0.22, 0.18) * values
    return jnp.clip(values, min=-bound, max=bound).astype(held_as)


def setup_inputs(seed: int = 0, part: int = 0) -> dict:
    key_of = jax.random.split(jax.random.key(seed), 10)
    part_splits = jax.random.split(jax.random.fold_in(key_of[9], part), 10)
    return {
        "queries": draw_queries(jax.random.fold_in(jax.random.fold_in(key_of[9], part), 71), part),
        "key_rows": draw_key_rows(jax.random.fold_in(jax.random.fold_in(key_of[9], part), 71), part),
        "value_rows": normal_values(part_splits[2], (TOKENS, HEADS * HD), 1.0, 6.0, ((0, 4), (1, 4))),
        "text_keys": normal_values(part_splits[3], (TEXT, HEADS * HD), 1.0, 6.0, ((1, 4),)),
        "text_values": normal_values(part_splits[4], (TEXT, HEADS * HD), 1.0, 6.0, ((1, 4),)),
        "shot_of_stretch": jnp.searchsorted(jnp.cumsum(uneven(part_splits[5], SHOTS, NCHUNK, NCHUNK // 2, 1)), jnp.arange(NCHUNK), side="right").astype(jnp.int32),
        "anchor_stretch": place_ends(jax.random.randint(part_splits[6], (SHOTS,), 0, NCHUNK), jax.random.fold_in(part_splits[6], 1), 0, NCHUNK - 1).astype(jnp.int32),
        "context_count": draw_context_count(jax.random.fold_in(jax.random.fold_in(key_of[9], part), 71), part),
        "context_ids": draw_context_ids(jax.random.fold_in(jax.random.fold_in(key_of[9], part), 71), part),
    }


def attend(own_queries, key_block, value_block):
    head_count = own_queries.shape[1] // HD
    query_heads = own_queries.reshape(own_queries.shape[0], head_count, HD).astype(jnp.float32)
    key_heads = key_block.reshape(key_block.shape[0], head_count, HD).astype(jnp.float32)
    value_heads = value_block.reshape(value_block.shape[0], head_count, HD).astype(jnp.float32)
    scores = jnp.einsum("qhd,khd->hqk", query_heads, key_heads) * (HD ** -0.5)
    row_peak = jnp.max(scores, axis=2)
    exp_scores = jnp.exp(scores - row_peak[:, :, None])
    row_total = jnp.sum(exp_scores, axis=2)
    weights = lax.optimization_barrier(exp_scores.astype(jnp.bfloat16)).astype(jnp.float32)
    mixture = jnp.einsum("hqk,khd->qhd", weights, value_heads)
    mixture = mixture / jnp.transpose(row_total)[:, :, None]
    return mixture.reshape(own_queries.shape[0], -1).astype(jnp.bfloat16), row_peak + jnp.log(row_total)


def scaled(matrix, factors):
    row_count = matrix.shape[0]
    head_count = factors.shape[0]
    return (matrix.reshape(row_count, head_count, -1) * jnp.transpose(factors)[:, :, None]).reshape(row_count, -1)


def opening(result):
    partial_value, lse = result
    return (lse, partial_value.astype(jnp.float32), jnp.ones_like(lse))


def absorb(running, result):
    row_peak, weighted, row_weight = running
    partial_value, lse = result
    new_peak = jnp.maximum(row_peak, lse)
    keep_old = jnp.exp(row_peak - new_peak)
    take_new = jnp.exp(lse - new_peak)
    weighted = scaled(weighted, keep_old) + scaled(partial_value.astype(jnp.float32), take_new)
    return (new_peak, weighted, row_weight * keep_old + take_new)


def finish(running):
    row_peak, weighted, row_weight = running
    return scaled(weighted, 1.0 / row_weight).astype(jnp.bfloat16)


def reference(queries, key_rows, value_rows, text_keys, text_values, shot_of_stretch, anchor_stretch, context_count, context_ids):
    columns = queries.shape[1]
    query_blocks = queries.reshape(NCHUNK, STRETCH, columns)
    key_blocks = key_rows.reshape(NCHUNK, STRETCH, columns)
    value_blocks = value_rows.reshape(NCHUNK, STRETCH, columns)

    def per_stretch(stretch_index):
        own_queries = query_blocks[stretch_index]
        running = opening(attend(own_queries, text_keys, text_values))
        running = absorb(running, attend(own_queries, key_blocks[stretch_index], value_blocks[stretch_index]))
        anchor = anchor_stretch[shot_of_stretch[stretch_index]]
        running = absorb(running, attend(own_queries, key_blocks[anchor], value_blocks[anchor]))
        for slot_index in range(MAXCTX):
            context_id = context_ids[stretch_index, slot_index]
            candidate = absorb(running, attend(own_queries, key_blocks[context_id], value_blocks[context_id]))
            is_live = slot_index < context_count[stretch_index]
            running = jax.tree.map(lambda updated, previous: jnp.where(is_live, updated, previous), candidate, running)
        return finish(running)

    attended = lax.map(per_stretch, jnp.arange(NCHUNK, dtype=jnp.int32))
    return attended.reshape(NCHUNK * STRETCH, columns)
```

```python
import functools
import math

import jax
import jax.numpy as jnp
from jax import lax
from jax.experimental import pallas as pl
from jax.experimental.pallas import tpu as pltpu
from jax.sharding import PartitionSpec as P

HD = 128
STRETCH = 512
STRETCH_DEV = 2
ROUNDS = (3, 4)
ROW = 8
HEADER = 8
TILE = 256
EXPONENT = HD ** (-0.5) * math.log2(math.e)
ANY = pl.BlockSpec(memory_space=pl.ANY)
SMEM = pl.BlockSpec(memory_space=pltpu.SMEM)
VMEM = pl.BlockSpec(memory_space=pltpu.VMEM)


def plan_kernel(
    groups, cap, shot, anchor, count, ids, keys, values,
    plan, key_up, key_down, value_up, value_down,
    dest, place, hold, stamp, times, best, sems,
):
    total = STRETCH_DEV * groups
    slots = ids.shape[1]
    small = total <= 16
    bits = total.bit_length()
    me = lax.axis_index("seq")
    mine = (me, groups - 1 - me)

    def each(length, body):
        if small:
            for i in range(length):
                body(i)
        else:
            lax.fori_loop(0, length, lambda i, c: (body(i), c)[1], 0)

    def clear(e):
        g = e >> 1
        dest[e] = g
        dest[total + e] = groups - 1 - g
        times[e] = 0
        times[total + e] = 0

    each(total, clear)

    def stand(e):
        g = e >> 1
        for d, at in enumerate((g, groups - 1 - g)):
            place[d * total + e] = at
            hold[d * total + e] = e & 1
            stamp[d * total + e] = -1

    each(total, stand)

    def read(c):
        g = c >> 1

        def entry(e):
            dest[e] = jnp.maximum(dest[e], g)
            dest[total + e] = jnp.maximum(dest[total + e], groups - 1 - g)

        entry(anchor[shot[c]])
        live = count[c]
        for s in range(slots):
            entry(jnp.where(s < live, ids[c, s], c))

    each(total, read)

    for q in range(STRETCH_DEV):
        c = STRETCH_DEV * me + q

        def one(e, amount, q=q):
            times[q * total + e] = times[q * total + e] + amount

        one(c, 1)
        one(anchor[shot[c]], 1)
        live = count[c]
        for s in range(slots):
            alive = s < live
            one(jnp.where(alive, ids[c, s], c), jnp.where(alive, 1, 0))

    for q in range(STRETCH_DEV):
        for j in range(STRETCH_DEV):
            plan[1 + 2 * q + j] = times[q * total + STRETCH_DEV * me + j]
    for i in range(ROW * ROUNDS[-1]):
        plan[HEADER + i] = 0

    def remaining():
        return lax.fori_loop(
            0, 2 * total, lambda e, s: s + dest[e] - place[e], jnp.int32(0), unroll=small
        )

    def a_round(r, transit):
        moves = jnp.int32(0)
        for d in range(2):
            base = d * total
            for k in range(groups) if small else ():
                best[k] = -1
            if not small:
                each(groups, lambda k: best.__setitem__(k, jnp.int32(-1)))

            def rank(e, base=base):
                at = place[base + e]
                to = dest[base + e]
                key = (to << bits) | e
                if transit:
                    key = jnp.where(stamp[base + e] == r, key + (groups << bits), key)
                best[at] = jnp.maximum(best[at], jnp.where(to > at, key, -1))

            each(total, rank)
            sent = best[mine[d]]
            mask = (1 << bits) - 1
            plan[HEADER + r * ROW + d] = jnp.where(sent < 0, 0, hold[base + (jnp.maximum(sent, 0) & mask)])
            came = jnp.where(mine[d] > 0, best[jnp.maximum(mine[d] - 1, 0)], -1)
            come = jnp.maximum(came, 0) & mask
            for q in range(STRETCH_DEV):
                plan[HEADER + r * ROW + 2 + 2 * d + q] = jnp.where(came < 0, 0, times[q * total + come])

            @pl.when(came >= 0)
            def _(come=come, base=base):
                hold[base + come] = 2 + r

            def move(k, base=base):
                key = best[k]

                @pl.when(key >= 0)
                def _():
                    e = key & mask
                    place[base + e] = k + 1
                    stamp[base + e] = r + 1

                return jnp.where(key >= 0, 1, 0)

            if small:
                for k in range(groups - 1):
                    moves += move(k)
            else:
                moves += lax.fori_loop(0, groups - 1, lambda k, s: s + move(k), jnp.int32(0))
        return moves

    hops = remaining()
    left = hops - a_round(0, False)
    copies = []
    for i, (source, target, d) in enumerate(
        ((keys, key_up, 0), (keys, key_down, 1), (values, value_up, 0), (values, value_down, 1))
    ):
        start = pl.multiple_of(plan[HEADER + d] * STRETCH, STRETCH)
        copy = pltpu.make_async_copy(source.at[pl.ds(start, STRETCH)], target, sems.at[i])
        copy.start()
        copies.append(copy)

    def go_on(carry):
        return (carry[1] > 0) & (carry[0] < cap)

    rounds, _ = lax.while_loop(
        go_on, lambda c: (c[0] + 1, c[1] - a_round(c[0], False)), (jnp.int32(1), left)
    )
    plan[0] = rounds
    plan[5] = rounds
    for copy in copies:
        copy.wait()

    @pl.when(rounds > ROUNDS[-1])
    def _():
        each(total, stand)
        again, _ = lax.while_loop(
            go_on, lambda c: (c[0] + 1, c[1] - a_round(c[0], True)), (jnp.int32(0), hops)
        )
        plan[5] = again


def make_plan(groups, tables, keys, values):
    total = STRETCH_DEV * groups
    cap = 2 * groups + 16
    block = jax.ShapeDtypeStruct((STRETCH, keys.shape[1]), keys.dtype)
    return pl.pallas_call(
        functools.partial(plan_kernel, groups, cap),
        out_shape=[jax.ShapeDtypeStruct((HEADER + cap * ROW,), jnp.int32)] + [block] * 4,
        in_specs=[SMEM] * 4 + [ANY] * 2,
        out_specs=[SMEM] + [ANY] * 4,
        scratch_shapes=[pltpu.SMEM((2 * total,), jnp.int32) for _ in range(5)]
        + [pltpu.SMEM((groups,), jnp.int32), pltpu.SemaphoreType.DMA((4,))],
        name="plan",
    )(*tables, keys, values)


def choose_kernel(row, arrivals, plan, *refs):
    if row is None:
        at, own, *refs = refs
        base = HEADER + at[0] * ROW
    else:
        own, *refs = refs
        base = HEADER + row * ROW
    came, outs, sems = refs[: 2 * arrivals], refs[2 * arrivals : 2 * arrivals + 2], refs[-1]
    for d in range(2):
        choice = plan[base + d]

        @pl.when(choice < STRETCH_DEV)
        def _(d=d, choice=choice):
            start = pl.multiple_of(choice * STRETCH, STRETCH)
            pltpu.make_async_copy(own.at[pl.ds(start, STRETCH)], outs[d], sems.at[d]).start()

        for i in range(arrivals):
            picked = choice == STRETCH_DEV + i if row is not None else choice >= STRETCH_DEV

            @pl.when(picked)
            def _(d=d, i=i):
                pltpu.make_async_copy(came[d * arrivals + i], outs[d], sems.at[d]).start()

    for d in range(2):
        pltpu.make_async_copy(own.at[pl.ds(0, STRETCH)], outs[d], sems.at[d]).wait()


def choose(plan, row, own, up, down):
    static = isinstance(row, int)
    block = jax.ShapeDtypeStruct((STRETCH, own.shape[1]), own.dtype)
    size = block.size * 2
    return pl.pallas_call(
        functools.partial(choose_kernel, row if static else None, len(up)),
        out_shape=[block] * 2,
        in_specs=[SMEM] + ([] if static else [SMEM]) + [ANY] * (1 + 2 * len(up)),
        out_specs=[ANY] * 2,
        scratch_shapes=[pltpu.SemaphoreType.DMA((2,))],
        cost_estimate=pl.CostEstimate(flops=0, bytes_accessed=4 * size, transcendentals=0),
        name="choose",
    )(plan, *(() if static else (row,)), own, *up, *down)


def attend_kernel(blocks, row, first, last, *refs):
    refs = list(refs)
    plan = refs.pop(0)
    base = HEADER + (refs.pop(0)[0] if row is None else row) * ROW
    queries = refs.pop(0)
    block_refs = [(refs.pop(0), refs.pop(0)) for _ in blocks]
    rows, columns = queries.shape
    heads = columns // HD
    if not first:
        acc_in, stat_in = refs.pop(0), refs.pop(0)
    if last:
        out, acc, stat = refs
    else:
        acc, stat = refs
    per_stretch = STRETCH // TILE

    if not first:
        def load(t, c):
            at = pl.ds(pl.multiple_of(t * TILE, TILE), TILE)
            acc[at, :] = acc_in[at, :]
            stat[at, :] = stat_in[at, :]
            return c

        lax.fori_loop(0, rows // TILE, load, 0)

    for number, ((start, length, weight_at), (key_ref, value_ref)) in enumerate(zip(blocks, block_refs)):
        opening = first and number == 0

        def step(t, at, weight, start=start, length=length, key_ref=key_ref, value_ref=value_ref, opening=opening):
            ones = jnp.ones((length, HD), jnp.bfloat16)
            for h in range(heads):
                cols = pl.ds(h * HD, HD)
                scores = lax.dot_general(
                    queries[at, cols], key_ref[pl.ds(start, length), cols],
                    (((1,), (1,)), ((), ())), preferred_element_type=jnp.float32,
                )
                peak = jnp.max(scores, axis=1, keepdims=True)
                if not opening:
                    before = stat[at, h : h + 1]
                    peak = jnp.maximum(peak, before)
                    keep = jnp.exp2((before - peak) * EXPONENT)
                weights = jnp.exp2((scores - peak) * EXPONENT).astype(jnp.bfloat16)
                wide = jnp.concatenate([value_ref[pl.ds(start, length), cols], ones], axis=1)
                both = jnp.dot(weights, wide, preferred_element_type=jnp.float32)
                if not opening:
                    both = both * weight
                mixed, mass = both[:, :HD], both[:, HD : HD + 1]
                if not opening:
                    mixed = mixed + acc[at, cols] * keep
                    mass = mass + stat[at, heads + h : heads + h + 1] * keep
                acc[at, cols] = mixed
                stat[at, h : h + 1] = peak
                stat[at, heads + h : heads + h + 1] = mass

        def tile(t, c, weight_at=weight_at, opening=opening, step=step):
            at = pl.ds(pl.multiple_of(t * TILE, TILE), TILE)
            if opening:
                step(t, at, None)
                return c
            q = t // per_stretch
            where = (base if weight_at[0] else 0) + weight_at[1] + weight_at[2] * q
            times = plan[where]

            @pl.when(times > 0)
            def _():
                step(t, at, times.astype(jnp.float32))

            return c

        lax.fori_loop(0, rows // TILE, tile, 0)

    if last:
        def finish(t, c):
            at = pl.ds(pl.multiple_of(t * TILE, TILE), TILE)
            for h in range(heads):
                cols = pl.ds(h * HD, HD)
                share = 1.0 / stat[at, heads + h : heads + h + 1]
                out[at, cols] = (acc[at, cols] * share).astype(out.dtype)
            return c

        lax.fori_loop(0, rows // TILE, finish, 0)


def attend(plan, row, queries, blocks, state, last):
    static = isinstance(row, int)
    rows, columns = queries.shape
    acc = jax.ShapeDtypeStruct((rows, columns), jnp.float32)
    stat = jax.ShapeDtypeStruct((rows, HD), jnp.float32)
    keys = sum(b[3] for b in blocks)
    scratch, outs = [], [acc, stat]
    if last:
        scratch = [pltpu.VMEM(acc.shape, acc.dtype), pltpu.VMEM(stat.shape, stat.dtype)]
        outs = [jax.ShapeDtypeStruct((rows, columns), queries.dtype)]
    operands = [plan] + ([] if static else [row])
    smem = len(operands)
    operands.append(queries)
    for b in blocks:
        operands += [b[0], b[1]]
    if state is not None:
        operands += list(state)
    result = pl.pallas_call(
        functools.partial(
            attend_kernel, [tuple(b[2:]) for b in blocks], row if static else None, state is None, last
        ),
        out_shape=outs,
        in_specs=[SMEM] * smem + [VMEM] * (len(operands) - smem),
        out_specs=[VMEM] * len(outs),
        scratch_shapes=scratch,
        compiler_params=pltpu.CompilerParams(vmem_limit_bytes=40 * 1024 * 1024),
        cost_estimate=pl.CostEstimate(
            flops=4 * rows * columns * keys, bytes_accessed=8 * rows * columns,
            transcendentals=rows * columns // HD * keys,
        ),
        name="attend",
    )(*operands)
    return result[0] if last else tuple(result)


def own_blocks(text_keys, text_values, keys, values):
    blocks = [(text_keys, text_values, 0, text_keys.shape[0], None)]
    for j in range(STRETCH_DEV):
        blocks.append((keys, values, j * STRETCH, STRETCH, (False, 1 + j, 2)))
    return blocks


def came_blocks(key_up, value_up, key_down, value_down):
    return [
        (key_up, value_up, 0, STRETCH, (True, 2, 1)),
        (key_down, value_down, 0, STRETCH, (True, 4, 1)),
    ]


def send(up, down):
    last = lax.axis_size("seq") - 1
    return (
        lax.ppermute(up, "seq", [(i, i + 1) for i in range(last)]),
        lax.ppermute(down, "seq", [(i + 1, i) for i in range(last)]),
    )


def exchange(rounds, plan, queries, text_keys, text_values, keys, values, key_first, value_first):
    key_came, value_came = ([], []), ([], [])
    key_next, value_next = key_first, value_first
    state = attend(plan, 0, queries, own_blocks(text_keys, text_values, keys, values), None, False)
    for r in range(rounds):
        for came, block in zip(key_came, send(*key_next)):
            came.append(block)
        for came, block in zip(value_came, send(*value_next)):
            came.append(block)
        if r + 1 < rounds:
            key_next = choose(plan, r + 1, keys, *key_came)
            value_next = choose(plan, r + 1, values, *value_came)
        blocks = came_blocks(key_came[0][r], value_came[0][r], key_came[1][r], value_came[1][r])
        state = attend(plan, r, queries, blocks, state, r + 1 == rounds)
    return state


def long_exchange(plan, queries, text_keys, text_values, keys, values, key_first, value_first):
    state = attend(plan, 0, queries, own_blocks(text_keys, text_values, keys, values), None, False)

    def body(carry):
        r, key_came, value_came, state = carry
        row = r.reshape(1)
        key_came = send(*choose(plan, row, keys, [key_came[0]], [key_came[1]]))
        value_came = send(*choose(plan, row, values, [value_came[0]], [value_came[1]]))
        blocks = came_blocks(key_came[0], value_came[0], key_came[1], value_came[1])
        state = attend(plan, row, queries, blocks, state, False)
        return (r + 1, key_came, value_came, state)

    carry = (jnp.int32(0), tuple(key_first), tuple(value_first), state)
    _, _, _, (acc, stat) = lax.while_loop(lambda c: c[0] < plan[5], body, carry)
    heads = queries.shape[1] // HD
    mass = jnp.repeat(stat[:, heads : 2 * heads], HD, axis=1)
    return (acc / mass).astype(queries.dtype)


def shards(
    queries, key_rows, value_rows, text_keys, text_values,
    shot_of_stretch, anchor_stretch, context_count, context_ids,
):
    groups = lax.axis_size("seq")
    tables = (shot_of_stretch, anchor_stretch, context_count, context_ids)
    plan, key_up, key_down, value_up, value_down = make_plan(groups, tables, key_rows, value_rows)
    branches = [functools.partial(exchange, rounds) for rounds in ROUNDS] + [long_exchange]
    index = sum((plan[0] > rounds).astype(jnp.int32) for rounds in ROUNDS)
    return lax.switch(
        index, branches, plan, queries, text_keys, text_values, key_rows, value_rows,
        (key_up, key_down), (value_up, value_down),
    )


def solution(mesh):
    return jax.shard_map(
        shards,
        mesh=mesh,
        in_specs=(
            P(("rep", "seq"), "shot"),
            P(("rep", "seq"), "shot"),
            P(("rep", "seq"), "shot"),
            P("rep", "shot"),
            P("rep", "shot"),
            P("rep"),
            P("rep"),
            P("rep"),
            P("rep", None),
        ),
        out_specs=P(("rep", "seq"), "shot"),
        check_vma=False,
    )
```

```python
import functools
import math

import jax
import jax.numpy as jnp
from jax import lax
from jax.experimental import pallas as pl
from jax.experimental.pallas import tpu as pltpu
from jax.sharding import PartitionSpec as P

HD = 128
STRETCH = 512
STRETCH_DEV = 2
ROUNDS = (3, 4)
ROW = 8
HEADER = 8
TILE = 256
EXPONENT = HD ** (-0.5) * math.log2(math.e)
SMEM = pl.BlockSpec(memory_space=pltpu.SMEM)
VMEM = pl.BlockSpec(memory_space=pltpu.VMEM)


def plan_kernel(
    groups, cap, shot, anchor, count, ids, keys,
    plan, branch, key_up, key_down,
    dest, place, hold, stamp, times, best,
):
    total = STRETCH_DEV * groups
    slots = ids.shape[0]
    small = total <= 16
    bits = total.bit_length()
    me = lax.axis_index("seq")
    mine = (me, groups - 1 - me)

    def each(length, body):
        if small:
            for i in range(length):
                body(i)
        else:
            lax.fori_loop(0, length, lambda i, c: (body(i), c)[1], 0)

    def clear(e):
        g = e >> 1
        dest[e] = g
        dest[total + e] = groups - 1 - g
        times[e] = 0
        times[total + e] = 0

    each(total, clear)

    def stand(e):
        g = e >> 1
        for d, at in enumerate((g, groups - 1 - g)):
            place[d * total + e] = at
            hold[d * total + e] = e & 1
            stamp[d * total + e] = -1

    each(total, stand)

    def read(c):
        g = c >> 1

        def entry(e):
            dest[e] = jnp.maximum(dest[e], g)
            dest[total + e] = jnp.maximum(dest[total + e], groups - 1 - g)

        entry(anchor[shot[c]])
        live = count[c]
        for s in range(slots):
            entry(jnp.where(s < live, ids[s, c], c))

    each(total, read)

    for q in range(STRETCH_DEV):
        c = STRETCH_DEV * me + q

        def one(e, amount, q=q):
            times[q * total + e] = times[q * total + e] + amount

        one(c, 1)
        one(anchor[shot[c]], 1)
        live = count[c]
        for s in range(slots):
            alive = s < live
            one(jnp.where(alive, ids[s, c], c), jnp.where(alive, 1, 0))

    for q in range(STRETCH_DEV):
        for j in range(STRETCH_DEV):
            plan[1 + 2 * q + j] = times[q * total + STRETCH_DEV * me + j]
    for i in range(ROW * ROUNDS[-1]):
        plan[HEADER + i] = 0

    def remaining():
        return lax.fori_loop(
            0, 2 * total, lambda e, s: s + dest[e] - place[e], jnp.int32(0), unroll=small
        )

    def a_round(r, transit):
        moves = jnp.int32(0)
        for d in range(2):
            base = d * total
            for k in range(groups) if small else ():
                best[k] = -1
            if not small:
                each(groups, lambda k: best.__setitem__(k, jnp.int32(-1)))

            def rank(e, base=base):
                at = place[base + e]
                to = dest[base + e]
                key = (to << bits) | e
                if transit:
                    key = jnp.where(stamp[base + e] == r, key + (groups << bits), key)
                best[at] = jnp.maximum(best[at], jnp.where(to > at, key, -1))

            each(total, rank)
            sent = best[mine[d]]
            mask = (1 << bits) - 1
            plan[HEADER + r * ROW + d] = jnp.where(sent < 0, 0, hold[base + (jnp.maximum(sent, 0) & mask)])
            came = jnp.where(mine[d] > 0, best[jnp.maximum(mine[d] - 1, 0)], -1)
            come = jnp.maximum(came, 0) & mask
            for q in range(STRETCH_DEV):
                plan[HEADER + r * ROW + 2 + 2 * d + q] = jnp.where(came < 0, 0, times[q * total + come])

            @pl.when(came >= 0)
            def _(come=come, base=base):
                hold[base + come] = 2 + r

            def move(k, base=base):
                key = best[k]

                @pl.when(key >= 0)
                def _():
                    e = key & mask
                    place[base + e] = k + 1
                    stamp[base + e] = r + 1

                return jnp.where(key >= 0, 1, 0)

            if small:
                for k in range(groups - 1):
                    moves += move(k)
            else:
                moves += lax.fori_loop(0, groups - 1, lambda k, s: s + move(k), jnp.int32(0))
        return moves

    hops = remaining()
    left = hops - a_round(0, False)
    for d, target in enumerate((key_up, key_down)):
        start = pl.multiple_of(plan[HEADER + d] * STRETCH, STRETCH)
        target[...] = keys[pl.ds(start, STRETCH), :]

    def go_on(carry):
        return (carry[1] > 0) & (carry[0] < cap)

    rounds, _ = lax.while_loop(
        go_on, lambda c: (c[0] + 1, c[1] - a_round(c[0], False)), (jnp.int32(1), left)
    )
    plan[0] = rounds
    plan[5] = rounds
    branch[0] = sum(jnp.where(rounds > length, 1, 0) for length in ROUNDS)

    @pl.when(rounds > ROUNDS[-1])
    def _():
        each(total, stand)
        again, _ = lax.while_loop(
            go_on, lambda c: (c[0] + 1, c[1] - a_round(c[0], True)), (jnp.int32(0), hops)
        )
        plan[5] = again


def make_plan(groups, tables, keys):
    total = STRETCH_DEV * groups
    cap = 2 * groups + 16
    block = jax.ShapeDtypeStruct((STRETCH, keys.shape[1]), keys.dtype)
    return pl.pallas_call(
        functools.partial(plan_kernel, groups, cap),
        out_shape=[
            jax.ShapeDtypeStruct((HEADER + cap * ROW,), jnp.int32),
            jax.ShapeDtypeStruct((1,), jnp.int32),
            block,
            block,
        ],
        in_specs=[SMEM] * 4 + [VMEM],
        out_specs=[SMEM] * 2 + [VMEM] * 2,
        scratch_shapes=[pltpu.SMEM((2 * total,), jnp.int32) for _ in range(5)]
        + [pltpu.SMEM((groups,), jnp.int32)],
        name="plan",
    )(*tables, keys)


def choose_kernel(row, arrivals, axis, plan, *refs):
    if row is None:
        at, own, *refs = refs
        base = HEADER + at[0] * ROW
    else:
        own, *refs = refs
        base = HEADER + row * ROW
    came, outs = refs[: 2 * arrivals], refs[2 * arrivals :]
    for d in range(2):
        choice = plan[base + d]

        @pl.when(choice < STRETCH_DEV)
        def _(d=d, choice=choice):
            part = pl.ds(pl.multiple_of(choice * STRETCH, STRETCH), STRETCH)
            outs[d][...] = own[part, :] if axis == 0 else own[:, part]

        for i in range(arrivals):
            picked = choice == STRETCH_DEV + i if row is not None else choice >= STRETCH_DEV

            @pl.when(picked)
            def _(d=d, i=i):
                outs[d][...] = came[d * arrivals + i][...]


def choose(plan, row, own, axis, up, down):
    static = isinstance(row, int)
    shape = list(own.shape)
    shape[axis] = STRETCH
    block = jax.ShapeDtypeStruct(tuple(shape), own.dtype)
    return pl.pallas_call(
        functools.partial(choose_kernel, row if static else None, len(up), axis),
        out_shape=[block] * 2,
        in_specs=[SMEM] + ([] if static else [SMEM]) + [VMEM] * (1 + 2 * len(up)),
        out_specs=[VMEM] * 2,
        cost_estimate=pl.CostEstimate(flops=0, bytes_accessed=8 * block.size, transcendentals=0),
        name="choose",
    )(plan, *(() if static else (row,)), own, *up, *down)


def turn_kernel(queries, values, text_values, split, values_out, text_out):
    columns = queries.shape[1]
    for h in range(columns // HD):
        cols = pl.ds(h * HD, HD)
        for t in range(queries.shape[0] // TILE):
            at = pl.ds(t * TILE, TILE)
            turned = jnp.transpose(queries[at, cols].astype(jnp.float32) * EXPONENT)
            high = turned.astype(jnp.bfloat16)
            split[pl.ds(2 * h * HD, HD), at] = high
            split[pl.ds((2 * h + 1) * HD, HD), at] = (turned - high.astype(jnp.float32)).astype(jnp.bfloat16)
            values_out[cols, at] = jnp.transpose(values[at, cols])
        for t in range(text_values.shape[0] // TILE):
            at = pl.ds(t * TILE, TILE)
            text_out[cols, at] = jnp.transpose(text_values[at, cols])


def turn(queries, values, text_values):
    rows, columns = queries.shape
    outs = [(2 * columns, rows), (columns, rows), (columns, text_values.shape[0])]
    return pl.pallas_call(
        turn_kernel,
        out_shape=[jax.ShapeDtypeStruct(shape, queries.dtype) for shape in outs],
        in_specs=[VMEM] * 3,
        out_specs=[VMEM] * 3,
        compiler_params=pltpu.CompilerParams(vmem_limit_bytes=40 * 1024 * 1024),
        name="turn",
    )(queries, values, text_values)


def attend_kernel(blocks, row, first, last, *refs):
    refs = list(refs)
    plan = refs.pop(0)
    base = HEADER + (refs.pop(0)[0] if row is None else row) * ROW
    queries = refs.pop(0)
    block_refs = [(refs.pop(0), refs.pop(0)) for _ in blocks]
    rows = queries.shape[1]
    heads = queries.shape[0] // (2 * HD)
    if not first:
        acc_in, stat_in = refs.pop(0), refs.pop(0)
    if last:
        out, acc, stat = refs
    else:
        acc, stat = refs
    per_stretch = STRETCH // TILE

    if not first:
        acc[...] = acc_in[...]
        stat[...] = stat_in[...]

    for number, ((start, length, weight_at), (key_ref, value_ref)) in enumerate(zip(blocks, block_refs)):
        opening = first and number == 0

        def step(at, weight, start=start, length=length, key_ref=key_ref, value_ref=value_ref, opening=opening):
            part = pl.ds(start, length)
            ones = jnp.ones((16, length), jnp.bfloat16)
            for h in range(heads):
                cols = pl.ds(h * HD, HD)
                keys = key_ref[part, cols]
                scores = jnp.dot(
                    jnp.concatenate([keys, keys], axis=1), queries[pl.ds(2 * h * HD, 2 * HD), at],
                    preferred_element_type=jnp.float32,
                )
                peak = jnp.max(scores, axis=0, keepdims=True)
                if not opening:
                    before = stat[h : h + 1, at]
                    peak = jnp.maximum(peak, before)
                    keep = jnp.exp2(before - peak)
                weights = jnp.exp2(scores - peak).astype(jnp.bfloat16)
                both = jnp.dot(
                    jnp.concatenate([value_ref[cols, part], ones], axis=0), weights,
                    preferred_element_type=jnp.float32,
                )
                mixed, mass = both[:HD], both[HD : HD + 1]
                if not opening:
                    mixed = mixed * weight + acc[cols, at] * keep
                    mass = mass * weight + stat[8 + h : 9 + h, at] * keep
                acc[cols, at] = mixed
                stat[h : h + 1, at] = peak
                stat[8 + h : 9 + h, at] = mass

        def tile(t, c, weight_at=weight_at, opening=opening, step=step):
            at = pl.ds(pl.multiple_of(t * TILE, TILE), TILE)
            if opening:
                step(at, None)
                return c
            where = (base if weight_at[0] else 0) + weight_at[1] + weight_at[2] * (t // per_stretch)
            times = plan[where]

            @pl.when(times > 0)
            def _():
                step(at, times.astype(jnp.float32))

            return c

        lax.fori_loop(0, rows // TILE, tile, 0)

    if last:
        for h in range(heads):
            cols = pl.ds(h * HD, HD)
            for t in range(rows // TILE):
                at = pl.ds(t * TILE, TILE)
                share = 1.0 / stat[8 + h : 9 + h, at]
                out[at, cols] = jnp.transpose(acc[cols, at] * share).astype(out.dtype)


def attend(plan, row, queries, blocks, state, last):
    static = isinstance(row, int)
    columns, rows = queries.shape[0] // 2, queries.shape[1]
    acc = jax.ShapeDtypeStruct((columns, rows), jnp.float32)
    stat = jax.ShapeDtypeStruct((16, rows), jnp.float32)
    keys = sum(b[3] for b in blocks)
    scratch, outs = [], [acc, stat]
    if last:
        scratch = [pltpu.VMEM(acc.shape, acc.dtype), pltpu.VMEM(stat.shape, stat.dtype)]
        outs = [jax.ShapeDtypeStruct((rows, columns), queries.dtype)]
    operands = [plan] + ([] if static else [row])
    smem = len(operands)
    operands.append(queries)
    for b in blocks:
        operands += [b[0], b[1]]
    if state is not None:
        operands += list(state)
    result = pl.pallas_call(
        functools.partial(
            attend_kernel, [tuple(b[2:]) for b in blocks], row if static else None, state is None, last
        ),
        out_shape=outs,
        in_specs=[SMEM] * smem + [VMEM] * (len(operands) - smem),
        out_specs=[VMEM] * len(outs),
        scratch_shapes=scratch,
        compiler_params=pltpu.CompilerParams(vmem_limit_bytes=40 * 1024 * 1024),
        cost_estimate=pl.CostEstimate(
            flops=4 * rows * columns * keys, bytes_accessed=8 * rows * columns,
            transcendentals=rows * columns // HD * keys,
        ),
        name="attend",
    )(*operands)
    return result[0] if last else tuple(result)


def own_blocks(text_keys, text_values, keys, values):
    blocks = [(text_keys, text_values, 0, text_keys.shape[0], None)]
    for j in range(STRETCH_DEV):
        blocks.append((keys, values, j * STRETCH, STRETCH, (False, 1 + j, 2)))
    return blocks


def came_blocks(key_came, value_came):
    return [
        (key_came[d], value_came[d], 0, STRETCH, (True, 2 + 2 * d, 1)) for d in range(2)
    ]


def send(up, down):
    last = lax.axis_size("seq") - 1
    return (
        lax.ppermute(up, "seq", [(i, i + 1) for i in range(last)]),
        lax.ppermute(down, "seq", [(i + 1, i) for i in range(last)]),
    )


def exchange(rounds, plan, queries, keys, values, text_keys, text_values, key_first):
    key_here = send(*key_first)
    queries, values, text_values = turn(queries, values, text_values)
    value_here = send(*choose(plan, 0, values, 1, [], []))
    state = attend(plan, 0, queries, own_blocks(text_keys, text_values, keys, values), None, False)
    key_came, value_came = ([], []), ([], [])
    for r in range(rounds):
        key_here, state = lax.optimization_barrier((key_here, state))
        blocks = came_blocks(key_here, value_here)
        if r + 1 < rounds:
            for d in range(2):
                key_came[d].append(key_here[d])
                value_came[d].append(value_here[d])
            key_here = send(*choose(plan, r + 1, keys, 0, *key_came))
            value_here = send(*choose(plan, r + 1, values, 1, *value_came))
        state = attend(plan, r, queries, blocks, state, r + 1 == rounds)
    return state


def long_exchange(plan, queries, keys, values, text_keys, text_values, key_first):
    queries, values, text_values = turn(queries, values, text_values)
    state = attend(plan, 0, queries, own_blocks(text_keys, text_values, keys, values), None, False)

    def body(carry):
        r, key_here, value_here, state = carry
        row = r.reshape(1)
        key_here = send(*choose(plan, row, keys, 0, [key_here[0]], [key_here[1]]))
        value_here = send(*choose(plan, row, values, 1, [value_here[0]], [value_here[1]]))
        state = attend(plan, row, queries, came_blocks(key_here, value_here), state, False)
        return (r + 1, key_here, value_here, state)

    nothing = jnp.zeros((values.shape[0], STRETCH), values.dtype)
    carry = (jnp.int32(0), tuple(key_first), (nothing, nothing), state)
    _, _, _, (acc, stat) = lax.while_loop(lambda c: c[0] < plan[5], body, carry)
    heads = acc.shape[0] // HD
    share = jnp.repeat(1.0 / stat[8 : 8 + heads], HD, axis=0)
    return jnp.transpose(acc * share).astype(queries.dtype)


def shards(
    queries, key_rows, value_rows, text_keys, text_values,
    shot_of_stretch, anchor_stretch, context_count, context_ids,
):
    groups = lax.axis_size("seq")
    tables = (shot_of_stretch, anchor_stretch, context_count, context_ids.T)
    plan, branch, key_up, key_down = make_plan(groups, tables, key_rows)
    branches = [functools.partial(exchange, rounds) for rounds in ROUNDS] + [long_exchange]
    return lax.switch(
        branch[0], branches, plan, queries, key_rows, value_rows, text_keys, text_values,
        (key_up, key_down),
    )


def solution(mesh):
    return jax.shard_map(
        shards,
        mesh=mesh,
        in_specs=(
            P(("rep", "seq"), "shot"),
            P(("rep", "seq"), "shot"),
            P(("rep", "seq"), "shot"),
            P("rep", "shot"),
            P("rep", "shot"),
            P("rep"),
            P("rep"),
            P("rep"),
            P("rep", None),
        ),
        out_specs=P(("rep", "seq"), "shot"),
        check_vma=False,
    )
```

```python
import functools
import math

import jax
import jax.numpy as jnp
from jax import lax
from jax.experimental import pallas as pl
from jax.experimental.pallas import tpu as pltpu
from jax.sharding import PartitionSpec as P

HD = 128
STRETCH = 512
STRETCH_DEV = 2
ROUNDS = (3, 4)
ROW = 8
HEADER = 8
TILE = 512
TURN = 256
EXPONENT = HD ** (-0.5) * math.log2(math.e)
SMEM = pl.BlockSpec(memory_space=pltpu.SMEM)
VMEM = pl.BlockSpec(memory_space=pltpu.VMEM)


def room(mebibytes):
    return pltpu.CompilerParams(vmem_limit_bytes=mebibytes * 1024 * 1024)


def plan_kernel(
    groups, cap, shot, anchor, count, ids, keys,
    plan, branch, key_up, key_down,
    dest, place, hold, stamp, times, best,
):
    total = STRETCH_DEV * groups
    slots = ids.shape[0]
    small = total <= 16
    bits = total.bit_length()
    me = lax.axis_index("seq")
    mine = (me, groups - 1 - me)

    def each(length, body):
        if small:
            for i in range(length):
                body(i)
        else:
            lax.fori_loop(0, length, lambda i, c: (body(i), c)[1], 0)

    def clear(e):
        g = e >> 1
        dest[e] = g
        dest[total + e] = groups - 1 - g
        times[e] = 0
        times[total + e] = 0

    each(total, clear)

    def stand(e):
        g = e >> 1
        for d, at in enumerate((g, groups - 1 - g)):
            place[d * total + e] = at
            hold[d * total + e] = e & 1
            stamp[d * total + e] = -1

    each(total, stand)

    def read(c):
        g = c >> 1

        def entry(e):
            dest[e] = jnp.maximum(dest[e], g)
            dest[total + e] = jnp.maximum(dest[total + e], groups - 1 - g)

        entry(anchor[shot[c]])
        live = count[c]
        for s in range(slots):
            entry(jnp.where(s < live, ids[s, c], c))

    each(total, read)

    for q in range(STRETCH_DEV):
        c = STRETCH_DEV * me + q

        def one(e, amount, q=q):
            times[q * total + e] = times[q * total + e] + amount

        one(c, 1)
        one(anchor[shot[c]], 1)
        live = count[c]
        for s in range(slots):
            alive = s < live
            one(jnp.where(alive, ids[s, c], c), jnp.where(alive, 1, 0))

    for q in range(STRETCH_DEV):
        for j in range(STRETCH_DEV):
            plan[1 + 2 * q + j] = times[q * total + STRETCH_DEV * me + j]
    for i in range(ROW * ROUNDS[-1]):
        plan[HEADER + i] = 0

    def remaining():
        return lax.fori_loop(
            0, 2 * total, lambda e, s: s + dest[e] - place[e], jnp.int32(0), unroll=small
        )

    def a_round(r, transit):
        moves = jnp.int32(0)
        for d in range(2):
            base = d * total
            for k in range(groups) if small else ():
                best[k] = -1
            if not small:
                each(groups, lambda k: best.__setitem__(k, jnp.int32(-1)))

            def rank(e, base=base):
                at = place[base + e]
                to = dest[base + e]
                key = (to << bits) | e
                if transit:
                    key = jnp.where(stamp[base + e] == r, key + (groups << bits), key)
                best[at] = jnp.maximum(best[at], jnp.where(to > at, key, -1))

            each(total, rank)
            sent = best[mine[d]]
            mask = (1 << bits) - 1
            plan[HEADER + r * ROW + d] = jnp.where(sent < 0, 0, hold[base + (jnp.maximum(sent, 0) & mask)])
            came = jnp.where(mine[d] > 0, best[jnp.maximum(mine[d] - 1, 0)], -1)
            come = jnp.maximum(came, 0) & mask
            for q in range(STRETCH_DEV):
                plan[HEADER + r * ROW + 2 + 2 * d + q] = jnp.where(came < 0, 0, times[q * total + come])

            @pl.when(came >= 0)
            def _(come=come, base=base):
                hold[base + come] = 2 + r

            def move(k, base=base):
                key = best[k]

                @pl.when(key >= 0)
                def _():
                    e = key & mask
                    place[base + e] = k + 1
                    stamp[base + e] = r + 1

                return jnp.where(key >= 0, 1, 0)

            if small:
                for k in range(groups - 1):
                    moves += move(k)
            else:
                moves += lax.fori_loop(0, groups - 1, lambda k, s: s + move(k), jnp.int32(0))
        return moves

    hops = remaining()
    left = hops - a_round(0, False)
    for d, target in enumerate((key_up, key_down)):
        start = pl.multiple_of(plan[HEADER + d] * STRETCH, STRETCH)
        target[...] = keys[pl.ds(start, STRETCH), :]

    def go_on(carry):
        return (carry[1] > 0) & (carry[0] < cap)

    rounds, _ = lax.while_loop(
        go_on, lambda c: (c[0] + 1, c[1] - a_round(c[0], False)), (jnp.int32(1), left)
    )
    plan[0] = rounds
    plan[5] = rounds
    branch[0] = sum(jnp.where(rounds > length, 1, 0) for length in ROUNDS)

    @pl.when(rounds > ROUNDS[-1])
    def _():
        each(total, stand)
        again, _ = lax.while_loop(
            go_on, lambda c: (c[0] + 1, c[1] - a_round(c[0], True)), (jnp.int32(0), hops)
        )
        plan[5] = again


def make_plan(groups, tables, keys):
    total = STRETCH_DEV * groups
    cap = 2 * groups + 16
    block = jax.ShapeDtypeStruct((STRETCH, keys.shape[1]), keys.dtype)
    return pl.pallas_call(
        functools.partial(plan_kernel, groups, cap),
        out_shape=[
            jax.ShapeDtypeStruct((HEADER + cap * ROW,), jnp.int32),
            jax.ShapeDtypeStruct((1,), jnp.int32),
            block,
            block,
        ],
        in_specs=[SMEM] * 4 + [VMEM],
        out_specs=[SMEM] * 2 + [VMEM] * 2,
        scratch_shapes=[pltpu.SMEM((2 * total,), jnp.int32) for _ in range(5)]
        + [pltpu.SMEM((groups,), jnp.int32)],
        compiler_params=room(6),
        name="plan",
    )(*tables, keys)


def choose_kernel(row, arrivals, axis, plan, *refs):
    if row is None:
        at, own, *refs = refs
        base = HEADER + at[0] * ROW
    else:
        own, *refs = refs
        base = HEADER + row * ROW
    came, outs = refs[: 2 * arrivals], refs[2 * arrivals :]
    for d in range(2):
        choice = plan[base + d]

        @pl.when(choice < STRETCH_DEV)
        def _(d=d, choice=choice):
            part = pl.ds(pl.multiple_of(choice * STRETCH, STRETCH), STRETCH)
            outs[d][...] = own[part, :] if axis == 0 else own[:, part]

        for i in range(arrivals):
            picked = choice == STRETCH_DEV + i if row is not None else choice >= STRETCH_DEV

            @pl.when(picked)
            def _(d=d, i=i):
                outs[d][...] = came[d * arrivals + i][...]


def choose(plan, row, own, axis, up, down):
    static = isinstance(row, int)
    shape = list(own.shape)
    shape[axis] = STRETCH
    block = jax.ShapeDtypeStruct(tuple(shape), own.dtype)
    return pl.pallas_call(
        functools.partial(choose_kernel, row if static else None, len(up), axis),
        out_shape=[block] * 2,
        in_specs=[SMEM] + ([] if static else [SMEM]) + [VMEM] * (1 + 2 * len(up)),
        out_specs=[VMEM] * 2,
        compiler_params=room(8),
        cost_estimate=pl.CostEstimate(flops=0, bytes_accessed=8 * block.size, transcendentals=0),
        name="choose",
    )(plan, *(() if static else (row,)), own, *up, *down)


def turn_kernel(queries, values, text_values, split, values_out, text_out):
    columns = queries.shape[1]
    for h in range(columns // HD):
        cols = pl.ds(h * HD, HD)
        for t in range(queries.shape[0] // TURN):
            at = pl.ds(t * TURN, TURN)
            turned = jnp.transpose(queries[at, cols].astype(jnp.float32) * EXPONENT)
            high = turned.astype(jnp.bfloat16)
            split[pl.ds(2 * h * HD, HD), at] = high
            split[pl.ds((2 * h + 1) * HD, HD), at] = (turned - high.astype(jnp.float32)).astype(jnp.bfloat16)
            values_out[cols, at] = jnp.transpose(values[at, cols])
        for t in range(text_values.shape[0] // TURN):
            at = pl.ds(t * TURN, TURN)
            text_out[cols, at] = jnp.transpose(text_values[at, cols])


def turn(queries, values, text_values):
    rows, columns = queries.shape
    outs = [(2 * columns, rows), (columns, rows), (columns, text_values.shape[0])]
    return pl.pallas_call(
        turn_kernel,
        out_shape=[jax.ShapeDtypeStruct(shape, queries.dtype) for shape in outs],
        in_specs=[VMEM] * 3,
        out_specs=[VMEM] * 3,
        compiler_params=room(10),
        name="turn",
    )(queries, values, text_values)


def attend_kernel(blocks, row, first, last, *refs):
    refs = list(refs)
    plan = refs.pop(0)
    base = HEADER + (refs.pop(0)[0] if row is None else row) * ROW
    queries = refs.pop(0)
    block_refs = [(refs.pop(0), refs.pop(0)) for _ in blocks]
    rows = queries.shape[1]
    heads = queries.shape[0] // (2 * HD)
    if not first:
        acc_in, stat_in = refs.pop(0), refs.pop(0)
    if last:
        out, acc, stat = refs
    else:
        acc, stat = refs
    per_stretch = STRETCH // TILE

    if not first:
        acc[...] = acc_in[...]
        stat[...] = stat_in[...]

    for number, ((start, length, weight_at), (key_ref, value_ref)) in enumerate(zip(blocks, block_refs)):
        opening = first and number == 0

        def step(at, weight, start=start, length=length, key_ref=key_ref, value_ref=value_ref, opening=opening):
            part = pl.ds(start, length)
            ones = jnp.ones((16, length), jnp.bfloat16)

            def score(h):
                keys = key_ref[part, pl.ds(h * HD, HD)]
                return jnp.dot(
                    jnp.concatenate([keys, keys], axis=1), queries[pl.ds(2 * h * HD, 2 * HD), at],
                    preferred_element_type=jnp.float32,
                )

            def mix(h, scores):
                cols = pl.ds(h * HD, HD)
                peak = jnp.max(scores, axis=0, keepdims=True)
                if not opening:
                    before = stat[h : h + 1, at]
                    peak = jnp.maximum(peak, before)
                    keep = jnp.exp2(before - peak)
                weights = jnp.exp2(scores - peak).astype(jnp.bfloat16)
                both = jnp.dot(
                    jnp.concatenate([value_ref[cols, part], ones], axis=0), weights,
                    preferred_element_type=jnp.float32,
                )
                mixed, mass = both[:HD], both[HD : HD + 1]
                if not opening:
                    mixed = mixed * weight + acc[cols, at] * keep
                    mass = mass * weight + stat[8 + h : 9 + h, at] * keep
                acc[cols, at] = mixed
                stat[h : h + 1, at] = peak
                stat[8 + h : 9 + h, at] = mass

            scores = score(0)
            for h in range(heads):
                following = score(h + 1) if h + 1 < heads else None
                mix(h, scores)
                scores = following

        def tile(t, c, weight_at=weight_at, opening=opening, step=step):
            at = pl.ds(pl.multiple_of(t * TILE, TILE), TILE)
            if opening:
                step(at, None)
                return c
            where = (base if weight_at[0] else 0) + weight_at[1] + weight_at[2] * (t // per_stretch)
            times = plan[where]

            @pl.when(times > 0)
            def _():
                step(at, times.astype(jnp.float32))

            return c

        lax.fori_loop(0, rows // TILE, tile, 0)

    if last:
        for h in range(heads):
            cols = pl.ds(h * HD, HD)
            for t in range(rows // TURN):
                at = pl.ds(t * TURN, TURN)
                share = 1.0 / stat[8 + h : 9 + h, at]
                out[at, cols] = jnp.transpose(acc[cols, at] * share).astype(out.dtype)


def attend(plan, row, queries, blocks, state, last):
    static = isinstance(row, int)
    columns, rows = queries.shape[0] // 2, queries.shape[1]
    acc = jax.ShapeDtypeStruct((columns, rows), jnp.float32)
    stat = jax.ShapeDtypeStruct((16, rows), jnp.float32)
    keys = sum(b[3] for b in blocks)
    scratch, outs = [], [acc, stat]
    if last:
        scratch = [pltpu.VMEM(acc.shape, acc.dtype), pltpu.VMEM(stat.shape, stat.dtype)]
        outs = [jax.ShapeDtypeStruct((rows, columns), queries.dtype)]
    operands = [plan] + ([] if static else [row])
    smem = len(operands)
    operands.append(queries)
    for b in blocks:
        operands += [b[0], b[1]]
    if state is not None:
        operands += list(state)
    result = pl.pallas_call(
        functools.partial(
            attend_kernel, [tuple(b[2:]) for b in blocks], row if static else None, state is None, last
        ),
        out_shape=outs,
        in_specs=[SMEM] * smem + [VMEM] * (len(operands) - smem),
        out_specs=[VMEM] * len(outs),
        scratch_shapes=scratch,
        compiler_params=room(24),
        cost_estimate=pl.CostEstimate(
            flops=4 * rows * columns * keys, bytes_accessed=8 * rows * columns,
            transcendentals=rows * columns // HD * keys,
        ),
        name="attend",
    )(*operands)
    return result[0] if last else tuple(result)


def own_blocks(text_keys, text_values, keys, values):
    blocks = [(text_keys, text_values, 0, text_keys.shape[0], None)]
    for j in range(STRETCH_DEV):
        blocks.append((keys, values, j * STRETCH, STRETCH, (False, 1 + j, 2)))
    return blocks


def came_blocks(key_came, value_came):
    return [
        (key_came[d], value_came[d], 0, STRETCH, (True, 2 + 2 * d, 1)) for d in range(2)
    ]


def send(up, down):
    last = lax.axis_size("seq") - 1
    return (
        lax.ppermute(up, "seq", [(i, i + 1) for i in range(last)]),
        lax.ppermute(down, "seq", [(i + 1, i) for i in range(last)]),
    )


def exchange(rounds, plan, queries, keys, values, text_keys, text_values, key_first):
    key_here = send(*key_first)
    queries, values, text_values = turn(queries, values, text_values)
    value_here = send(*choose(plan, 0, values, 1, [], []))
    state = attend(plan, 0, queries, own_blocks(text_keys, text_values, keys, values), None, False)
    key_came, value_came = ([], []), ([], [])
    for r in range(rounds):
        key_here, state = lax.optimization_barrier((key_here, state))
        blocks = came_blocks(key_here, value_here)
        if r + 1 < rounds:
            for d in range(2):
                key_came[d].append(key_here[d])
                value_came[d].append(value_here[d])
            key_here = send(*choose(plan, r + 1, keys, 0, *key_came))
            value_here = send(*choose(plan, r + 1, values, 1, *value_came))
        state = attend(plan, r, queries, blocks, state, r + 1 == rounds)
    return state


def long_exchange(plan, queries, keys, values, text_keys, text_values, key_first):
    queries, values, text_values = turn(queries, values, text_values)
    state = attend(plan, 0, queries, own_blocks(text_keys, text_values, keys, values), None, False)

    def body(carry):
        r, key_here, value_here, state = carry
        row = r.reshape(1)
        key_here = send(*choose(plan, row, keys, 0, [key_here[0]], [key_here[1]]))
        value_here = send(*choose(plan, row, values, 1, [value_here[0]], [value_here[1]]))
        state = attend(plan, row, queries, came_blocks(key_here, value_here), state, False)
        return (r + 1, key_here, value_here, state)

    nothing = jnp.zeros((values.shape[0], STRETCH), values.dtype)
    carry = (jnp.int32(0), tuple(key_first), (nothing, nothing), state)
    _, _, _, (acc, stat) = lax.while_loop(lambda c: c[0] < plan[5], body, carry)
    heads = acc.shape[0] // HD
    share = jnp.repeat(1.0 / stat[8 : 8 + heads], HD, axis=0)
    return jnp.transpose(acc * share).astype(queries.dtype)


def shards(
    queries, key_rows, value_rows, text_keys, text_values,
    shot_of_stretch, anchor_stretch, context_count, context_ids,
):
    groups = lax.axis_size("seq")
    tables = (shot_of_stretch, anchor_stretch, context_count, context_ids.T)
    plan, branch, key_up, key_down = make_plan(groups, tables, key_rows)
    branches = [functools.partial(exchange, rounds) for rounds in ROUNDS] + [long_exchange]
    return lax.switch(
        branch[0], branches, plan, queries, key_rows, value_rows, text_keys, text_values,
        (key_up, key_down),
    )


def solution(mesh):
    return jax.shard_map(
        shards,
        mesh=mesh,
        in_specs=(
            P(("rep", "seq"), "shot"),
            P(("rep", "seq"), "shot"),
            P(("rep", "seq"), "shot"),
            P("rep", "shot"),
            P("rep", "shot"),
            P("rep"),
            P("rep"),
            P("rep"),
            P("rep", None),
        ),
        out_specs=P(("rep", "seq"), "shot"),
        check_vma=False,
    )
```

```python
import functools
import math

import jax
import jax.numpy as jnp
from jax import lax
from jax.experimental import pallas as pl
from jax.experimental.pallas import tpu as pltpu
from jax.sharding import PartitionSpec as P

HD = 128
STRETCH = 512
STRETCH_DEV = 2
ROUNDS = (3, 4)
ROW = 8
HEADER = 8
TILE = 512
TURN = 256
LOWEST = -1e30
EXPONENT = HD ** (-0.5) * math.log2(math.e)
SMEM = pl.BlockSpec(memory_space=pltpu.SMEM)
VMEM = pl.BlockSpec(memory_space=pltpu.VMEM)


def room(mebibytes):
    return pltpu.CompilerParams(vmem_limit_bytes=mebibytes * 1024 * 1024)


def plan_kernel(
    groups, cap, shot, anchor, count, ids, keys,
    plan, branch, key_up, key_down,
    dest, place, hold, stamp, times, best,
):
    total = STRETCH_DEV * groups
    slots = ids.shape[0]
    small = total <= 16
    bits = total.bit_length()
    me = lax.axis_index("seq")
    mine = (me, groups - 1 - me)

    def each(length, body):
        if small:
            for i in range(length):
                body(i)
        else:
            lax.fori_loop(0, length, lambda i, c: (body(i), c)[1], 0)

    def clear(e):
        g = e >> 1
        dest[e] = g
        dest[total + e] = groups - 1 - g
        times[e] = 0
        times[total + e] = 0

    each(total, clear)

    def stand(e):
        g = e >> 1
        for d, at in enumerate((g, groups - 1 - g)):
            place[d * total + e] = at
            hold[d * total + e] = e & 1
            stamp[d * total + e] = -1

    each(total, stand)

    def read(c):
        g = c >> 1

        def entry(e):
            dest[e] = jnp.maximum(dest[e], g)
            dest[total + e] = jnp.maximum(dest[total + e], groups - 1 - g)

        entry(anchor[shot[c]])
        live = count[c]
        for s in range(slots):
            entry(jnp.where(s < live, ids[s, c], c))

    each(total, read)

    for q in range(STRETCH_DEV):
        c = STRETCH_DEV * me + q

        def one(e, amount, q=q):
            times[q * total + e] = times[q * total + e] + amount

        one(c, 1)
        one(anchor[shot[c]], 1)
        live = count[c]
        for s in range(slots):
            alive = s < live
            one(jnp.where(alive, ids[s, c], c), jnp.where(alive, 1, 0))

    for q in range(STRETCH_DEV):
        for j in range(STRETCH_DEV):
            plan[1 + 2 * q + j] = times[q * total + STRETCH_DEV * me + j]
    for i in range(ROW * ROUNDS[-1]):
        plan[HEADER + i] = 0

    def remaining():
        return lax.fori_loop(
            0, 2 * total, lambda e, s: s + dest[e] - place[e], jnp.int32(0), unroll=small
        )

    def a_round(r, transit):
        moves = jnp.int32(0)
        for d in range(2):
            base = d * total
            for k in range(groups) if small else ():
                best[k] = -1
            if not small:
                each(groups, lambda k: best.__setitem__(k, jnp.int32(-1)))

            def rank(e, base=base):
                at = place[base + e]
                to = dest[base + e]
                key = (to << bits) | e
                if transit:
                    key = jnp.where(stamp[base + e] == r, key + (groups << bits), key)
                best[at] = jnp.maximum(best[at], jnp.where(to > at, key, -1))

            each(total, rank)
            sent = best[mine[d]]
            mask = (1 << bits) - 1
            plan[HEADER + r * ROW + d] = jnp.where(sent < 0, 0, hold[base + (jnp.maximum(sent, 0) & mask)])
            came = jnp.where(mine[d] > 0, best[jnp.maximum(mine[d] - 1, 0)], -1)
            come = jnp.maximum(came, 0) & mask
            for q in range(STRETCH_DEV):
                plan[HEADER + r * ROW + 2 + 2 * d + q] = jnp.where(came < 0, 0, times[q * total + come])

            @pl.when(came >= 0)
            def _(come=come, base=base):
                hold[base + come] = 2 + r

            def move(k, base=base):
                key = best[k]

                @pl.when(key >= 0)
                def _():
                    e = key & mask
                    place[base + e] = k + 1
                    stamp[base + e] = r + 1

                return jnp.where(key >= 0, 1, 0)

            if small:
                for k in range(groups - 1):
                    moves += move(k)
            else:
                moves += lax.fori_loop(0, groups - 1, lambda k, s: s + move(k), jnp.int32(0))
        return moves

    hops = remaining()
    left = hops - a_round(0, False)
    for d, target in enumerate((key_up, key_down)):
        start = pl.multiple_of(plan[HEADER + d] * STRETCH, STRETCH)
        target[...] = keys[pl.ds(start, STRETCH), :]

    def go_on(carry):
        return (carry[1] > 0) & (carry[0] < cap)

    rounds, _ = lax.while_loop(
        go_on, lambda c: (c[0] + 1, c[1] - a_round(c[0], False)), (jnp.int32(1), left)
    )
    plan[0] = rounds
    plan[5] = rounds
    branch[0] = sum(jnp.where(rounds > length, 1, 0) for length in ROUNDS)

    @pl.when(rounds > ROUNDS[-1])
    def _():
        each(total, stand)
        again, _ = lax.while_loop(
            go_on, lambda c: (c[0] + 1, c[1] - a_round(c[0], True)), (jnp.int32(0), hops)
        )
        plan[5] = again


def make_plan(groups, tables, keys):
    total = STRETCH_DEV * groups
    cap = 2 * groups + 16
    block = jax.ShapeDtypeStruct((STRETCH, keys.shape[1]), keys.dtype)
    return pl.pallas_call(
        functools.partial(plan_kernel, groups, cap),
        out_shape=[
            jax.ShapeDtypeStruct((HEADER + cap * ROW,), jnp.int32),
            jax.ShapeDtypeStruct((1,), jnp.int32),
            block,
            block,
        ],
        in_specs=[SMEM] * 4 + [VMEM],
        out_specs=[SMEM] * 2 + [VMEM] * 2,
        scratch_shapes=[pltpu.SMEM((2 * total,), jnp.int32) for _ in range(5)]
        + [pltpu.SMEM((groups,), jnp.int32)],
        name="plan",
    )(*tables, keys)


def choose_kernel(row, arrivals, axis, plan, *refs):
    if row is None:
        at, own, *refs = refs
        base = HEADER + at[0] * ROW
    else:
        own, *refs = refs
        base = HEADER + row * ROW
    came, outs = refs[: 2 * arrivals], refs[2 * arrivals :]
    for d in range(2):
        choice = plan[base + d]

        @pl.when(choice < STRETCH_DEV)
        def _(d=d, choice=choice):
            part = pl.ds(pl.multiple_of(choice * STRETCH, STRETCH), STRETCH)
            outs[d][...] = own[part, :] if axis == 0 else own[:, part]

        for i in range(arrivals):
            picked = choice == STRETCH_DEV + i if row is not None else choice >= STRETCH_DEV

            @pl.when(picked)
            def _(d=d, i=i):
                outs[d][...] = came[d * arrivals + i][...]


def choose(plan, row, own, axis, up, down):
    static = isinstance(row, int)
    shape = list(own.shape)
    shape[axis] = STRETCH
    block = jax.ShapeDtypeStruct(tuple(shape), own.dtype)
    return pl.pallas_call(
        functools.partial(choose_kernel, row if static else None, len(up), axis),
        out_shape=[block] * 2,
        in_specs=[SMEM] + ([] if static else [SMEM]) + [VMEM] * (1 + 2 * len(up)),
        out_specs=[VMEM] * 2,
        compiler_params=room(8),
        cost_estimate=pl.CostEstimate(flops=0, bytes_accessed=8 * block.size, transcendentals=0),
        name="choose",
    )(plan, *(() if static else (row,)), own, *up, *down)


def turn_queries_kernel(queries, split):
    for h in range(queries.shape[1] // HD):
        cols = pl.ds(h * HD, HD)
        for t in range(queries.shape[0] // TURN):
            at = pl.ds(t * TURN, TURN)
            turned = jnp.transpose(queries[at, cols].astype(jnp.float32) * EXPONENT)
            high = turned.astype(jnp.bfloat16)
            split[pl.ds(2 * h * HD, HD), at] = high
            split[pl.ds((2 * h + 1) * HD, HD), at] = (turned - high.astype(jnp.float32)).astype(jnp.bfloat16)


def turn_queries(queries):
    rows, columns = queries.shape
    return pl.pallas_call(
        turn_queries_kernel,
        out_shape=jax.ShapeDtypeStruct((2 * columns, rows), queries.dtype),
        in_specs=[VMEM],
        out_specs=VMEM,
        compiler_params=room(10),
        name="turn_queries",
    )(queries)


def turn_values_kernel(plan, values, text_values, values_out, text_out, up, down):
    for h in range(values.shape[1] // HD):
        cols = pl.ds(h * HD, HD)
        for source, target in ((values, values_out), (text_values, text_out)):
            for t in range(source.shape[0] // TURN):
                at = pl.ds(t * TURN, TURN)
                target[cols, at] = jnp.transpose(source[at, cols])
    for d, target in enumerate((up, down)):
        start = pl.multiple_of(plan[HEADER + d] * STRETCH, STRETCH)
        target[...] = values_out[:, pl.ds(start, STRETCH)]


def turn_values(plan, values, text_values):
    rows, columns = values.shape
    outs = [(columns, rows), (columns, text_values.shape[0]), (columns, STRETCH), (columns, STRETCH)]
    return pl.pallas_call(
        turn_values_kernel,
        out_shape=[jax.ShapeDtypeStruct(shape, values.dtype) for shape in outs],
        in_specs=[SMEM, VMEM, VMEM],
        out_specs=[VMEM] * 4,
        compiler_params=room(10),
        name="turn_values",
    )(plan, values, text_values)


def attend_kernel(blocks, rowed, first, last, *refs):
    refs = list(refs)
    plan = refs.pop(0)
    base = HEADER + refs.pop(0)[0] * ROW if rowed else 0
    queries = refs.pop(0)
    block_refs = [(refs.pop(0), refs.pop(0)) for _ in blocks]
    rows = queries.shape[1]
    heads = queries.shape[0] // (2 * HD)
    if not first:
        acc_in, stat_in = refs.pop(0), refs.pop(0)
    if last:
        out, acc, stat = refs
    else:
        acc, stat = refs
    per_stretch = STRETCH // TILE

    if first:
        acc[...] = jnp.zeros_like(acc)
        stat[:8] = jnp.full((8, rows), LOWEST, jnp.float32)
        stat[8:] = jnp.zeros((8, rows), jnp.float32)
    else:
        acc[...] = acc_in[...]
        stat[...] = stat_in[...]

    for (start, length, weight_at), (key_ref, value_ref) in zip(blocks, block_refs):

        def step(at, weight, start=start, length=length, key_ref=key_ref, value_ref=value_ref):
            part = pl.ds(start, length)
            ones = jnp.ones((16, length), jnp.bfloat16)

            def score(h):
                keys = key_ref[part, pl.ds(h * HD, HD)]
                return jnp.dot(
                    jnp.concatenate([keys, keys], axis=1), queries[pl.ds(2 * h * HD, 2 * HD), at],
                    preferred_element_type=jnp.float32,
                )

            def mix(h, scores):
                cols = pl.ds(h * HD, HD)
                before = stat[h : h + 1, at]
                peak = jnp.maximum(jnp.max(scores, axis=0, keepdims=True), before)
                keep = jnp.exp2(before - peak)
                weights = jnp.exp2(scores - peak).astype(jnp.bfloat16)
                both = jnp.dot(
                    jnp.concatenate([value_ref[cols, part], ones], axis=0), weights,
                    preferred_element_type=jnp.float32,
                )
                if weight is not None:
                    both = both * weight
                acc[cols, at] = both[:HD] + acc[cols, at] * keep
                stat[8 + h : 9 + h, at] = both[HD : HD + 1] + stat[8 + h : 9 + h, at] * keep
                stat[h : h + 1, at] = peak

            scores = score(0)
            for h in range(heads):
                following = score(h + 1) if h + 1 < heads else None
                mix(h, scores)
                scores = following

        def tile(t, c, weight_at=weight_at, step=step):
            at = pl.ds(pl.multiple_of(t * TILE, TILE), TILE)
            if weight_at is None:
                step(at, None)
                return c
            where = base + weight_at[0] + weight_at[1] * (t // per_stretch)
            times = plan[where]

            @pl.when(times > 0)
            def _():
                step(at, times.astype(jnp.float32))

            return c

        lax.fori_loop(0, rows // TILE, tile, 0)

    if last:
        for h in range(heads):
            cols = pl.ds(h * HD, HD)
            for t in range(rows // TURN):
                at = pl.ds(t * TURN, TURN)
                share = 1.0 / stat[8 + h : 9 + h, at]
                out[at, cols] = jnp.transpose(acc[cols, at] * share).astype(out.dtype)


def attend(plan, row, queries, blocks, state, last):
    static = row is None
    columns, rows = queries.shape[0] // 2, queries.shape[1]
    acc = jax.ShapeDtypeStruct((columns, rows), jnp.float32)
    stat = jax.ShapeDtypeStruct((16, rows), jnp.float32)
    keys = sum(b[3] for b in blocks)
    scratch, outs = [], [acc, stat]
    if last:
        scratch = [pltpu.VMEM(acc.shape, acc.dtype), pltpu.VMEM(stat.shape, stat.dtype)]
        outs = [jax.ShapeDtypeStruct((rows, columns), queries.dtype)]
    operands = [plan] + ([] if static else [row])
    smem = len(operands)
    operands.append(queries)
    for b in blocks:
        operands += [b[0], b[1]]
    if state is not None:
        operands += list(state)
    result = pl.pallas_call(
        functools.partial(
            attend_kernel, [tuple(b[2:]) for b in blocks], row is not None, state is None, last
        ),
        out_shape=outs,
        in_specs=[SMEM] * smem + [VMEM] * (len(operands) - smem),
        out_specs=[VMEM] * len(outs),
        scratch_shapes=scratch,
        compiler_params=room(24),
        cost_estimate=pl.CostEstimate(
            flops=4 * rows * columns * keys, bytes_accessed=8 * rows * columns,
            transcendentals=rows * columns // HD * keys,
        ),
        name="attend",
    )(*operands)
    return result[0] if last else tuple(result)


def own_blocks(keys, values, text_keys, text_values):
    blocks = [(text_keys, text_values, 0, text_keys.shape[0], None)]
    for j in range(STRETCH_DEV):
        blocks.append((keys, values, j * STRETCH, STRETCH, (1 + j, 2)))
    return blocks


def came_blocks(base, key_came, value_came):
    return [(key_came[d], value_came[d], 0, STRETCH, (base + 2 + 2 * d, 1)) for d in range(2)]


def send(up, down):
    last = lax.axis_size("seq") - 1
    return (
        lax.ppermute(up, "seq", [(i, i + 1) for i in range(last)]),
        lax.ppermute(down, "seq", [(i + 1, i) for i in range(last)]),
    )


def exchange(rounds, plan, queries, keys, values, text_keys, text_values, key_first):
    key_here = send(*key_first)
    values, text_values, *value_first = turn_values(plan, values, text_values)
    value_here = send(*value_first)
    queries = turn_queries(queries)
    state = None
    own = own_blocks(keys, values, text_keys, text_values)
    key_came, value_came = ([], []), ([], [])
    for r in range(rounds):
        key_here, queries, state = lax.optimization_barrier((key_here, queries, state))
        blocks = came_blocks(HEADER + r * ROW, key_here, value_here)
        if r + 1 == rounds:
            return attend(plan, None, queries, blocks, state, True)
        for d in range(2):
            key_came[d].append(key_here[d])
            value_came[d].append(value_here[d])
        key_here = send(*choose(plan, r + 1, keys, 0, *key_came))
        value_here = send(*choose(plan, r + 1, values, 1, *value_came))
        state = attend(plan, None, queries, blocks + (own if r + 2 == rounds else []), state, False)


def long_exchange(plan, queries, keys, values, text_keys, text_values, key_first):
    values, text_values, *value_first = turn_values(plan, values, text_values)
    queries = turn_queries(queries)
    state = attend(plan, None, queries, own_blocks(keys, values, text_keys, text_values), None, False)

    def body(carry):
        r, key_here, value_here, state = carry
        row = r.reshape(1)
        key_here = send(*choose(plan, row, keys, 0, [key_here[0]], [key_here[1]]))
        value_here = send(*choose(plan, row, values, 1, [value_here[0]], [value_here[1]]))
        state = attend(plan, row, queries, came_blocks(0, key_here, value_here), state, False)
        return (r + 1, key_here, value_here, state)

    carry = (jnp.int32(0), tuple(key_first), tuple(value_first), state)
    _, _, _, (acc, stat) = lax.while_loop(lambda c: c[0] < plan[5], body, carry)
    heads = acc.shape[0] // HD
    share = jnp.repeat(1.0 / stat[8 : 8 + heads], HD, axis=0)
    return jnp.transpose(acc * share).astype(queries.dtype)


def shards(
    queries, key_rows, value_rows, text_keys, text_values,
    shot_of_stretch, anchor_stretch, context_count, context_ids,
):
    groups = lax.axis_size("seq")
    tables = (shot_of_stretch, anchor_stretch, context_count, context_ids.T)
    plan, branch, key_up, key_down = make_plan(groups, tables, key_rows)
    branches = [functools.partial(exchange, rounds) for rounds in ROUNDS] + [long_exchange]
    return lax.switch(
        branch[0], branches, plan, queries, key_rows, value_rows, text_keys, text_values,
        (key_up, key_down),
    )


def solution(mesh):
    return jax.shard_map(
        shards,
        mesh=mesh,
        in_specs=(
            P(("rep", "seq"), "shot"),
            P(("rep", "seq"), "shot"),
            P(("rep", "seq"), "shot"),
            P("rep", "shot"),
            P("rep", "shot"),
            P("rep"),
            P("rep"),
            P("rep"),
            P("rep", None),
        ),
        out_specs=P(("rep", "seq"), "shot"),
        check_vma=False,
    )
```

```python
import functools
import math

import jax
import jax.numpy as jnp
from jax import lax
from jax.experimental import pallas as pl
from jax.experimental.pallas import tpu as pltpu
from jax.sharding import PartitionSpec as P

HD = 128
STRETCH = 512
STRETCH_DEV = 2
ROUNDS = (3, 4)
ROW = 8
HEADER = 8
TURN = 256
ONES = 16
EXPONENT = HD ** (-0.5) * math.log2(math.e)
SMEM = pl.BlockSpec(memory_space=pltpu.SMEM)
VMEM = pl.BlockSpec(memory_space=pltpu.VMEM)


def room(mebibytes):
    return pltpu.CompilerParams(vmem_limit_bytes=mebibytes * 1024 * 1024)


def plan_kernel(
    groups, cap, shot, anchor, count, ids, keys,
    plan, branch, key_up, key_down,
    dest, place, hold, stamp, times, best,
):
    total = STRETCH_DEV * groups
    slots = ids.shape[0]
    small = total <= 16
    bits = total.bit_length()
    me = lax.axis_index("seq")
    mine = (me, groups - 1 - me)

    def each(length, body):
        if small:
            for i in range(length):
                body(i)
        else:
            lax.fori_loop(0, length, lambda i, c: (body(i), c)[1], 0)

    def clear(e):
        g = e >> 1
        dest[e] = g
        dest[total + e] = groups - 1 - g
        times[e] = 0
        times[total + e] = 0

    each(total, clear)

    def stand(e):
        g = e >> 1
        for d, at in enumerate((g, groups - 1 - g)):
            place[d * total + e] = at
            hold[d * total + e] = e & 1
            stamp[d * total + e] = -1

    each(total, stand)

    def read(c):
        g = c >> 1

        def entry(e):
            dest[e] = jnp.maximum(dest[e], g)
            dest[total + e] = jnp.maximum(dest[total + e], groups - 1 - g)

        entry(anchor[shot[c]])
        live = count[c]
        for s in range(slots):
            entry(jnp.where(s < live, ids[s, c], c))

    each(total, read)

    for q in range(STRETCH_DEV):
        c = STRETCH_DEV * me + q

        def one(e, amount, q=q):
            times[q * total + e] = times[q * total + e] + amount

        one(c, 1)
        one(anchor[shot[c]], 1)
        live = count[c]
        for s in range(slots):
            alive = s < live
            one(jnp.where(alive, ids[s, c], c), jnp.where(alive, 1, 0))

    for q in range(STRETCH_DEV):
        for j in range(STRETCH_DEV):
            plan[1 + 2 * q + j] = times[q * total + STRETCH_DEV * me + j]
    for i in range(ROW * ROUNDS[-1]):
        plan[HEADER + i] = 0

    def remaining():
        return lax.fori_loop(
            0, 2 * total, lambda e, s: s + dest[e] - place[e], jnp.int32(0), unroll=small
        )

    def a_round(r, transit):
        moves = jnp.int32(0)
        for d in range(2):
            base = d * total
            for k in range(groups) if small else ():
                best[k] = -1
            if not small:
                each(groups, lambda k: best.__setitem__(k, jnp.int32(-1)))

            def rank(e, base=base):
                at = place[base + e]
                to = dest[base + e]
                key = (to << bits) | e
                if transit:
                    key = jnp.where(stamp[base + e] == r, key + (groups << bits), key)
                best[at] = jnp.maximum(best[at], jnp.where(to > at, key, -1))

            each(total, rank)
            sent = best[mine[d]]
            mask = (1 << bits) - 1
            plan[HEADER + r * ROW + d] = jnp.where(sent < 0, 0, hold[base + (jnp.maximum(sent, 0) & mask)])
            came = jnp.where(mine[d] > 0, best[jnp.maximum(mine[d] - 1, 0)], -1)
            come = jnp.maximum(came, 0) & mask
            for q in range(STRETCH_DEV):
                plan[HEADER + r * ROW + 2 + 2 * d + q] = jnp.where(came < 0, 0, times[q * total + come])

            @pl.when(came >= 0)
            def _(come=come, base=base):
                hold[base + come] = 2 + r

            def move(k, base=base):
                key = best[k]

                @pl.when(key >= 0)
                def _():
                    e = key & mask
                    place[base + e] = k + 1
                    stamp[base + e] = r + 1

                return jnp.where(key >= 0, 1, 0)

            if small:
                for k in range(groups - 1):
                    moves += move(k)
            else:
                moves += lax.fori_loop(0, groups - 1, lambda k, s: s + move(k), jnp.int32(0))
        return moves

    hops = remaining()
    left = hops - a_round(0, False)
    for d, target in enumerate((key_up, key_down)):
        start = pl.multiple_of(plan[HEADER + d] * STRETCH, STRETCH)
        target[...] = keys[pl.ds(start, STRETCH), :]

    def go_on(carry):
        return (carry[1] > 0) & (carry[0] < cap)

    rounds, _ = lax.while_loop(
        go_on, lambda c: (c[0] + 1, c[1] - a_round(c[0], False)), (jnp.int32(1), left)
    )
    plan[0] = rounds
    plan[5] = rounds
    branch[0] = sum(jnp.where(rounds > length, 1, 0) for length in ROUNDS)

    @pl.when(rounds > ROUNDS[-1])
    def _():
        each(total, stand)
        again, _ = lax.while_loop(
            go_on, lambda c: (c[0] + 1, c[1] - a_round(c[0], True)), (jnp.int32(0), hops)
        )
        plan[5] = again


def make_plan(groups, tables, keys):
    total = STRETCH_DEV * groups
    cap = 2 * groups + 16
    block = jax.ShapeDtypeStruct((STRETCH, keys.shape[1]), keys.dtype)
    return pl.pallas_call(
        functools.partial(plan_kernel, groups, cap),
        out_shape=[
            jax.ShapeDtypeStruct((HEADER + cap * ROW,), jnp.int32),
            jax.ShapeDtypeStruct((1,), jnp.int32),
            block,
            block,
        ],
        in_specs=[SMEM] * 4 + [VMEM],
        out_specs=[SMEM] * 2 + [VMEM] * 2,
        scratch_shapes=[pltpu.SMEM((2 * total,), jnp.int32) for _ in range(5)]
        + [pltpu.SMEM((groups,), jnp.int32)],
        name="plan",
    )(*tables, keys)


def choose_kernel(row, arrivals, axis, plan, *refs):
    if row is None:
        at, own, *refs = refs
        base = HEADER + at[0] * ROW
    else:
        own, *refs = refs
        base = HEADER + row * ROW
    came, outs = refs[: 2 * arrivals], refs[2 * arrivals :]
    for d in range(2):
        choice = plan[base + d]

        @pl.when(choice < STRETCH_DEV)
        def _(d=d, choice=choice):
            part = pl.ds(pl.multiple_of(choice * STRETCH, STRETCH), STRETCH)
            outs[d][...] = own[part, :] if axis == 0 else own[:, part]

        for i in range(arrivals):
            picked = choice == STRETCH_DEV + i if row is not None else choice >= STRETCH_DEV

            @pl.when(picked)
            def _(d=d, i=i):
                outs[d][...] = came[d * arrivals + i][...]


def choose(plan, row, own, axis, up, down):
    static = isinstance(row, int)
    shape = list(own.shape)
    shape[axis] = STRETCH
    block = jax.ShapeDtypeStruct(tuple(shape), own.dtype)
    return pl.pallas_call(
        functools.partial(choose_kernel, row if static else None, len(up), axis),
        out_shape=[block] * 2,
        in_specs=[SMEM] + ([] if static else [SMEM]) + [VMEM] * (1 + 2 * len(up)),
        out_specs=[VMEM] * 2,
        compiler_params=room(8),
        cost_estimate=pl.CostEstimate(flops=0, bytes_accessed=8 * block.size, transcendentals=0),
        name="choose",
    )(plan, *(() if static else (row,)), own, *up, *down)


def score(keys, queries, h, at):
    return jnp.dot(
        jnp.concatenate([keys, keys], axis=1), queries[pl.ds(2 * h * HD, 2 * HD), at],
        preferred_element_type=jnp.float32,
    )


def open_kernel(queries, text_keys, text_values, split, acc, stat):
    heads = queries.shape[1] // HD
    for h in range(heads):
        cols = pl.ds(h * HD, HD)
        for t in range(queries.shape[0] // TURN):
            at = pl.ds(t * TURN, TURN)
            turned = jnp.transpose(queries[at, cols].astype(jnp.float32) * EXPONENT)
            high = turned.astype(jnp.bfloat16)
            split[pl.ds(2 * h * HD, HD), at] = high
            split[pl.ds((2 * h + 1) * HD, HD), at] = (turned - high.astype(jnp.float32)).astype(jnp.bfloat16)
    ones = jnp.ones((ONES, text_keys.shape[0]), jnp.bfloat16)

    def stretch(t, c):
        at = pl.ds(pl.multiple_of(t * STRETCH, STRETCH), STRETCH)
        for h in range(heads):
            cols = pl.ds(h * HD, HD)
            scores = score(text_keys[:, cols], split, h, at)
            peak = jnp.max(scores, axis=0, keepdims=True)
            both = jnp.dot(
                jnp.concatenate([text_values[cols, :], ones], axis=0),
                jnp.exp2(scores - peak).astype(jnp.bfloat16), preferred_element_type=jnp.float32,
            )
            acc[cols, at] = both[:HD]
            stat[h : h + 1, at] = peak
            stat[8 + h : 9 + h, at] = both[HD : HD + 1]
        return c

    lax.fori_loop(0, queries.shape[0] // STRETCH, stretch, 0)


def open_state(queries, text_keys, text_values):
    rows, columns = queries.shape
    return pl.pallas_call(
        open_kernel,
        out_shape=[
            jax.ShapeDtypeStruct((2 * columns, rows), queries.dtype),
            jax.ShapeDtypeStruct((columns, rows), jnp.float32),
            jax.ShapeDtypeStruct((16, rows), jnp.float32),
        ],
        in_specs=[VMEM] * 3,
        out_specs=[VMEM] * 3,
        compiler_params=room(16),
        name="open_state",
    )(queries, text_keys, text_values)


def turn_values_kernel(plan, values, text_values, values_out, text_out, up, down):
    for h in range(values.shape[1] // HD):
        cols = pl.ds(h * HD, HD)
        for source, target in ((values, values_out), (text_values, text_out)):
            for t in range(source.shape[0] // TURN):
                at = pl.ds(t * TURN, TURN)
                target[cols, at] = jnp.transpose(source[at, cols])
    for d, target in enumerate((up, down)):
        start = pl.multiple_of(plan[HEADER + d] * STRETCH, STRETCH)
        target[...] = values_out[:, pl.ds(start, STRETCH)]


def turn_values(plan, values, text_values):
    rows, columns = values.shape
    outs = [(columns, rows), (columns, text_values.shape[0]), (columns, STRETCH), (columns, STRETCH)]
    return pl.pallas_call(
        turn_values_kernel,
        out_shape=[jax.ShapeDtypeStruct(shape, values.dtype) for shape in outs],
        in_specs=[SMEM, VMEM, VMEM],
        out_specs=[VMEM] * 4,
        compiler_params=room(10),
        name="turn_values",
    )(plan, values, text_values)


def attend_kernel(blocks, rowed, last, *refs):
    refs = list(refs)
    plan = refs.pop(0)
    base = HEADER + refs.pop(0)[0] * ROW if rowed else 0
    queries = refs.pop(0)
    block_refs = [(refs.pop(0), refs.pop(0)) for _ in blocks]
    acc_in, stat_in, *refs = refs
    *refs, keys_at, values_at = refs
    if last:
        out, acc, stat = refs
    else:
        acc, stat = refs
    rows = queries.shape[1]
    heads = queries.shape[0] // (2 * HD)
    wide = HD + ONES

    acc[...] = acc_in[...]
    stat[...] = stat_in[...]
    for h in range(heads):
        values_at[pl.ds(h * wide + HD, ONES), :] = jnp.ones((ONES, STRETCH), jnp.bfloat16)

    def step(at, weight):
        def mix(h, scores):
            cols = pl.ds(h * HD, HD)
            before = stat[h : h + 1, at]
            peak = jnp.maximum(jnp.max(scores, axis=0, keepdims=True), before)
            keep = jnp.exp2(before - peak)
            weights = jnp.exp2(scores - peak).astype(jnp.bfloat16)
            both = weight * jnp.dot(
                values_at[pl.ds(h * wide, wide), :], weights, preferred_element_type=jnp.float32
            )
            acc[cols, at] = both[:HD] + acc[cols, at] * keep
            stat[8 + h : 9 + h, at] = both[HD : HD + 1] + stat[8 + h : 9 + h, at] * keep
            stat[h : h + 1, at] = peak

        scores = score(keys_at[:, pl.ds(0, HD)], queries, 0, at)
        for h in range(heads):
            following = score(keys_at[:, pl.ds((h + 1) * HD, HD)], queries, h + 1, at) if h + 1 < heads else None
            mix(h, scores)
            scores = following

    def visit(b, c):
        place, stride = jnp.int32(0), jnp.int32(0)
        for number, (_, (first, second)) in enumerate(blocks):
            place = jnp.where(b == number, first, place)
            stride = jnp.where(b == number, second, stride)
        place = base + place

        @pl.when(plan[place] + plan[place + stride] > 0)
        def _():
            for number, (start, _) in enumerate(blocks):
                @pl.when(b == number)
                def _(start=start, number=number):
                    part = pl.ds(start, STRETCH)
                    keys_at[...] = block_refs[number][0][part, :]
                    for h in range(heads):
                        values_at[pl.ds(h * wide, HD), :] = block_refs[number][1][pl.ds(h * HD, HD), part]

            def stretch(t, c):
                times = plan[place + t * stride]

                @pl.when(times > 0)
                def _():
                    step(pl.ds(pl.multiple_of(t * STRETCH, STRETCH), STRETCH), times.astype(jnp.float32))

                return c

            lax.fori_loop(0, rows // STRETCH, stretch, 0)

        return c

    lax.fori_loop(0, len(blocks), visit, 0)

    if last:
        for h in range(heads):
            cols = pl.ds(h * HD, HD)
            for t in range(rows // TURN):
                at = pl.ds(t * TURN, TURN)
                share = 1.0 / stat[8 + h : 9 + h, at]
                out[at, cols] = jnp.transpose(acc[cols, at] * share).astype(out.dtype)


def attend(plan, row, queries, blocks, state, last):
    columns, rows = queries.shape[0] // 2, queries.shape[1]
    acc = jax.ShapeDtypeStruct((columns, rows), jnp.float32)
    stat = jax.ShapeDtypeStruct((16, rows), jnp.float32)
    scratch, outs = [], [acc, stat]
    if last:
        scratch = [pltpu.VMEM(acc.shape, acc.dtype), pltpu.VMEM(stat.shape, stat.dtype)]
        outs = [jax.ShapeDtypeStruct((rows, columns), queries.dtype)]
    scratch += [
        pltpu.VMEM((STRETCH, columns), queries.dtype),
        pltpu.VMEM((columns // HD * (HD + ONES), STRETCH), queries.dtype),
    ]
    operands = [plan] + ([] if row is None else [row])
    smem = len(operands)
    operands.append(queries)
    for b in blocks:
        operands += [b[0], b[1]]
    operands += list(state)
    keys = len(blocks) * STRETCH
    result = pl.pallas_call(
        functools.partial(attend_kernel, [tuple(b[2:]) for b in blocks], row is not None, last),
        out_shape=outs,
        in_specs=[SMEM] * smem + [VMEM] * (len(operands) - smem),
        out_specs=[VMEM] * len(outs),
        scratch_shapes=scratch,
        compiler_params=room(24),
        cost_estimate=pl.CostEstimate(
            flops=4 * rows * columns * keys, bytes_accessed=8 * rows * columns,
            transcendentals=rows * columns // HD * keys,
        ),
        name="attend",
    )(*operands)
    return result[0] if last else tuple(result)


def own_blocks(keys, values):
    return [(keys, values, j * STRETCH, (1 + j, 2)) for j in range(STRETCH_DEV)]


def came_blocks(base, key_came, value_came):
    return [(key_came[d], value_came[d], 0, (base + 2 + 2 * d, 1)) for d in range(2)]


def send(up, down):
    last = lax.axis_size("seq") - 1
    return (
        lax.ppermute(up, "seq", [(i, i + 1) for i in range(last)]),
        lax.ppermute(down, "seq", [(i + 1, i) for i in range(last)]),
    )


def exchange(rounds, plan, queries, keys, values, text_keys, text_values, key_first):
    key_here = send(*key_first)
    values, text_values, *value_first = turn_values(plan, values, text_values)
    value_here = send(*value_first)
    queries, *state = open_state(queries, text_keys, text_values)
    own = own_blocks(keys, values)
    key_came, value_came = ([], []), ([], [])
    for r in range(rounds):
        key_here, queries, state = lax.optimization_barrier((key_here, queries, state))
        blocks = came_blocks(HEADER + r * ROW, key_here, value_here)
        if r + 1 == rounds:
            return attend(plan, None, queries, blocks, state, True)
        for d in range(2):
            key_came[d].append(key_here[d])
            value_came[d].append(value_here[d])
        key_here = send(*choose(plan, r + 1, keys, 0, *key_came))
        value_here = send(*choose(plan, r + 1, values, 1, *value_came))
        state = attend(plan, None, queries, blocks + (own if r + 2 == rounds else []), state, False)


def long_exchange(plan, queries, keys, values, text_keys, text_values, key_first):
    values, text_values, *value_first = turn_values(plan, values, text_values)
    queries, *state = open_state(queries, text_keys, text_values)
    state = attend(plan, None, queries, own_blocks(keys, values), state, False)

    def body(carry):
        r, key_here, value_here, state = carry
        row = r.reshape(1)
        key_here = send(*choose(plan, row, keys, 0, [key_here[0]], [key_here[1]]))
        value_here = send(*choose(plan, row, values, 1, [value_here[0]], [value_here[1]]))
        state = attend(plan, row, queries, came_blocks(0, key_here, value_here), state, False)
        return (r + 1, key_here, value_here, state)

    carry = (jnp.int32(0), tuple(key_first), tuple(value_first), state)
    _, _, _, (acc, stat) = lax.while_loop(lambda c: c[0] < plan[5], body, carry)
    heads = acc.shape[0] // HD
    share = jnp.repeat(1.0 / stat[8 : 8 + heads], HD, axis=0)
    return jnp.transpose(acc * share).astype(queries.dtype)


def shards(
    queries, key_rows, value_rows, text_keys, text_values,
    shot_of_stretch, anchor_stretch, context_count, context_ids,
):
    groups = lax.axis_size("seq")
    tables = (shot_of_stretch, anchor_stretch, context_count, context_ids.T)
    plan, branch, key_up, key_down = make_plan(groups, tables, key_rows)
    branches = [functools.partial(exchange, rounds) for rounds in ROUNDS] + [long_exchange]
    return lax.switch(
        branch[0], branches, plan, queries, key_rows, value_rows, text_keys, text_values,
        (key_up, key_down),
    )


def solution(mesh):
    return jax.shard_map(
        shards,
        mesh=mesh,
        in_specs=(
            P(("rep", "seq"), "shot"),
            P(("rep", "seq"), "shot"),
            P(("rep", "seq"), "shot"),
            P("rep", "shot"),
            P("rep", "shot"),
            P("rep"),
            P("rep"),
            P("rep"),
            P("rep", None),
        ),
        out_specs=P(("rep", "seq"), "shot"),
        check_vma=False,
    )
```

```python
import functools
import math

import jax
import jax.numpy as jnp
from jax import lax
from jax.experimental import pallas as pl
from jax.experimental.pallas import tpu as pltpu
from jax.sharding import PartitionSpec as P

HD = 128
STRETCH = 512
STRETCH_DEV = 2
ROUNDS = (3, 4)
ROW = 8
HEADER = 8
TURN = 256
WIDE = 256
ONES = 16
EXPONENT = HD ** (-0.5) * math.log2(math.e)
SMEM = pl.BlockSpec(memory_space=pltpu.SMEM)
VMEM = pl.BlockSpec(memory_space=pltpu.VMEM)


def room(mebibytes):
    return pltpu.CompilerParams(vmem_limit_bytes=mebibytes * 1024 * 1024)


def quick_plan(groups, shot, anchor, count, ids, keys, plan, targets):
    total = STRETCH_DEV * groups
    slots = ids.shape[0]
    me = lax.axis_index("seq")
    one = jnp.int32(1)

    def listed(c):
        live = count[c]
        yield one << anchor[shot[c]]
        for s in range(slots):
            yield jnp.where(s < live, one << ids[s, c], 0)

    need = []
    for g in range(groups):
        mask = jnp.int32(0)
        for c in range(STRETCH_DEV * g, STRETCH_DEV * (g + 1)):
            for entry in listed(c):
                mask = mask | entry
        need.append(mask)

    once, twice = [], []
    for q in range(STRETCH_DEV):
        c = STRETCH_DEV * me + q
        seen, again = one << c, jnp.int32(0)
        for entry in listed(c):
            again = again | (seen & entry)
            seen = seen | entry
        once.append(seen)
        twice.append(again)

    def times(q, stretch):
        return jnp.where((once[q] & stretch) != 0, 1, 0) + jnp.where((twice[q] & stretch) != 0, 1, 0)

    first_own = one << (STRETCH_DEV * me)
    second_own = first_own << 1
    for q in range(STRETCH_DEV):
        plan[1 + 2 * q] = times(q, first_own)
        plan[2 + 2 * q] = times(q, second_own)

    ways = []
    for d in range(2):
        order = list(range(groups))[:: 1 - 2 * d]
        own = [((1 << STRETCH_DEV) - 1) << (STRETCH_DEV * g) for g in order]
        before = [sum(own[:k]) for k in range(groups)]
        beyond = _beyond(need, order, before)
        ways.append((own, beyond, [own[k] & beyond[k] for k in range(groups)]))

    rounds = jnp.int32(0)
    arrived = [[], []]
    for r in range(ROUNDS[-1]):
        pending = jnp.int32(0)
        for d in range(2):
            _, beyond, onward = ways[d]
            at = me if d == 0 else groups - 1 - me
            picks = []
            for k in range(groups - 1):
                pending = pending | onward[k]
                pick = onward[k] & beyond[groups - 2]
                for g in reversed(range(k, groups - 2)):
                    pick = jnp.where(pick != 0, pick, onward[k] & beyond[g])
                picks.append(pick & -pick)
            for k in range(groups - 1):
                onward[k] = onward[k] & ~picks[k]
            for k in range(1, groups - 1):
                onward[k] = onward[k] | (picks[k - 1] & beyond[k])
            sent, came = jnp.int32(0), jnp.int32(0)
            for k in range(groups - 1):
                sent = jnp.where(at == k, picks[k], sent)
                came = jnp.where(at == k + 1, picks[k], came)
            choice = jnp.where(sent == second_own, 1, 0)
            for i, earlier in enumerate(arrived[d]):
                choice = jnp.where((sent == earlier) & (sent != 0), STRETCH_DEV + i, choice)
            arrived[d].append(came)
            plan[HEADER + r * ROW + d] = choice
            for q in range(STRETCH_DEV):
                plan[HEADER + r * ROW + 2 + 2 * d + q] = times(q, came)
            if r == 0:
                start = pl.multiple_of(choice * STRETCH, STRETCH)
                targets[d][...] = keys[pl.ds(start, STRETCH), :]
        rounds = rounds + jnp.where(pending != 0, 1, 0)
    pending = jnp.int32(0)
    for _, _, onward in ways:
        for left in onward[: groups - 1]:
            pending = pending | left
    return rounds + jnp.where(pending != 0, 1, 0)


def _beyond(need, order, before):
    beyond = []
    for k in range(len(order)):
        mask = jnp.int32(0)
        held = before[k + 1] if k + 1 < len(order) else 0
        for g in order[k + 1 :]:
            mask = mask | need[g]
        beyond.append(mask & held)
    return beyond


def plan_kernel(
    groups, cap, shot, anchor, count, ids, keys,
    plan, branch, key_up, key_down, *scratch,
):
    def list_plan():
        return long_plan(groups, cap, shot, anchor, count, ids, plan, *scratch)

    if STRETCH_DEV * groups <= 16:
        rounds = quick_plan(groups, shot, anchor, count, ids, keys, plan, (key_up, key_down))
        plan[0] = rounds

        @pl.when(rounds > ROUNDS[-1])
        def _():
            list_plan()
    else:
        rounds = list_plan()
        for d, target in enumerate((key_up, key_down)):
            start = pl.multiple_of(plan[HEADER + d] * STRETCH, STRETCH)
            target[...] = keys[pl.ds(start, STRETCH), :]
    branch[0] = sum(jnp.where(rounds > length, 1, 0) for length in ROUNDS)


def long_plan(groups, cap, shot, anchor, count, ids, plan, dest, place, hold, stamp, times, best):
    total = STRETCH_DEV * groups
    slots = ids.shape[0]
    small = total <= 16
    bits = total.bit_length()
    me = lax.axis_index("seq")
    mine = (me, groups - 1 - me)

    def each(length, body):
        if small:
            for i in range(length):
                body(i)
        else:
            lax.fori_loop(0, length, lambda i, c: (body(i), c)[1], 0)

    def clear(e):
        g = e >> 1
        dest[e] = g
        dest[total + e] = groups - 1 - g
        times[e] = 0
        times[total + e] = 0

    each(total, clear)

    def stand(e):
        g = e >> 1
        for d, at in enumerate((g, groups - 1 - g)):
            place[d * total + e] = at
            hold[d * total + e] = e & 1
            stamp[d * total + e] = -1

    each(total, stand)

    def read(c):
        g = c >> 1

        def entry(e):
            dest[e] = jnp.maximum(dest[e], g)
            dest[total + e] = jnp.maximum(dest[total + e], groups - 1 - g)

        entry(anchor[shot[c]])
        live = count[c]
        for s in range(slots):
            entry(jnp.where(s < live, ids[s, c], c))

    each(total, read)

    for q in range(STRETCH_DEV):
        c = STRETCH_DEV * me + q

        def one(e, amount, q=q):
            times[q * total + e] = times[q * total + e] + amount

        one(c, 1)
        one(anchor[shot[c]], 1)
        live = count[c]
        for s in range(slots):
            alive = s < live
            one(jnp.where(alive, ids[s, c], c), jnp.where(alive, 1, 0))

    for q in range(STRETCH_DEV):
        for j in range(STRETCH_DEV):
            plan[1 + 2 * q + j] = times[q * total + STRETCH_DEV * me + j]
    for i in range(ROW * ROUNDS[-1]):
        plan[HEADER + i] = 0

    def remaining():
        return lax.fori_loop(
            0, 2 * total, lambda e, s: s + dest[e] - place[e], jnp.int32(0), unroll=small
        )

    def a_round(r, transit):
        moves = jnp.int32(0)
        for d in range(2):
            base = d * total
            for k in range(groups) if small else ():
                best[k] = -1
            if not small:
                each(groups, lambda k: best.__setitem__(k, jnp.int32(-1)))

            def rank(e, base=base):
                at = place[base + e]
                to = dest[base + e]
                key = (to << bits) | e
                if transit:
                    key = jnp.where(stamp[base + e] == r, key + (groups << bits), key)
                best[at] = jnp.maximum(best[at], jnp.where(to > at, key, -1))

            each(total, rank)
            sent = best[mine[d]]
            mask = (1 << bits) - 1
            plan[HEADER + r * ROW + d] = jnp.where(sent < 0, 0, hold[base + (jnp.maximum(sent, 0) & mask)])
            came = jnp.where(mine[d] > 0, best[jnp.maximum(mine[d] - 1, 0)], -1)
            come = jnp.maximum(came, 0) & mask
            for q in range(STRETCH_DEV):
                plan[HEADER + r * ROW + 2 + 2 * d + q] = jnp.where(came < 0, 0, times[q * total + come])

            @pl.when(came >= 0)
            def _(come=come, base=base):
                hold[base + come] = 2 + r

            def move(k, base=base):
                key = best[k]

                @pl.when(key >= 0)
                def _():
                    e = key & mask
                    place[base + e] = k + 1
                    stamp[base + e] = r + 1

                return jnp.where(key >= 0, 1, 0)

            if small:
                for k in range(groups - 1):
                    moves += move(k)
            else:
                moves += lax.fori_loop(0, groups - 1, lambda k, s: s + move(k), jnp.int32(0))
        return moves

    hops = remaining()

    def go_on(carry):
        return (carry[1] > 0) & (carry[0] < cap)

    rounds, _ = lax.while_loop(
        go_on, lambda c: (c[0] + 1, c[1] - a_round(c[0], False)), (jnp.int32(0), hops)
    )
    plan[0] = rounds

    @pl.when(rounds > ROUNDS[-1])
    def _():
        each(total, stand)
        again, _ = lax.while_loop(
            go_on, lambda c: (c[0] + 1, c[1] - a_round(c[0], True)), (jnp.int32(0), hops)
        )
        plan[5] = again

    return rounds


def make_plan(groups, tables, keys):
    total = STRETCH_DEV * groups
    cap = 2 * groups + 16
    block = jax.ShapeDtypeStruct((STRETCH, keys.shape[1]), keys.dtype)
    return pl.pallas_call(
        functools.partial(plan_kernel, groups, cap),
        out_shape=[
            jax.ShapeDtypeStruct((HEADER + cap * ROW,), jnp.int32),
            jax.ShapeDtypeStruct((1,), jnp.int32),
            block,
            block,
        ],
        in_specs=[SMEM] * 4 + [VMEM],
        out_specs=[SMEM] * 2 + [VMEM] * 2,
        scratch_shapes=[pltpu.SMEM((2 * total,), jnp.int32) for _ in range(5)]
        + [pltpu.SMEM((groups,), jnp.int32)],
        name="plan",
    )(*tables, keys)


def choose_kernel(row, arrivals, axis, plan, *refs):
    if row is None:
        at, own, *refs = refs
        base = HEADER + at[0] * ROW
    else:
        own, *refs = refs
        base = HEADER + row * ROW
    came, outs = refs[: 2 * arrivals], refs[2 * arrivals :]
    for d in range(2):
        choice = plan[base + d]

        @pl.when(choice < STRETCH_DEV)
        def _(d=d, choice=choice):
            part = pl.ds(pl.multiple_of(choice * STRETCH, STRETCH), STRETCH)
            outs[d][...] = own[part, :] if axis == 0 else own[:, part]

        for i in range(arrivals):
            picked = choice == STRETCH_DEV + i if row is not None else choice >= STRETCH_DEV

            @pl.when(picked)
            def _(d=d, i=i):
                outs[d][...] = came[d * arrivals + i][...]


def choose(plan, row, own, axis, up, down):
    static = isinstance(row, int)
    shape = list(own.shape)
    shape[axis] = STRETCH
    block = jax.ShapeDtypeStruct(tuple(shape), own.dtype)
    return pl.pallas_call(
        functools.partial(choose_kernel, row if static else None, len(up), axis),
        out_shape=[block] * 2,
        in_specs=[SMEM] + ([] if static else [SMEM]) + [VMEM] * (1 + 2 * len(up)),
        out_specs=[VMEM] * 2,
        compiler_params=room(8),
        cost_estimate=pl.CostEstimate(flops=0, bytes_accessed=8 * block.size, transcendentals=0),
        name="choose",
    )(plan, *(() if static else (row,)), own, *up, *down)


def score(keys, queries, h, at):
    return jnp.dot(
        jnp.concatenate([keys, keys], axis=1), queries[pl.ds(2 * h * HD, 2 * HD), at],
        preferred_element_type=jnp.float32,
    )


def open_kernel(queries, text_keys, text_values, split, acc, stat):
    heads = queries.shape[1] // HD
    for h in range(heads):
        cols = pl.ds(h * HD, HD)
        for t in range(queries.shape[0] // TURN):
            at = pl.ds(t * TURN, TURN)
            turned = jnp.transpose(queries[at, cols].astype(jnp.float32) * EXPONENT)
            high = turned.astype(jnp.bfloat16)
            split[pl.ds(2 * h * HD, HD), at] = high
            split[pl.ds((2 * h + 1) * HD, HD), at] = (turned - high.astype(jnp.float32)).astype(jnp.bfloat16)
    ones = jnp.ones((ONES, text_keys.shape[0]), jnp.bfloat16)

    def stretch(t, c):
        at = pl.ds(pl.multiple_of(t * STRETCH, STRETCH), STRETCH)
        for h in range(heads):
            cols = pl.ds(h * HD, HD)
            scores = score(text_keys[:, cols], split, h, at)
            peak = jnp.max(scores, axis=0, keepdims=True)
            both = jnp.dot(
                jnp.concatenate([text_values[cols, :], ones], axis=0),
                jnp.exp2(scores - peak).astype(jnp.bfloat16), preferred_element_type=jnp.float32,
            )
            acc[cols, at] = both[:HD]
            stat[h : h + 1, at] = peak
            stat[8 + h : 9 + h, at] = both[HD : HD + 1]
        return c

    lax.fori_loop(0, queries.shape[0] // STRETCH, stretch, 0)


def open_state(queries, text_keys, text_values):
    rows, columns = queries.shape
    return pl.pallas_call(
        open_kernel,
        out_shape=[
            jax.ShapeDtypeStruct((2 * columns, rows), queries.dtype),
            jax.ShapeDtypeStruct((columns, rows), jnp.float32),
            jax.ShapeDtypeStruct((16, rows), jnp.float32),
        ],
        in_specs=[VMEM] * 3,
        out_specs=[VMEM] * 3,
        compiler_params=room(16),
        name="open_state",
    )(queries, text_keys, text_values)


def turn_values_kernel(plan, values, text_values, values_out, text_out, up, down):
    for h in range(values.shape[1] // HD):
        cols = pl.ds(h * HD, HD)
        for source, target in ((values, values_out), (text_values, text_out)):
            for t in range(source.shape[0] // TURN):
                at = pl.ds(t * TURN, TURN)
                target[cols, at] = jnp.transpose(source[at, cols])
    for d, target in enumerate((up, down)):
        start = pl.multiple_of(plan[HEADER + d] * STRETCH, STRETCH)
        target[...] = values_out[:, pl.ds(start, STRETCH)]


def turn_values(plan, values, text_values):
    rows, columns = values.shape
    outs = [(columns, rows), (columns, text_values.shape[0]), (columns, STRETCH), (columns, STRETCH)]
    return pl.pallas_call(
        turn_values_kernel,
        out_shape=[jax.ShapeDtypeStruct(shape, values.dtype) for shape in outs],
        in_specs=[SMEM, VMEM, VMEM],
        out_specs=[VMEM] * 4,
        compiler_params=room(10),
        name="turn_values",
    )(plan, values, text_values)


def attend_kernel(blocks, rowed, last, *refs):
    refs = list(refs)
    plan = refs.pop(0)
    base = HEADER + refs.pop(0)[0] * ROW if rowed else 0
    queries = refs.pop(0)
    block_refs = [(refs.pop(0), refs.pop(0)) for _ in blocks]
    acc_in, stat_in, *refs = refs
    *refs, keys_at, values_at = refs
    if last:
        out, acc, stat = refs
    else:
        acc, stat = refs
    rows = queries.shape[1]
    heads = queries.shape[0] // (2 * HD)
    wide = HD + ONES

    acc[...] = acc_in[...]
    stat[...] = stat_in[...]
    for h in range(heads):
        values_at[pl.ds(h * wide + HD, ONES), :] = jnp.ones((ONES, STRETCH), jnp.bfloat16)

    def step(at, twice):
        units = [(h, w) for h in range(heads) for w in range(STRETCH // WIDE)]

        def place(w):
            return pl.ds(pl.multiple_of(at + w * WIDE, WIDE), WIDE)

        def ahead(h, w):
            return score(keys_at[:, pl.ds(h * HD, HD)], queries, h, place(w))

        def mix(h, w, scores):
            cols, at = pl.ds(h * HD, HD), place(w)
            before = stat[h : h + 1, at]
            peak = jnp.maximum(jnp.max(scores, axis=0, keepdims=True), before)
            keep = jnp.exp2(before - peak)
            weights = jnp.exp2(scores - (peak - twice)).astype(jnp.bfloat16)
            both = jnp.dot(
                values_at[pl.ds(h * wide, wide), :], weights, preferred_element_type=jnp.float32
            )
            acc[cols, at] = both[:HD] + acc[cols, at] * keep
            stat[8 + h : 9 + h, at] = both[HD : HD + 1] + stat[8 + h : 9 + h, at] * keep
            stat[h : h + 1, at] = peak

        scores = ahead(*units[0])
        for i, unit in enumerate(units):
            following = ahead(*units[i + 1]) if i + 1 < len(units) else None
            mix(*unit, scores)
            scores = following

    def visit(b, c):
        place, stride = jnp.int32(0), jnp.int32(0)
        for number, (_, (first, second)) in enumerate(blocks):
            place = jnp.where(b == number, first, place)
            stride = jnp.where(b == number, second, stride)
        place = base + place

        @pl.when(plan[place] + plan[place + stride] > 0)
        def _():
            for number, (start, _) in enumerate(blocks):
                @pl.when(b == number)
                def _(start=start, number=number):
                    part = pl.ds(start, STRETCH)
                    keys_at[...] = block_refs[number][0][part, :]
                    for h in range(heads):
                        values_at[pl.ds(h * wide, HD), :] = block_refs[number][1][pl.ds(h * HD, HD), part]

            def stretch(t, c):
                times = plan[place + t * stride]

                @pl.when(times > 0)
                def _():
                    step(t * STRETCH, jnp.where(times > 1, 1.0, 0.0))

                return c

            lax.fori_loop(0, rows // STRETCH, stretch, 0)

        return c

    lax.fori_loop(0, len(blocks), visit, 0)

    if last:
        for h in range(heads):
            cols = pl.ds(h * HD, HD)
            for t in range(rows // TURN):
                at = pl.ds(t * TURN, TURN)
                share = 1.0 / stat[8 + h : 9 + h, at]
                out[at, cols] = jnp.transpose(acc[cols, at] * share).astype(out.dtype)


def attend(plan, row, queries, blocks, state, last):
    columns, rows = queries.shape[0] // 2, queries.shape[1]
    acc = jax.ShapeDtypeStruct((columns, rows), jnp.float32)
    stat = jax.ShapeDtypeStruct((16, rows), jnp.float32)
    scratch, outs = [], [acc, stat]
    if last:
        scratch = [pltpu.VMEM(acc.shape, acc.dtype), pltpu.VMEM(stat.shape, stat.dtype)]
        outs = [jax.ShapeDtypeStruct((rows, columns), queries.dtype)]
    scratch += [
        pltpu.VMEM((STRETCH, columns), queries.dtype),
        pltpu.VMEM((columns // HD * (HD + ONES), STRETCH), queries.dtype),
    ]
    operands = [plan] + ([] if row is None else [row])
    smem = len(operands)
    operands.append(queries)
    for b in blocks:
        operands += [b[0], b[1]]
    operands += list(state)
    keys = len(blocks) * STRETCH
    result = pl.pallas_call(
        functools.partial(attend_kernel, [tuple(b[2:]) for b in blocks], row is not None, last),
        out_shape=outs,
        in_specs=[SMEM] * smem + [VMEM] * (len(operands) - smem),
        out_specs=[VMEM] * len(outs),
        scratch_shapes=scratch,
        compiler_params=room(24),
        cost_estimate=pl.CostEstimate(
            flops=4 * rows * columns * keys, bytes_accessed=8 * rows * columns,
            transcendentals=rows * columns // HD * keys,
        ),
        name="attend",
    )(*operands)
    return result[0] if last else tuple(result)


def own_blocks(keys, values):
    return [(keys, values, j * STRETCH, (1 + j, 2)) for j in range(STRETCH_DEV)]


def came_blocks(base, key_came, value_came):
    return [(key_came[d], value_came[d], 0, (base + 2 + 2 * d, 1)) for d in range(2)]


def send(up, down):
    last = lax.axis_size("seq") - 1
    return (
        lax.ppermute(up, "seq", [(i, i + 1) for i in range(last)]),
        lax.ppermute(down, "seq", [(i + 1, i) for i in range(last)]),
    )


def exchange(rounds, plan, queries, keys, values, text_keys, text_values, key_first):
    key_here = send(*key_first)
    values, text_values, *value_first = turn_values(plan, values, text_values)
    value_here = send(*value_first)
    queries, *state = open_state(queries, text_keys, text_values)
    own = own_blocks(keys, values)
    key_came, value_came = ([], []), ([], [])
    for r in range(rounds):
        key_here, queries, state = lax.optimization_barrier((key_here, queries, state))
        blocks = came_blocks(HEADER + r * ROW, key_here, value_here)
        if r + 1 == rounds:
            return attend(plan, None, queries, blocks, state, True)
        for d in range(2):
            key_came[d].append(key_here[d])
            value_came[d].append(value_here[d])
        key_here = send(*choose(plan, r + 1, keys, 0, *key_came))
        value_here = send(*choose(plan, r + 1, values, 1, *value_came))
        state = attend(plan, None, queries, blocks + (own if r + 2 == rounds else []), state, False)


def long_exchange(plan, queries, keys, values, text_keys, text_values, key_first):
    values, text_values, *value_first = turn_values(plan, values, text_values)
    queries, *state = open_state(queries, text_keys, text_values)
    state = attend(plan, None, queries, own_blocks(keys, values), state, False)

    def body(carry):
        r, key_here, value_here, state = carry
        row = r.reshape(1)
        key_here = send(*choose(plan, row, keys, 0, [key_here[0]], [key_here[1]]))
        value_here = send(*choose(plan, row, values, 1, [value_here[0]], [value_here[1]]))
        state = attend(plan, row, queries, came_blocks(0, key_here, value_here), state, False)
        return (r + 1, key_here, value_here, state)

    carry = (jnp.int32(0), tuple(key_first), tuple(value_first), state)
    _, _, _, (acc, stat) = lax.while_loop(lambda c: c[0] < plan[5], body, carry)
    heads = acc.shape[0] // HD
    share = jnp.repeat(1.0 / stat[8 : 8 + heads], HD, axis=0)
    return jnp.transpose(acc * share).astype(queries.dtype)


def shards(
    queries, key_rows, value_rows, text_keys, text_values,
    shot_of_stretch, anchor_stretch, context_count, context_ids,
):
    groups = lax.axis_size("seq")
    tables = (shot_of_stretch, anchor_stretch, context_count, context_ids.T)
    plan, branch, key_up, key_down = make_plan(groups, tables, key_rows)
    branches = [functools.partial(exchange, rounds) for rounds in ROUNDS] + [long_exchange]
    return lax.switch(
        branch[0], branches, plan, queries, key_rows, value_rows, text_keys, text_values,
        (key_up, key_down),
    )


def solution(mesh):
    return jax.shard_map(
        shards,
        mesh=mesh,
        in_specs=(
            P(("rep", "seq"), "shot"),
            P(("rep", "seq"), "shot"),
            P(("rep", "seq"), "shot"),
            P("rep", "shot"),
            P("rep", "shot"),
            P("rep"),
            P("rep"),
            P("rep"),
            P("rep", None),
        ),
        out_specs=P(("rep", "seq"), "shot"),
        check_vma=False,
    )
```

```python
import functools
import math

import jax
import jax.numpy as jnp
from jax import lax
from jax.experimental import pallas as pl
from jax.experimental.pallas import tpu as pltpu
from jax.sharding import PartitionSpec as P

HD = 128
STRETCH = 512
STRETCH_DEV = 2
ROUNDS = (3, 4)
ROW = 8
HEADER = 8
TURN = 256
GUARD = 2.0 ** 100
ONES = 16
EXPONENT = HD ** (-0.5) * math.log2(math.e)
SMEM = pl.BlockSpec(memory_space=pltpu.SMEM)
VMEM = pl.BlockSpec(memory_space=pltpu.VMEM)


def room(mebibytes):
    return pltpu.CompilerParams(vmem_limit_bytes=mebibytes * 1024 * 1024)


def quick_plan(groups, shot, anchor, count, ids, keys, plan, targets):
    total = STRETCH_DEV * groups
    slots = ids.shape[0]
    me = lax.axis_index("seq")
    one = jnp.int32(1)

    def listed(c):
        live = count[c]
        yield one << anchor[shot[c]]
        for s in range(slots):
            yield jnp.where(s < live, one << ids[s, c], 0)

    need = []
    for g in range(groups):
        mask = jnp.int32(0)
        for c in range(STRETCH_DEV * g, STRETCH_DEV * (g + 1)):
            for entry in listed(c):
                mask = mask | entry
        need.append(mask)

    once, twice = [], []
    for q in range(STRETCH_DEV):
        c = STRETCH_DEV * me + q
        seen, again = one << c, jnp.int32(0)
        for entry in listed(c):
            again = again | (seen & entry)
            seen = seen | entry
        once.append(seen)
        twice.append(again)

    def times(q, stretch):
        return jnp.where((once[q] & stretch) != 0, 1, 0) + jnp.where((twice[q] & stretch) != 0, 1, 0)

    first_own = one << (STRETCH_DEV * me)
    second_own = first_own << 1
    for q in range(STRETCH_DEV):
        plan[1 + 2 * q] = times(q, first_own)
        plan[2 + 2 * q] = times(q, second_own)

    ways = []
    for d in range(2):
        order = list(range(groups))[:: 1 - 2 * d]
        own = [((1 << STRETCH_DEV) - 1) << (STRETCH_DEV * g) for g in order]
        before = [sum(own[:k]) for k in range(groups)]
        beyond = _beyond(need, order, before)
        ways.append((own, beyond, [own[k] & beyond[k] for k in range(groups)]))

    rounds = jnp.int32(0)
    arrived = [[], []]
    for r in range(ROUNDS[-1]):
        pending = jnp.int32(0)
        for d in range(2):
            _, beyond, onward = ways[d]
            at = me if d == 0 else groups - 1 - me
            picks = []
            for k in range(groups - 1):
                pending = pending | onward[k]
                pick = onward[k] & beyond[groups - 2]
                for g in reversed(range(k, groups - 2)):
                    pick = jnp.where(pick != 0, pick, onward[k] & beyond[g])
                picks.append(pick & -pick)
            for k in range(groups - 1):
                onward[k] = onward[k] & ~picks[k]
            for k in range(1, groups - 1):
                onward[k] = onward[k] | (picks[k - 1] & beyond[k])
            sent, came = jnp.int32(0), jnp.int32(0)
            for k in range(groups - 1):
                sent = jnp.where(at == k, picks[k], sent)
                came = jnp.where(at == k + 1, picks[k], came)
            choice = jnp.where(sent == second_own, 1, 0)
            for i, earlier in enumerate(arrived[d]):
                choice = jnp.where((sent == earlier) & (sent != 0), STRETCH_DEV + i, choice)
            arrived[d].append(came)
            plan[HEADER + r * ROW + d] = choice
            for q in range(STRETCH_DEV):
                plan[HEADER + r * ROW + 2 + 2 * d + q] = times(q, came)
            if r == 0:
                start = pl.multiple_of(choice * STRETCH, STRETCH)
                targets[d][...] = keys[pl.ds(start, STRETCH), :]
        rounds = rounds + jnp.where(pending != 0, 1, 0)
    pending = jnp.int32(0)
    for _, _, onward in ways:
        for left in onward[: groups - 1]:
            pending = pending | left
    return rounds + jnp.where(pending != 0, 1, 0)


def _beyond(need, order, before):
    beyond = []
    for k in range(len(order)):
        mask = jnp.int32(0)
        held = before[k + 1] if k + 1 < len(order) else 0
        for g in order[k + 1 :]:
            mask = mask | need[g]
        beyond.append(mask & held)
    return beyond


def plan_kernel(
    groups, cap, shot, anchor, count, ids, keys,
    plan, branch, key_up, key_down, *scratch,
):
    def list_plan():
        return long_plan(groups, cap, shot, anchor, count, ids, plan, *scratch)

    if STRETCH_DEV * groups <= 16:
        rounds = quick_plan(groups, shot, anchor, count, ids, keys, plan, (key_up, key_down))
        plan[0] = rounds

        @pl.when(rounds > ROUNDS[-1])
        def _():
            list_plan()
    else:
        rounds = list_plan()
        for d, target in enumerate((key_up, key_down)):
            start = pl.multiple_of(plan[HEADER + d] * STRETCH, STRETCH)
            target[...] = keys[pl.ds(start, STRETCH), :]
    branch[0] = sum(jnp.where(rounds > length, 1, 0) for length in ROUNDS)


def long_plan(groups, cap, shot, anchor, count, ids, plan, dest, place, hold, stamp, times, best):
    total = STRETCH_DEV * groups
    slots = ids.shape[0]
    small = total <= 16
    bits = total.bit_length()
    me = lax.axis_index("seq")
    mine = (me, groups - 1 - me)

    def each(length, body):
        if small:
            for i in range(length):
                body(i)
        else:
            lax.fori_loop(0, length, lambda i, c: (body(i), c)[1], 0)

    def clear(e):
        g = e >> 1
        dest[e] = g
        dest[total + e] = groups - 1 - g
        times[e] = 0
        times[total + e] = 0

    each(total, clear)

    def stand(e):
        g = e >> 1
        for d, at in enumerate((g, groups - 1 - g)):
            place[d * total + e] = at
            hold[d * total + e] = e & 1
            stamp[d * total + e] = -1

    each(total, stand)

    def read(c):
        g = c >> 1

        def entry(e):
            dest[e] = jnp.maximum(dest[e], g)
            dest[total + e] = jnp.maximum(dest[total + e], groups - 1 - g)

        entry(anchor[shot[c]])
        live = count[c]
        for s in range(slots):
            entry(jnp.where(s < live, ids[s, c], c))

    each(total, read)

    for q in range(STRETCH_DEV):
        c = STRETCH_DEV * me + q

        def one(e, amount, q=q):
            times[q * total + e] = times[q * total + e] + amount

        one(c, 1)
        one(anchor[shot[c]], 1)
        live = count[c]
        for s in range(slots):
            alive = s < live
            one(jnp.where(alive, ids[s, c], c), jnp.where(alive, 1, 0))

    for q in range(STRETCH_DEV):
        for j in range(STRETCH_DEV):
            plan[1 + 2 * q + j] = times[q * total + STRETCH_DEV * me + j]
    for i in range(ROW * ROUNDS[-1]):
        plan[HEADER + i] = 0

    def remaining():
        return lax.fori_loop(
            0, 2 * total, lambda e, s: s + dest[e] - place[e], jnp.int32(0), unroll=small
        )

    def a_round(r, transit):
        moves = jnp.int32(0)
        for d in range(2):
            base = d * total
            for k in range(groups) if small else ():
                best[k] = -1
            if not small:
                each(groups, lambda k: best.__setitem__(k, jnp.int32(-1)))

            def rank(e, base=base):
                at = place[base + e]
                to = dest[base + e]
                key = (to << bits) | e
                if transit:
                    key = jnp.where(stamp[base + e] == r, key + (groups << bits), key)
                best[at] = jnp.maximum(best[at], jnp.where(to > at, key, -1))

            each(total, rank)
            sent = best[mine[d]]
            mask = (1 << bits) - 1
            plan[HEADER + r * ROW + d] = jnp.where(sent < 0, 0, hold[base + (jnp.maximum(sent, 0) & mask)])
            came = jnp.where(mine[d] > 0, best[jnp.maximum(mine[d] - 1, 0)], -1)
            come = jnp.maximum(came, 0) & mask
            for q in range(STRETCH_DEV):
                plan[HEADER + r * ROW + 2 + 2 * d + q] = jnp.where(came < 0, 0, times[q * total + come])

            @pl.when(came >= 0)
            def _(come=come, base=base):
                hold[base + come] = 2 + r

            def move(k, base=base):
                key = best[k]

                @pl.when(key >= 0)
                def _():
                    e = key & mask
                    place[base + e] = k + 1
                    stamp[base + e] = r + 1

                return jnp.where(key >= 0, 1, 0)

            if small:
                for k in range(groups - 1):
                    moves += move(k)
            else:
                moves += lax.fori_loop(0, groups - 1, lambda k, s: s + move(k), jnp.int32(0))
        return moves

    hops = remaining()

    def go_on(carry):
        return (carry[1] > 0) & (carry[0] < cap)

    rounds, _ = lax.while_loop(
        go_on, lambda c: (c[0] + 1, c[1] - a_round(c[0], False)), (jnp.int32(0), hops)
    )
    plan[0] = rounds

    @pl.when(rounds > ROUNDS[-1])
    def _():
        each(total, stand)
        again, _ = lax.while_loop(
            go_on, lambda c: (c[0] + 1, c[1] - a_round(c[0], True)), (jnp.int32(0), hops)
        )
        plan[5] = again

    return rounds


def make_plan(groups, tables, keys):
    total = STRETCH_DEV * groups
    cap = 2 * groups + 16
    block = jax.ShapeDtypeStruct((STRETCH, keys.shape[1]), keys.dtype)
    return pl.pallas_call(
        functools.partial(plan_kernel, groups, cap),
        out_shape=[
            jax.ShapeDtypeStruct((HEADER + cap * ROW,), jnp.int32),
            jax.ShapeDtypeStruct((1,), jnp.int32),
            block,
            block,
        ],
        in_specs=[SMEM] * 4 + [VMEM],
        out_specs=[SMEM] * 2 + [VMEM] * 2,
        scratch_shapes=[pltpu.SMEM((2 * total,), jnp.int32) for _ in range(5)]
        + [pltpu.SMEM((groups,), jnp.int32)],
        name="plan",
    )(*tables, keys)


def choose_kernel(row, arrivals, axis, plan, *refs):
    if row is None:
        at, own, *refs = refs
        base = HEADER + at[0] * ROW
    else:
        own, *refs = refs
        base = HEADER + row * ROW
    came, outs = refs[: 2 * arrivals], refs[2 * arrivals :]
    for d in range(2):
        choice = plan[base + d]

        @pl.when(choice < STRETCH_DEV)
        def _(d=d, choice=choice):
            part = pl.ds(pl.multiple_of(choice * STRETCH, STRETCH), STRETCH)
            outs[d][...] = own[part, :] if axis == 0 else own[:, part]

        for i in range(arrivals):
            picked = choice == STRETCH_DEV + i if row is not None else choice >= STRETCH_DEV

            @pl.when(picked)
            def _(d=d, i=i):
                outs[d][...] = came[d * arrivals + i][...]


def choose(plan, row, own, axis, up, down):
    static = isinstance(row, int)
    shape = list(own.shape)
    shape[axis] = STRETCH
    block = jax.ShapeDtypeStruct(tuple(shape), own.dtype)
    return pl.pallas_call(
        functools.partial(choose_kernel, row if static else None, len(up), axis),
        out_shape=[block] * 2,
        in_specs=[SMEM] + ([] if static else [SMEM]) + [VMEM] * (1 + 2 * len(up)),
        out_specs=[VMEM] * 2,
        compiler_params=room(8),
        cost_estimate=pl.CostEstimate(flops=0, bytes_accessed=8 * block.size, transcendentals=0),
        name="choose",
    )(plan, *(() if static else (row,)), own, *up, *down)


def score(keys, queries, h, at):
    return jnp.dot(
        jnp.concatenate([keys, keys], axis=1), queries[pl.ds(2 * h * HD, 2 * HD), at],
        preferred_element_type=jnp.float32,
    )


def open_kernel(queries, text_keys, text_values, split, acc, stat):
    heads = queries.shape[1] // HD
    for h in range(heads):
        cols = pl.ds(h * HD, HD)
        for t in range(queries.shape[0] // TURN):
            at = pl.ds(t * TURN, TURN)
            turned = jnp.transpose(queries[at, cols].astype(jnp.float32) * EXPONENT)
            high = turned.astype(jnp.bfloat16)
            split[pl.ds(2 * h * HD, HD), at] = high
            split[pl.ds((2 * h + 1) * HD, HD), at] = (turned - high.astype(jnp.float32)).astype(jnp.bfloat16)
    ones = jnp.ones((ONES, text_keys.shape[0]), jnp.bfloat16)

    def stretch(t, c):
        at = pl.ds(pl.multiple_of(t * STRETCH, STRETCH), STRETCH)
        for h in range(heads):
            cols = pl.ds(h * HD, HD)
            scores = score(text_keys[:, cols], split, h, at)
            peak = jnp.max(scores, axis=0, keepdims=True)
            both = jnp.dot(
                jnp.concatenate([text_values[cols, :], ones], axis=0),
                jnp.exp2(scores - peak).astype(jnp.bfloat16), preferred_element_type=jnp.float32,
            )
            acc[cols, at] = both[:HD]
            stat[h : h + 1, at] = peak
            stat[8 + h : 9 + h, at] = both[HD : HD + 1]
        return c

    lax.fori_loop(0, queries.shape[0] // STRETCH, stretch, 0)


def open_state(queries, text_keys, text_values):
    rows, columns = queries.shape
    return pl.pallas_call(
        open_kernel,
        out_shape=[
            jax.ShapeDtypeStruct((2 * columns, rows), queries.dtype),
            jax.ShapeDtypeStruct((columns, rows), jnp.float32),
            jax.ShapeDtypeStruct((16, rows), jnp.float32),
        ],
        in_specs=[VMEM] * 3,
        out_specs=[VMEM] * 3,
        compiler_params=room(16),
        name="open_state",
    )(queries, text_keys, text_values)


def turn_values_kernel(plan, values, text_values, values_out, text_out, up, down):
    for h in range(values.shape[1] // HD):
        cols = pl.ds(h * HD, HD)
        for source, target in ((values, values_out), (text_values, text_out)):
            for t in range(source.shape[0] // TURN):
                at = pl.ds(t * TURN, TURN)
                target[cols, at] = jnp.transpose(source[at, cols])
    for d, target in enumerate((up, down)):
        start = pl.multiple_of(plan[HEADER + d] * STRETCH, STRETCH)
        target[...] = values_out[:, pl.ds(start, STRETCH)]


def turn_values(plan, values, text_values):
    rows, columns = values.shape
    outs = [(columns, rows), (columns, text_values.shape[0]), (columns, STRETCH), (columns, STRETCH)]
    return pl.pallas_call(
        turn_values_kernel,
        out_shape=[jax.ShapeDtypeStruct(shape, values.dtype) for shape in outs],
        in_specs=[SMEM, VMEM, VMEM],
        out_specs=[VMEM] * 4,
        compiler_params=room(10),
        name="turn_values",
    )(plan, values, text_values)


def attend_kernel(blocks, rowed, last, *refs):
    refs = list(refs)
    plan = refs.pop(0)
    base = HEADER + refs.pop(0)[0] * ROW if rowed else 0
    queries = refs.pop(0)
    block_refs = [(refs.pop(0), refs.pop(0)) for _ in blocks]
    acc_in, stat_in, *refs = refs
    *refs, keys_at, values_at, fine = refs
    if last:
        out, acc, stat = refs
    else:
        acc, stat = refs
    rows = queries.shape[1]
    heads = queries.shape[0] // (2 * HD)
    wide = HD + ONES

    acc[...] = acc_in[...]
    stat[...] = stat_in[...]
    for h in range(heads):
        values_at[pl.ds(h * wide + HD, ONES), :] = jnp.ones((ONES, STRETCH), jnp.bfloat16)

    def step(start, twice):
        at = pl.ds(pl.multiple_of(start, STRETCH), STRETCH)
        lowest = jnp.ones((1, STRETCH), jnp.float32)
        scores = score(keys_at[:, pl.ds(0, HD)], queries, 0, at)
        for h in range(heads):
            following = score(keys_at[:, pl.ds((h + 1) * HD, HD)], queries, h + 1, at) if h + 1 < heads else None
            cols = pl.ds(h * HD, HD)
            weights = jnp.exp2(scores - (stat[h : h + 1, at] - twice)).astype(jnp.bfloat16)
            both = jnp.dot(values_at[pl.ds(h * wide, wide), :], weights, preferred_element_type=jnp.float32)
            mass = both[HD : HD + 1]
            fits = mass < GUARD
            acc[cols, at] = jnp.where(fits, acc[cols, at] + both[:HD], acc[cols, at])
            stat[8 + h : 9 + h, at] += jnp.where(fits, mass, 0.0)
            fit = jnp.where(fits, 1.0, 0.0)
            fine[h : h + 1, :] = fit
            lowest = jnp.minimum(lowest, fit)
            scores = following

        @pl.when(jnp.min(lowest) < 0.5)
        def _():
            lax.fori_loop(0, STRETCH // HD, lambda w, c: (again(start, w * HD, twice), c)[1], 0)

    def again(start, w, twice):
        at = pl.ds(pl.multiple_of(start + w, HD), HD)
        for h in range(heads):
            cols = pl.ds(h * HD, HD)
            scores = score(keys_at[:, cols], queries, h, at)
            before = stat[h : h + 1, at]
            peak = jnp.maximum(jnp.max(scores, axis=0, keepdims=True), before)
            keep = jnp.exp2(before - peak)
            weights = jnp.exp2(scores - (peak - twice)).astype(jnp.bfloat16)
            both = jnp.dot(values_at[pl.ds(h * wide, wide), :], weights, preferred_element_type=jnp.float32)
            miss = fine[h : h + 1, pl.ds(pl.multiple_of(w, HD), HD)] < 0.5
            mass = both[HD : HD + 1] + stat[8 + h : 9 + h, at] * keep
            acc[cols, at] = jnp.where(miss, both[:HD] + acc[cols, at] * keep, acc[cols, at])
            stat[8 + h : 9 + h, at] = jnp.where(miss, mass, stat[8 + h : 9 + h, at])
            stat[h : h + 1, at] = jnp.where(miss, peak, before)

    def visit(b, c):
        place, stride = jnp.int32(0), jnp.int32(0)
        for number, (_, (first, second)) in enumerate(blocks):
            place = jnp.where(b == number, first, place)
            stride = jnp.where(b == number, second, stride)
        place = base + place

        @pl.when(plan[place] + plan[place + stride] > 0)
        def _():
            for number, (start, _) in enumerate(blocks):
                @pl.when(b == number)
                def _(start=start, number=number):
                    part = pl.ds(start, STRETCH)
                    keys_at[...] = block_refs[number][0][part, :]
                    for h in range(heads):
                        values_at[pl.ds(h * wide, HD), :] = block_refs[number][1][pl.ds(h * HD, HD), part]

            def stretch(t, c):
                times = plan[place + t * stride]

                @pl.when(times > 0)
                def _():
                    step(t * STRETCH, jnp.where(times > 1, 1.0, 0.0))

                return c

            lax.fori_loop(0, rows // STRETCH, stretch, 0)

        return c

    lax.fori_loop(0, len(blocks), visit, 0)

    if last:
        for h in range(heads):
            cols = pl.ds(h * HD, HD)
            for t in range(rows // TURN):
                at = pl.ds(t * TURN, TURN)
                share = 1.0 / stat[8 + h : 9 + h, at]
                out[at, cols] = jnp.transpose(acc[cols, at] * share).astype(out.dtype)


def attend(plan, row, queries, blocks, state, last):
    columns, rows = queries.shape[0] // 2, queries.shape[1]
    acc = jax.ShapeDtypeStruct((columns, rows), jnp.float32)
    stat = jax.ShapeDtypeStruct((16, rows), jnp.float32)
    scratch, outs = [], [acc, stat]
    if last:
        scratch = [pltpu.VMEM(acc.shape, acc.dtype), pltpu.VMEM(stat.shape, stat.dtype)]
        outs = [jax.ShapeDtypeStruct((rows, columns), queries.dtype)]
    scratch += [
        pltpu.VMEM((STRETCH, columns), queries.dtype),
        pltpu.VMEM((columns // HD * (HD + ONES), STRETCH), queries.dtype),
        pltpu.VMEM((8, STRETCH), jnp.float32),
    ]
    operands = [plan] + ([] if row is None else [row])
    smem = len(operands)
    operands.append(queries)
    for b in blocks:
        operands += [b[0], b[1]]
    operands += list(state)
    keys = len(blocks) * STRETCH
    result = pl.pallas_call(
        functools.partial(attend_kernel, [tuple(b[2:]) for b in blocks], row is not None, last),
        out_shape=outs,
        in_specs=[SMEM] * smem + [VMEM] * (len(operands) - smem),
        out_specs=[VMEM] * len(outs),
        scratch_shapes=scratch,
        compiler_params=room(24),
        cost_estimate=pl.CostEstimate(
            flops=4 * rows * columns * keys, bytes_accessed=8 * rows * columns,
            transcendentals=rows * columns // HD * keys,
        ),
        name="attend",
    )(*operands)
    return result[0] if last else tuple(result)


def own_blocks(keys, values):
    return [(keys, values, j * STRETCH, (1 + j, 2)) for j in range(STRETCH_DEV)]


def came_blocks(base, key_came, value_came):
    return [(key_came[d], value_came[d], 0, (base + 2 + 2 * d, 1)) for d in range(2)]


def send(up, down):
    last = lax.axis_size("seq") - 1
    return (
        lax.ppermute(up, "seq", [(i, i + 1) for i in range(last)]),
        lax.ppermute(down, "seq", [(i + 1, i) for i in range(last)]),
    )


def exchange(rounds, plan, queries, keys, values, text_keys, text_values, key_first):
    key_here = send(*key_first)
    values, text_values, *value_first = turn_values(plan, values, text_values)
    value_here = send(*value_first)
    queries, *state = open_state(queries, text_keys, text_values)
    own = own_blocks(keys, values)
    key_came, value_came = ([], []), ([], [])
    for r in range(rounds):
        key_here, queries, state = lax.optimization_barrier((key_here, queries, state))
        blocks = came_blocks(HEADER + r * ROW, key_here, value_here)
        if r + 1 == rounds:
            return attend(plan, None, queries, blocks, state, True)
        for d in range(2):
            key_came[d].append(key_here[d])
            value_came[d].append(value_here[d])
        key_here = send(*choose(plan, r + 1, keys, 0, *key_came))
        value_here = send(*choose(plan, r + 1, values, 1, *value_came))
        state = attend(plan, None, queries, blocks + (own if r + 2 == rounds else []), state, False)


def long_exchange(plan, queries, keys, values, text_keys, text_values, key_first):
    values, text_values, *value_first = turn_values(plan, values, text_values)
    queries, *state = open_state(queries, text_keys, text_values)
    state = attend(plan, None, queries, own_blocks(keys, values), state, False)

    def body(carry):
        r, key_here, value_here, state = carry
        row = r.reshape(1)
        key_here = send(*choose(plan, row, keys, 0, [key_here[0]], [key_here[1]]))
        value_here = send(*choose(plan, row, values, 1, [value_here[0]], [value_here[1]]))
        state = attend(plan, row, queries, came_blocks(0, key_here, value_here), state, False)
        return (r + 1, key_here, value_here, state)

    carry = (jnp.int32(0), tuple(key_first), tuple(value_first), state)
    _, _, _, (acc, stat) = lax.while_loop(lambda c: c[0] < plan[5], body, carry)
    heads = acc.shape[0] // HD
    share = jnp.repeat(1.0 / stat[8 : 8 + heads], HD, axis=0)
    return jnp.transpose(acc * share).astype(queries.dtype)


def shards(
    queries, key_rows, value_rows, text_keys, text_values,
    shot_of_stretch, anchor_stretch, context_count, context_ids,
):
    groups = lax.axis_size("seq")
    tables = (shot_of_stretch, anchor_stretch, context_count, context_ids.T)
    plan, branch, key_up, key_down = make_plan(groups, tables, key_rows)
    branches = [functools.partial(exchange, rounds) for rounds in ROUNDS] + [long_exchange]
    return lax.switch(
        branch[0], branches, plan, queries, key_rows, value_rows, text_keys, text_values,
        (key_up, key_down),
    )


def solution(mesh):
    return jax.shard_map(
        shards,
        mesh=mesh,
        in_specs=(
            P(("rep", "seq"), "shot"),
            P(("rep", "seq"), "shot"),
            P(("rep", "seq"), "shot"),
            P("rep", "shot"),
            P("rep", "shot"),
            P("rep"),
            P("rep"),
            P("rep"),
            P("rep", None),
        ),
        out_specs=P(("rep", "seq"), "shot"),
        check_vma=False,
    )
```

```python
import functools
import math

import jax
import jax.numpy as jnp
from jax import lax
from jax.experimental import pallas as pl
from jax.experimental.pallas import tpu as pltpu
from jax.sharding import PartitionSpec as P

HD = 128
STRETCH = 512
STRETCH_DEV = 2
ROUNDS = (3, 4)
ROW = 8
HEADER = 8
TURN = 256
GUARD = 2.0 ** 100
ONES = 16
EXPONENT = HD ** (-0.5) * math.log2(math.e)
SMEM = pl.BlockSpec(memory_space=pltpu.SMEM)
VMEM = pl.BlockSpec(memory_space=pltpu.VMEM)


def room(mebibytes):
    return pltpu.CompilerParams(vmem_limit_bytes=mebibytes * 1024 * 1024)


def quick_plan(groups, shot, anchor, count, ids, keys, plan, targets):
    total = STRETCH_DEV * groups
    slots = ids.shape[0]
    me = lax.axis_index("seq")
    one = jnp.int32(1)

    def listed(c):
        live = count[c]
        yield one << anchor[shot[c]]
        for s in range(slots):
            yield jnp.where(s < live, one << ids[s, c], 0)

    need = []
    for g in range(groups):
        mask = jnp.int32(0)
        for c in range(STRETCH_DEV * g, STRETCH_DEV * (g + 1)):
            for entry in listed(c):
                mask = mask | entry
        need.append(mask)

    once, twice = [], []
    for q in range(STRETCH_DEV):
        c = STRETCH_DEV * me + q
        seen, again = one << c, jnp.int32(0)
        for entry in listed(c):
            again = again | (seen & entry)
            seen = seen | entry
        once.append(seen)
        twice.append(again)

    def times(q, stretch):
        return jnp.where((once[q] & stretch) != 0, 1, 0) + jnp.where((twice[q] & stretch) != 0, 1, 0)

    first_own = one << (STRETCH_DEV * me)
    second_own = first_own << 1
    for q in range(STRETCH_DEV):
        plan[1 + 2 * q] = times(q, first_own)
        plan[2 + 2 * q] = times(q, second_own)

    ways = []
    for d in range(2):
        order = list(range(groups))[:: 1 - 2 * d]
        own = [((1 << STRETCH_DEV) - 1) << (STRETCH_DEV * g) for g in order]
        before = [sum(own[:k]) for k in range(groups)]
        beyond = _beyond(need, order, before)
        ways.append((own, beyond, [own[k] & beyond[k] for k in range(groups)]))

    rounds = jnp.int32(0)
    arrived = [[], []]
    for r in range(ROUNDS[-1]):
        pending = jnp.int32(0)
        for d in range(2):
            _, beyond, onward = ways[d]
            at = me if d == 0 else groups - 1 - me
            picks = []
            for k in range(groups - 1):
                pending = pending | onward[k]
                pick = onward[k] & beyond[groups - 2]
                for g in reversed(range(k, groups - 2)):
                    pick = jnp.where(pick != 0, pick, onward[k] & beyond[g])
                picks.append(pick & -pick)
            for k in range(groups - 1):
                onward[k] = onward[k] & ~picks[k]
            for k in range(1, groups - 1):
                onward[k] = onward[k] | (picks[k - 1] & beyond[k])
            sent, came = jnp.int32(0), jnp.int32(0)
            for k in range(groups - 1):
                sent = jnp.where(at == k, picks[k], sent)
                came = jnp.where(at == k + 1, picks[k], came)
            choice = jnp.where(sent == second_own, 1, 0)
            for i, earlier in enumerate(arrived[d]):
                choice = jnp.where((sent == earlier) & (sent != 0), STRETCH_DEV + i, choice)
            arrived[d].append(came)
            plan[HEADER + r * ROW + d] = choice
            for q in range(STRETCH_DEV):
                plan[HEADER + r * ROW + 2 + 2 * d + q] = times(q, came)
            if r == 0:
                start = pl.multiple_of(choice * STRETCH, STRETCH)
                targets[d][...] = keys[pl.ds(start, STRETCH), :]
        rounds = rounds + jnp.where(pending != 0, 1, 0)
    pending = jnp.int32(0)
    for _, _, onward in ways:
        for left in onward[: groups - 1]:
            pending = pending | left
    return rounds + jnp.where(pending != 0, 1, 0)


def _beyond(need, order, before):
    beyond = []
    for k in range(len(order)):
        mask = jnp.int32(0)
        held = before[k + 1] if k + 1 < len(order) else 0
        for g in order[k + 1 :]:
            mask = mask | need[g]
        beyond.append(mask & held)
    return beyond


def plan_kernel(
    groups, cap, shot, anchor, count, ids, keys,
    plan, branch, key_up, key_down, *scratch,
):
    def list_plan():
        return long_plan(groups, cap, shot, anchor, count, ids, plan, *scratch)

    if STRETCH_DEV * groups <= 16:
        rounds = quick_plan(groups, shot, anchor, count, ids, keys, plan, (key_up, key_down))
        plan[0] = rounds

        @pl.when(rounds > ROUNDS[-1])
        def _():
            list_plan()
    else:
        rounds = list_plan()
        for d, target in enumerate((key_up, key_down)):
            start = pl.multiple_of(plan[HEADER + d] * STRETCH, STRETCH)
            target[...] = keys[pl.ds(start, STRETCH), :]
    branch[0] = sum(jnp.where(rounds > length, 1, 0) for length in ROUNDS)


def long_plan(groups, cap, shot, anchor, count, ids, plan, dest, place, hold, stamp, times, best):
    total = STRETCH_DEV * groups
    slots = ids.shape[0]
    small = total <= 16
    bits = total.bit_length()
    me = lax.axis_index("seq")
    mine = (me, groups - 1 - me)

    def each(length, body):
        if small:
            for i in range(length):
                body(i)
        else:
            lax.fori_loop(0, length, lambda i, c: (body(i), c)[1], 0)

    def clear(e):
        g = e >> 1
        dest[e] = g
        dest[total + e] = groups - 1 - g
        times[e] = 0
        times[total + e] = 0

    each(total, clear)

    def stand(e):
        g = e >> 1
        for d, at in enumerate((g, groups - 1 - g)):
            place[d * total + e] = at
            hold[d * total + e] = e & 1
            stamp[d * total + e] = -1

    each(total, stand)

    def read(c):
        g = c >> 1

        def entry(e):
            dest[e] = jnp.maximum(dest[e], g)
            dest[total + e] = jnp.maximum(dest[total + e], groups - 1 - g)

        entry(anchor[shot[c]])
        live = count[c]
        for s in range(slots):
            entry(jnp.where(s < live, ids[s, c], c))

    each(total, read)

    for q in range(STRETCH_DEV):
        c = STRETCH_DEV * me + q

        def one(e, amount, q=q):
            times[q * total + e] = times[q * total + e] + amount

        one(c, 1)
        one(anchor[shot[c]], 1)
        live = count[c]
        for s in range(slots):
            alive = s < live
            one(jnp.where(alive, ids[s, c], c), jnp.where(alive, 1, 0))

    for q in range(STRETCH_DEV):
        for j in range(STRETCH_DEV):
            plan[1 + 2 * q + j] = times[q * total + STRETCH_DEV * me + j]
    for i in range(ROW * ROUNDS[-1]):
        plan[HEADER + i] = 0

    def remaining():
        return lax.fori_loop(
            0, 2 * total, lambda e, s: s + dest[e] - place[e], jnp.int32(0), unroll=small
        )

    def a_round(r, transit):
        moves = jnp.int32(0)
        for d in range(2):
            base = d * total
            for k in range(groups) if small else ():
                best[k] = -1
            if not small:
                each(groups, lambda k: best.__setitem__(k, jnp.int32(-1)))

            def rank(e, base=base):
                at = place[base + e]
                to = dest[base + e]
                key = (to << bits) | e
                if transit:
                    key = jnp.where(stamp[base + e] == r, key + (groups << bits), key)
                best[at] = jnp.maximum(best[at], jnp.where(to > at, key, -1))

            each(total, rank)
            sent = best[mine[d]]
            mask = (1 << bits) - 1
            plan[HEADER + r * ROW + d] = jnp.where(sent < 0, 0, hold[base + (jnp.maximum(sent, 0) & mask)])
            came = jnp.where(mine[d] > 0, best[jnp.maximum(mine[d] - 1, 0)], -1)
            come = jnp.maximum(came, 0) & mask
            for q in range(STRETCH_DEV):
                plan[HEADER + r * ROW + 2 + 2 * d + q] = jnp.where(came < 0, 0, times[q * total + come])

            @pl.when(came >= 0)
            def _(come=come, base=base):
                hold[base + come] = 2 + r

            def move(k, base=base):
                key = best[k]

                @pl.when(key >= 0)
                def _():
                    e = key & mask
                    place[base + e] = k + 1
                    stamp[base + e] = r + 1

                return jnp.where(key >= 0, 1, 0)

            if small:
                for k in range(groups - 1):
                    moves += move(k)
            else:
                moves += lax.fori_loop(0, groups - 1, lambda k, s: s + move(k), jnp.int32(0))
        return moves

    hops = remaining()

    def go_on(carry):
        return (carry[1] > 0) & (carry[0] < cap)

    rounds, _ = lax.while_loop(
        go_on, lambda c: (c[0] + 1, c[1] - a_round(c[0], False)), (jnp.int32(0), hops)
    )
    plan[0] = rounds

    @pl.when(rounds > ROUNDS[-1])
    def _():
        each(total, stand)
        again, _ = lax.while_loop(
            go_on, lambda c: (c[0] + 1, c[1] - a_round(c[0], True)), (jnp.int32(0), hops)
        )
        plan[5] = again

    return rounds


def make_plan(groups, tables, keys):
    total = STRETCH_DEV * groups
    cap = 2 * groups + 16
    block = jax.ShapeDtypeStruct((STRETCH, keys.shape[1]), keys.dtype)
    return pl.pallas_call(
        functools.partial(plan_kernel, groups, cap),
        out_shape=[
            jax.ShapeDtypeStruct((HEADER + cap * ROW,), jnp.int32),
            jax.ShapeDtypeStruct((1,), jnp.int32),
            block,
            block,
        ],
        in_specs=[SMEM] * 4 + [VMEM],
        out_specs=[SMEM] * 2 + [VMEM] * 2,
        scratch_shapes=[pltpu.SMEM((2 * total,), jnp.int32) for _ in range(5)]
        + [pltpu.SMEM((groups,), jnp.int32)],
        name="plan",
    )(*tables, keys)


def choose_kernel(row, arrivals, axis, plan, *refs):
    if row is None:
        at, own, *refs = refs
        base = HEADER + at[0] * ROW
    else:
        own, *refs = refs
        base = HEADER + row * ROW
    came, outs = refs[: 2 * arrivals], refs[2 * arrivals :]
    for d in range(2):
        choice = plan[base + d]

        @pl.when(choice < STRETCH_DEV)
        def _(d=d, choice=choice):
            part = pl.ds(pl.multiple_of(choice * STRETCH, STRETCH), STRETCH)
            outs[d][...] = own[part, :] if axis == 0 else own[:, part]

        for i in range(arrivals):
            picked = choice == STRETCH_DEV + i if row is not None else choice >= STRETCH_DEV

            @pl.when(picked)
            def _(d=d, i=i):
                outs[d][...] = came[d * arrivals + i][...]


def choose(plan, row, own, axis, up, down):
    static = isinstance(row, int)
    shape = list(own.shape)
    shape[axis] = STRETCH
    block = jax.ShapeDtypeStruct(tuple(shape), own.dtype)
    return pl.pallas_call(
        functools.partial(choose_kernel, row if static else None, len(up), axis),
        out_shape=[block] * 2,
        in_specs=[SMEM] + ([] if static else [SMEM]) + [VMEM] * (1 + 2 * len(up)),
        out_specs=[VMEM] * 2,
        compiler_params=room(8),
        cost_estimate=pl.CostEstimate(flops=0, bytes_accessed=8 * block.size, transcendentals=0),
        name="choose",
    )(plan, *(() if static else (row,)), own, *up, *down)


def score(keys, queries, h, at):
    return jnp.dot(
        jnp.concatenate([keys, keys], axis=1), queries[pl.ds(2 * h * HD, 2 * HD), at],
        preferred_element_type=jnp.float32,
    )


def turn_queries_kernel(queries, split):
    for h in range(queries.shape[1] // HD):
        cols = pl.ds(h * HD, HD)
        for t in range(queries.shape[0] // TURN):
            at = pl.ds(t * TURN, TURN)
            turned = jnp.transpose(queries[at, cols].astype(jnp.float32) * EXPONENT)
            high = turned.astype(jnp.bfloat16)
            split[pl.ds(2 * h * HD, HD), at] = high
            split[pl.ds((2 * h + 1) * HD, HD), at] = (turned - high.astype(jnp.float32)).astype(jnp.bfloat16)


def turn_queries(queries):
    rows, columns = queries.shape
    return pl.pallas_call(
        turn_queries_kernel,
        out_shape=jax.ShapeDtypeStruct((2 * columns, rows), queries.dtype),
        in_specs=[VMEM],
        out_specs=VMEM,
        compiler_params=room(10),
        name="turn_queries",
    )(queries)


def text_kernel(queries, text_keys, text_values, acc, stat):
    ones = jnp.ones((ONES, text_keys.shape[0]), jnp.bfloat16)

    def stretch(t, c):
        at = pl.ds(pl.multiple_of(t * STRETCH, STRETCH), STRETCH)
        for h in range(text_keys.shape[1] // HD):
            cols = pl.ds(h * HD, HD)
            scores = score(text_keys[:, cols], queries, h, at)
            peak = jnp.max(scores, axis=0, keepdims=True)
            both = jnp.dot(
                jnp.concatenate([text_values[cols, :], ones], axis=0),
                jnp.exp2(scores - peak).astype(jnp.bfloat16), preferred_element_type=jnp.float32,
            )
            acc[cols, at] = both[:HD]
            stat[h : h + 1, at] = peak
            stat[8 + h : 9 + h, at] = both[HD : HD + 1]
        return c

    lax.fori_loop(0, queries.shape[1] // STRETCH, stretch, 0)


def attend_text(queries, text_keys, text_values):
    columns, rows = queries.shape[0] // 2, queries.shape[1]
    return pl.pallas_call(
        text_kernel,
        out_shape=[
            jax.ShapeDtypeStruct((columns, rows), jnp.float32),
            jax.ShapeDtypeStruct((16, rows), jnp.float32),
        ],
        in_specs=[VMEM] * 3,
        out_specs=[VMEM] * 2,
        compiler_params=room(16),
        name="attend_text",
    )(queries, text_keys, text_values)


def turn_values_kernel(plan, values, text_values, values_out, text_out, up, down):
    for h in range(values.shape[1] // HD):
        cols = pl.ds(h * HD, HD)
        for source, target in ((values, values_out), (text_values, text_out)):
            for t in range(source.shape[0] // TURN):
                at = pl.ds(t * TURN, TURN)
                target[cols, at] = jnp.transpose(source[at, cols])
    for d, target in enumerate((up, down)):
        start = pl.multiple_of(plan[HEADER + d] * STRETCH, STRETCH)
        target[...] = values_out[:, pl.ds(start, STRETCH)]


def turn_values(plan, values, text_values):
    rows, columns = values.shape
    outs = [(columns, rows), (columns, text_values.shape[0]), (columns, STRETCH), (columns, STRETCH)]
    return pl.pallas_call(
        turn_values_kernel,
        out_shape=[jax.ShapeDtypeStruct(shape, values.dtype) for shape in outs],
        in_specs=[SMEM, VMEM, VMEM],
        out_specs=[VMEM] * 4,
        compiler_params=room(10),
        name="turn_values",
    )(plan, values, text_values)


def attend_kernel(blocks, rowed, last, *refs):
    refs = list(refs)
    plan = refs.pop(0)
    base = HEADER + refs.pop(0)[0] * ROW if rowed else 0
    queries = refs.pop(0)
    block_refs = [(refs.pop(0), refs.pop(0)) for _ in blocks]
    acc_in, stat_in, *refs = refs
    *refs, keys_at, values_at, fine = refs
    if last:
        out, acc, stat = refs
    else:
        acc, stat = refs
    rows = queries.shape[1]
    heads = queries.shape[0] // (2 * HD)
    wide = HD + ONES

    acc[...] = acc_in[...]
    stat[...] = stat_in[...]
    for h in range(heads):
        values_at[pl.ds(h * wide + HD, ONES), :] = jnp.ones((ONES, STRETCH), jnp.bfloat16)

    def step(start, twice):
        at = pl.ds(pl.multiple_of(start, STRETCH), STRETCH)
        lowest = jnp.ones((1, STRETCH), jnp.float32)
        scores = score(keys_at[:, pl.ds(0, HD)], queries, 0, at)
        for h in range(heads):
            following = score(keys_at[:, pl.ds((h + 1) * HD, HD)], queries, h + 1, at) if h + 1 < heads else None
            cols = pl.ds(h * HD, HD)
            weights = jnp.exp2(scores - (stat[h : h + 1, at] - twice)).astype(jnp.bfloat16)
            both = jnp.dot(values_at[pl.ds(h * wide, wide), :], weights, preferred_element_type=jnp.float32)
            mass = both[HD : HD + 1]
            fits = mass < GUARD
            acc[cols, at] = jnp.where(fits, acc[cols, at] + both[:HD], acc[cols, at])
            stat[8 + h : 9 + h, at] += jnp.where(fits, mass, 0.0)
            fit = jnp.where(fits, 1.0, 0.0)
            fine[h : h + 1, :] = fit
            lowest = jnp.minimum(lowest, fit)
            scores = following

        @pl.when(jnp.min(lowest) < 0.5)
        def _():
            lax.fori_loop(0, STRETCH // HD, lambda w, c: (again(start, w * HD, twice), c)[1], 0)

    def again(start, w, twice):
        at = pl.ds(pl.multiple_of(start + w, HD), HD)
        for h in range(heads):
            cols = pl.ds(h * HD, HD)
            scores = score(keys_at[:, cols], queries, h, at)
            before = stat[h : h + 1, at]
            peak = jnp.maximum(jnp.max(scores, axis=0, keepdims=True), before)
            keep = jnp.exp2(before - peak)
            weights = jnp.exp2(scores - (peak - twice)).astype(jnp.bfloat16)
            both = jnp.dot(values_at[pl.ds(h * wide, wide), :], weights, preferred_element_type=jnp.float32)
            miss = fine[h : h + 1, pl.ds(pl.multiple_of(w, HD), HD)] < 0.5
            mass = both[HD : HD + 1] + stat[8 + h : 9 + h, at] * keep
            acc[cols, at] = jnp.where(miss, both[:HD] + acc[cols, at] * keep, acc[cols, at])
            stat[8 + h : 9 + h, at] = jnp.where(miss, mass, stat[8 + h : 9 + h, at])
            stat[h : h + 1, at] = jnp.where(miss, peak, before)

    def visit(b, c):
        place, stride = jnp.int32(0), jnp.int32(0)
        for number, (_, (first, second)) in enumerate(blocks):
            place = jnp.where(b == number, first, place)
            stride = jnp.where(b == number, second, stride)
        place = base + place

        @pl.when(plan[place] + plan[place + stride] > 0)
        def _():
            for number, (start, _) in enumerate(blocks):
                @pl.when(b == number)
                def _(start=start, number=number):
                    part = pl.ds(start, STRETCH)
                    keys_at[...] = block_refs[number][0][part, :]
                    for h in range(heads):
                        values_at[pl.ds(h * wide, HD), :] = block_refs[number][1][pl.ds(h * HD, HD), part]

            def stretch(t, c):
                times = plan[place + t * stride]

                @pl.when(times > 0)
                def _():
                    step(t * STRETCH, jnp.where(times > 1, 1.0, 0.0))

                return c

            lax.fori_loop(0, rows // STRETCH, stretch, 0)

        return c

    lax.fori_loop(0, len(blocks), visit, 0)

    if last:
        for h in range(heads):
            cols = pl.ds(h * HD, HD)
            for t in range(rows // TURN):
                at = pl.ds(t * TURN, TURN)
                share = 1.0 / stat[8 + h : 9 + h, at]
                out[at, cols] = jnp.transpose(acc[cols, at] * share).astype(out.dtype)


def attend(plan, row, queries, blocks, state, last):
    columns, rows = queries.shape[0] // 2, queries.shape[1]
    acc = jax.ShapeDtypeStruct((columns, rows), jnp.float32)
    stat = jax.ShapeDtypeStruct((16, rows), jnp.float32)
    scratch, outs = [], [acc, stat]
    if last:
        scratch = [pltpu.VMEM(acc.shape, acc.dtype), pltpu.VMEM(stat.shape, stat.dtype)]
        outs = [jax.ShapeDtypeStruct((rows, columns), queries.dtype)]
    scratch += [
        pltpu.VMEM((STRETCH, columns), queries.dtype),
        pltpu.VMEM((columns // HD * (HD + ONES), STRETCH), queries.dtype),
        pltpu.VMEM((8, STRETCH), jnp.float32),
    ]
    operands = [plan] + ([] if row is None else [row])
    smem = len(operands)
    operands.append(queries)
    for b in blocks:
        operands += [b[0], b[1]]
    operands += list(state)
    keys = len(blocks) * STRETCH
    result = pl.pallas_call(
        functools.partial(attend_kernel, [tuple(b[2:]) for b in blocks], row is not None, last),
        out_shape=outs,
        in_specs=[SMEM] * smem + [VMEM] * (len(operands) - smem),
        out_specs=[VMEM] * len(outs),
        scratch_shapes=scratch,
        compiler_params=room(24),
        cost_estimate=pl.CostEstimate(
            flops=4 * rows * columns * keys, bytes_accessed=8 * rows * columns,
            transcendentals=rows * columns // HD * keys,
        ),
        name="attend",
    )(*operands)
    return result[0] if last else tuple(result)


def own_blocks(keys, values):
    return [(keys, values, j * STRETCH, (1 + j, 2)) for j in range(STRETCH_DEV)]


def came_blocks(base, key_came, value_came):
    return [(key_came[d], value_came[d], 0, (base + 2 + 2 * d, 1)) for d in range(2)]


def send(up, down):
    last = lax.axis_size("seq") - 1
    return (
        lax.ppermute(up, "seq", [(i, i + 1) for i in range(last)]),
        lax.ppermute(down, "seq", [(i + 1, i) for i in range(last)]),
    )


def exchange(rounds, plan, queries, keys, values, text_keys, text_values, key_first):
    key_here = send(*key_first)
    values, text_values, *value_first = turn_values(plan, values, text_values)
    value_here = send(*value_first)
    key_came, value_came = ([], []), ([], [])
    state, waiting = None, []

    def work(window):
        nonlocal queries, state
        if window == 0:
            queries = turn_queries(queries)
        elif window == 1:
            state = attend_text(queries, text_keys, text_values)
        else:
            state = attend(plan, None, queries, [waiting.pop(0)], state, False)

    def before(blocks):
        nonlocal queries, state
        blocks, queries, state = lax.optimization_barrier((blocks, queries, state))
        return blocks

    for r in range(rounds):
        key_here = before(key_here)
        if r + 1 == rounds:
            break
        for d in range(2):
            key_came[d].append(key_here[d])
        key_next = send(*before(choose(plan, r + 1, keys, 0, *key_came)))
        work(2 * r)
        value_here = before(value_here)
        for d in range(2):
            value_came[d].append(value_here[d])
        waiting += came_blocks(HEADER + r * ROW, key_here, value_here)
        key_here, value_here = key_next, send(*before(choose(plan, r + 1, values, 1, *value_came)))
        if r + 2 < rounds:
            work(2 * r + 1)
        else:
            state = attend(plan, None, queries, own_blocks(keys, values) + waiting, state, False)
    blocks = came_blocks(HEADER + r * ROW, key_here, value_here)
    return attend(plan, None, queries, blocks, state, True)


def long_exchange(plan, queries, keys, values, text_keys, text_values, key_first):
    values, text_values, *value_first = turn_values(plan, values, text_values)
    queries = turn_queries(queries)
    state = attend_text(queries, text_keys, text_values)
    state = attend(plan, None, queries, own_blocks(keys, values), state, False)

    def body(carry):
        r, key_here, value_here, state = carry
        row = r.reshape(1)
        key_here = send(*choose(plan, row, keys, 0, [key_here[0]], [key_here[1]]))
        value_here = send(*choose(plan, row, values, 1, [value_here[0]], [value_here[1]]))
        state = attend(plan, row, queries, came_blocks(0, key_here, value_here), state, False)
        return (r + 1, key_here, value_here, state)

    carry = (jnp.int32(0), tuple(key_first), tuple(value_first), state)
    _, _, _, (acc, stat) = lax.while_loop(lambda c: c[0] < plan[5], body, carry)
    heads = acc.shape[0] // HD
    share = jnp.repeat(1.0 / stat[8 : 8 + heads], HD, axis=0)
    return jnp.transpose(acc * share).astype(queries.dtype)


def shards(
    queries, key_rows, value_rows, text_keys, text_values,
    shot_of_stretch, anchor_stretch, context_count, context_ids,
):
    groups = lax.axis_size("seq")
    tables = (shot_of_stretch, anchor_stretch, context_count, context_ids.T)
    plan, branch, key_up, key_down = make_plan(groups, tables, key_rows)
    branches = [functools.partial(exchange, rounds) for rounds in ROUNDS] + [long_exchange]
    return lax.switch(
        branch[0], branches, plan, queries, key_rows, value_rows, text_keys, text_values,
        (key_up, key_down),
    )


def solution(mesh):
    return jax.shard_map(
        shards,
        mesh=mesh,
        in_specs=(
            P(("rep", "seq"), "shot"),
            P(("rep", "seq"), "shot"),
            P(("rep", "seq"), "shot"),
            P("rep", "shot"),
            P("rep", "shot"),
            P("rep"),
            P("rep"),
            P("rep"),
            P("rep", None),
        ),
        out_specs=P(("rep", "seq"), "shot"),
        check_vma=False,
    )
```

```python
import functools
import math

import jax
import jax.numpy as jnp
from jax import lax
from jax.experimental import pallas as pl
from jax.experimental.pallas import tpu as pltpu
from jax.sharding import PartitionSpec as P

HD = 128
STRETCH = 512
STRETCH_DEV = 2
ROUNDS = (3, 4)
ROW = 8
HEADER = 8
TURN = 256
GUARD = 2.0 ** 100
ONES = 16
EXPONENT = HD ** (-0.5) * math.log2(math.e)
SMEM = pl.BlockSpec(memory_space=pltpu.SMEM)
VMEM = pl.BlockSpec(memory_space=pltpu.VMEM)


def room(mebibytes):
    return pltpu.CompilerParams(vmem_limit_bytes=mebibytes * 1024 * 1024)


def quick_plan(groups, shot, anchor, count, ids, keys, plan, targets):
    total = STRETCH_DEV * groups
    slots = ids.shape[0]
    me = lax.axis_index("seq")
    one = jnp.int32(1)

    def listed(c):
        live = count[c]
        yield one << anchor[shot[c]]
        for s in range(slots):
            yield jnp.where(s < live, one << ids[s, c], 0)

    need = []
    for g in range(groups):
        mask = jnp.int32(0)
        for c in range(STRETCH_DEV * g, STRETCH_DEV * (g + 1)):
            for entry in listed(c):
                mask = mask | entry
        need.append(mask)

    once, twice = [], []
    for q in range(STRETCH_DEV):
        c = STRETCH_DEV * me + q
        seen, again = one << c, jnp.int32(0)
        for entry in listed(c):
            again = again | (seen & entry)
            seen = seen | entry
        once.append(seen)
        twice.append(again)

    def times(q, stretch):
        return jnp.where((once[q] & stretch) != 0, 1, 0) + jnp.where((twice[q] & stretch) != 0, 1, 0)

    first_own = one << (STRETCH_DEV * me)
    second_own = first_own << 1
    for q in range(STRETCH_DEV):
        plan[1 + 2 * q] = times(q, first_own)
        plan[2 + 2 * q] = times(q, second_own)

    ways = []
    for d in range(2):
        order = list(range(groups))[:: 1 - 2 * d]
        own = [((1 << STRETCH_DEV) - 1) << (STRETCH_DEV * g) for g in order]
        before = [sum(own[:k]) for k in range(groups)]
        beyond = _beyond(need, order, before)
        ways.append((own, beyond, [own[k] & beyond[k] for k in range(groups)]))

    rounds = jnp.int32(0)
    arrived = [[], []]
    for r in range(ROUNDS[-1]):
        pending = jnp.int32(0)
        for d in range(2):
            _, beyond, onward = ways[d]
            at = me if d == 0 else groups - 1 - me
            picks = []
            for k in range(groups - 1):
                pending = pending | onward[k]
                pick = onward[k] & beyond[groups - 2]
                for g in reversed(range(k, groups - 2)):
                    pick = jnp.where(pick != 0, pick, onward[k] & beyond[g])
                picks.append(pick & -pick)
            for k in range(groups - 1):
                onward[k] = onward[k] & ~picks[k]
            for k in range(1, groups - 1):
                onward[k] = onward[k] | (picks[k - 1] & beyond[k])
            sent, came = jnp.int32(0), jnp.int32(0)
            for k in range(groups - 1):
                sent = jnp.where(at == k, picks[k], sent)
                came = jnp.where(at == k + 1, picks[k], came)
            choice = jnp.where(sent == second_own, 1, 0)
            for i, earlier in enumerate(arrived[d]):
                choice = jnp.where((sent == earlier) & (sent != 0), STRETCH_DEV + i, choice)
            arrived[d].append(came)
            plan[HEADER + r * ROW + d] = choice
            for q in range(STRETCH_DEV):
                plan[HEADER + r * ROW + 2 + 2 * d + q] = times(q, came)
            if r == 0:
                start = pl.multiple_of(choice * STRETCH, STRETCH)
                targets[d][...] = keys[pl.ds(start, STRETCH), :]
        rounds = rounds + jnp.where(pending != 0, 1, 0)
    pending = jnp.int32(0)
    for _, _, onward in ways:
        for left in onward[: groups - 1]:
            pending = pending | left
    return rounds + jnp.where(pending != 0, 1, 0)


def _beyond(need, order, before):
    beyond = []
    for k in range(len(order)):
        mask = jnp.int32(0)
        held = before[k + 1] if k + 1 < len(order) else 0
        for g in order[k + 1 :]:
            mask = mask | need[g]
        beyond.append(mask & held)
    return beyond


def plan_kernel(
    groups, cap, shot, anchor, count, ids, keys,
    plan, branch, key_up, key_down, *scratch,
):
    def list_plan():
        return long_plan(groups, cap, shot, anchor, count, ids, plan, *scratch)

    if STRETCH_DEV * groups <= 16:
        rounds = quick_plan(groups, shot, anchor, count, ids, keys, plan, (key_up, key_down))
        plan[0] = rounds

        @pl.when(rounds > ROUNDS[-1])
        def _():
            list_plan()
    else:
        rounds = list_plan()
        for d, target in enumerate((key_up, key_down)):
            start = pl.multiple_of(plan[HEADER + d] * STRETCH, STRETCH)
            target[...] = keys[pl.ds(start, STRETCH), :]
    branch[0] = sum(jnp.where(rounds > length, 1, 0) for length in ROUNDS)


def long_plan(groups, cap, shot, anchor, count, ids, plan, dest, place, hold, stamp, times, best):
    total = STRETCH_DEV * groups
    slots = ids.shape[0]
    small = total <= 16
    bits = total.bit_length()
    me = lax.axis_index("seq")
    mine = (me, groups - 1 - me)

    def each(length, body):
        if small:
            for i in range(length):
                body(i)
        else:
            lax.fori_loop(0, length, lambda i, c: (body(i), c)[1], 0)

    def clear(e):
        g = e >> 1
        dest[e] = g
        dest[total + e] = groups - 1 - g
        times[e] = 0
        times[total + e] = 0

    each(total, clear)

    def stand(e):
        g = e >> 1
        for d, at in enumerate((g, groups - 1 - g)):
            place[d * total + e] = at
            hold[d * total + e] = e & 1
            stamp[d * total + e] = -1

    each(total, stand)

    def read(c):
        g = c >> 1

        def entry(e):
            dest[e] = jnp.maximum(dest[e], g)
            dest[total + e] = jnp.maximum(dest[total + e], groups - 1 - g)

        entry(anchor[shot[c]])
        live = count[c]
        for s in range(slots):
            entry(jnp.where(s < live, ids[s, c], c))

    each(total, read)

    for q in range(STRETCH_DEV):
        c = STRETCH_DEV * me + q

        def one(e, amount, q=q):
            times[q * total + e] = times[q * total + e] + amount

        one(c, 1)
        one(anchor[shot[c]], 1)
        live = count[c]
        for s in range(slots):
            alive = s < live
            one(jnp.where(alive, ids[s, c], c), jnp.where(alive, 1, 0))

    for q in range(STRETCH_DEV):
        for j in range(STRETCH_DEV):
            plan[1 + 2 * q + j] = times[q * total + STRETCH_DEV * me + j]
    for i in range(ROW * ROUNDS[-1]):
        plan[HEADER + i] = 0

    def remaining():
        return lax.fori_loop(
            0, 2 * total, lambda e, s: s + dest[e] - place[e], jnp.int32(0), unroll=small
        )

    def a_round(r, transit):
        moves = jnp.int32(0)
        for d in range(2):
            base = d * total
            for k in range(groups) if small else ():
                best[k] = -1
            if not small:
                each(groups, lambda k: best.__setitem__(k, jnp.int32(-1)))

            def rank(e, base=base):
                at = place[base + e]
                to = dest[base + e]
                key = (to << bits) | e
                if transit:
                    key = jnp.where(stamp[base + e] == r, key + (groups << bits), key)
                best[at] = jnp.maximum(best[at], jnp.where(to > at, key, -1))

            each(total, rank)
            sent = best[mine[d]]
            mask = (1 << bits) - 1
            plan[HEADER + r * ROW + d] = jnp.where(sent < 0, 0, hold[base + (jnp.maximum(sent, 0) & mask)])
            came = jnp.where(mine[d] > 0, best[jnp.maximum(mine[d] - 1, 0)], -1)
            come = jnp.maximum(came, 0) & mask
            for q in range(STRETCH_DEV):
                plan[HEADER + r * ROW + 2 + 2 * d + q] = jnp.where(came < 0, 0, times[q * total + come])

            @pl.when(came >= 0)
            def _(come=come, base=base):
                hold[base + come] = 2 + r

            def move(k, base=base):
                key = best[k]

                @pl.when(key >= 0)
                def _():
                    e = key & mask
                    place[base + e] = k + 1
                    stamp[base + e] = r + 1

                return jnp.where(key >= 0, 1, 0)

            if small:
                for k in range(groups - 1):
                    moves += move(k)
            else:
                moves += lax.fori_loop(0, groups - 1, lambda k, s: s + move(k), jnp.int32(0))
        return moves

    hops = remaining()

    def go_on(carry):
        return (carry[1] > 0) & (carry[0] < cap)

    rounds, _ = lax.while_loop(
        go_on, lambda c: (c[0] + 1, c[1] - a_round(c[0], False)), (jnp.int32(0), hops)
    )
    plan[0] = rounds

    @pl.when(rounds > ROUNDS[-1])
    def _():
        each(total, stand)
        again, _ = lax.while_loop(
            go_on, lambda c: (c[0] + 1, c[1] - a_round(c[0], True)), (jnp.int32(0), hops)
        )
        plan[5] = again

    return rounds


def make_plan(groups, tables, keys):
    total = STRETCH_DEV * groups
    cap = 2 * groups + 16
    block = jax.ShapeDtypeStruct((STRETCH, keys.shape[1]), keys.dtype)
    return pl.pallas_call(
        functools.partial(plan_kernel, groups, cap),
        out_shape=[
            jax.ShapeDtypeStruct((HEADER + cap * ROW,), jnp.int32),
            jax.ShapeDtypeStruct((1,), jnp.int32),
            block,
            block,
        ],
        in_specs=[SMEM] * 4 + [VMEM],
        out_specs=[SMEM] * 2 + [VMEM] * 2,
        scratch_shapes=[pltpu.SMEM((2 * total,), jnp.int32) for _ in range(5)]
        + [pltpu.SMEM((groups,), jnp.int32)],
        name="plan",
    )(*tables, keys)


def choose_kernel(row, arrivals, axis, plan, *refs):
    if row is None:
        at, own, *refs = refs
        base = HEADER + at[0] * ROW
    else:
        own, *refs = refs
        base = HEADER + row * ROW
    came, outs = refs[: 2 * arrivals], refs[2 * arrivals :]
    for d in range(2):
        choice = plan[base + d]

        @pl.when(choice < STRETCH_DEV)
        def _(d=d, choice=choice):
            part = pl.ds(pl.multiple_of(choice * STRETCH, STRETCH), STRETCH)
            outs[d][...] = own[part, :] if axis == 0 else own[:, part]

        for i in range(arrivals):
            picked = choice == STRETCH_DEV + i if row is not None else choice >= STRETCH_DEV

            @pl.when(picked)
            def _(d=d, i=i):
                outs[d][...] = came[d * arrivals + i][...]


def choose(plan, row, own, axis, up, down):
    static = isinstance(row, int)
    shape = list(own.shape)
    shape[axis] = STRETCH
    block = jax.ShapeDtypeStruct(tuple(shape), own.dtype)
    return pl.pallas_call(
        functools.partial(choose_kernel, row if static else None, len(up), axis),
        out_shape=[block] * 2,
        in_specs=[SMEM] + ([] if static else [SMEM]) + [VMEM] * (1 + 2 * len(up)),
        out_specs=[VMEM] * 2,
        compiler_params=room(8),
        cost_estimate=pl.CostEstimate(flops=0, bytes_accessed=8 * block.size, transcendentals=0),
        name="choose",
    )(plan, *(() if static else (row,)), own, *up, *down)


def score(keys, queries, h, at):
    return jnp.dot(
        jnp.concatenate([keys, keys], axis=1), queries[pl.ds(2 * h * HD, 2 * HD), at],
        preferred_element_type=jnp.float32,
    )


def turn_queries_kernel(queries, split):
    for h in range(queries.shape[1] // HD):
        cols = pl.ds(h * HD, HD)
        for t in range(queries.shape[0] // TURN):
            at = pl.ds(t * TURN, TURN)
            turned = jnp.transpose(queries[at, cols].astype(jnp.float32) * EXPONENT)
            high = turned.astype(jnp.bfloat16)
            split[pl.ds(2 * h * HD, HD), at] = high
            split[pl.ds((2 * h + 1) * HD, HD), at] = (turned - high.astype(jnp.float32)).astype(jnp.bfloat16)


def turn_queries(queries):
    rows, columns = queries.shape
    return pl.pallas_call(
        turn_queries_kernel,
        out_shape=jax.ShapeDtypeStruct((2 * columns, rows), queries.dtype),
        in_specs=[VMEM],
        out_specs=VMEM,
        compiler_params=room(10),
        name="turn_queries",
    )(queries)


def text_kernel(queries, text_keys, text_values, acc, stat):
    ones = jnp.ones((ONES, text_keys.shape[0]), jnp.bfloat16)

    def stretch(t, c):
        at = pl.ds(pl.multiple_of(t * STRETCH, STRETCH), STRETCH)
        for h in range(text_keys.shape[1] // HD):
            cols = pl.ds(h * HD, HD)
            scores = score(text_keys[:, cols], queries, h, at)
            peak = jnp.max(scores, axis=0, keepdims=True)
            both = jnp.dot(
                jnp.concatenate([text_values[cols, :], ones], axis=0),
                jnp.exp2(scores - peak).astype(jnp.bfloat16), preferred_element_type=jnp.float32,
            )
            acc[cols, at] = both[:HD]
            stat[h : h + 1, at] = peak
            stat[8 + h : 9 + h, at] = both[HD : HD + 1]
        return c

    lax.fori_loop(0, queries.shape[1] // STRETCH, stretch, 0)


def attend_text(queries, text_keys, text_values):
    columns, rows = queries.shape[0] // 2, queries.shape[1]
    return pl.pallas_call(
        text_kernel,
        out_shape=[
            jax.ShapeDtypeStruct((columns, rows), jnp.float32),
            jax.ShapeDtypeStruct((16, rows), jnp.float32),
        ],
        in_specs=[VMEM] * 3,
        out_specs=[VMEM] * 2,
        compiler_params=room(16),
        name="attend_text",
    )(queries, text_keys, text_values)


def turn_values_kernel(plan, values, text_values, values_out, text_out, up, down):
    for h in range(values.shape[1] // HD):
        cols = pl.ds(h * HD, HD)
        for source, target in ((values, values_out), (text_values, text_out)):
            for t in range(source.shape[0] // TURN):
                at = pl.ds(t * TURN, TURN)
                target[cols, at] = jnp.transpose(source[at, cols])
    for d, target in enumerate((up, down)):
        start = pl.multiple_of(plan[HEADER + d] * STRETCH, STRETCH)
        target[...] = values_out[:, pl.ds(start, STRETCH)]


def turn_values(plan, values, text_values):
    rows, columns = values.shape
    outs = [(columns, rows), (columns, text_values.shape[0]), (columns, STRETCH), (columns, STRETCH)]
    return pl.pallas_call(
        turn_values_kernel,
        out_shape=[jax.ShapeDtypeStruct(shape, values.dtype) for shape in outs],
        in_specs=[SMEM, VMEM, VMEM],
        out_specs=[VMEM] * 4,
        compiler_params=room(10),
        name="turn_values",
    )(plan, values, text_values)


def attend_kernel(blocks, rowed, last, *refs):
    refs = list(refs)
    plan = refs.pop(0)
    base = HEADER + refs.pop(0)[0] * ROW if rowed else 0
    queries = refs.pop(0)
    block_refs = [(refs.pop(0), refs.pop(0)) for _ in blocks]
    acc_in, stat_in, *refs = refs
    *refs, keys_at, values_at, fine = refs
    if last:
        out, acc, stat = refs
    else:
        acc, stat = refs
    rows = queries.shape[1]
    heads = queries.shape[0] // (2 * HD)
    wide = HD + ONES

    acc[...] = acc_in[...]
    stat[...] = stat_in[...]
    for h in range(heads):
        values_at[pl.ds(h * wide + HD, ONES), :] = jnp.ones((ONES, STRETCH), jnp.bfloat16)

    def step(start, twice):
        at = pl.ds(pl.multiple_of(start, STRETCH), STRETCH)
        lowest = jnp.ones((1, STRETCH), jnp.float32)
        scores = score(keys_at[:, pl.ds(0, HD)], queries, 0, at)
        for h in range(heads):
            following = score(keys_at[:, pl.ds((h + 1) * HD, HD)], queries, h + 1, at) if h + 1 < heads else None
            cols = pl.ds(h * HD, HD)
            weights = jnp.exp2(scores - (stat[h : h + 1, at] - twice)).astype(jnp.bfloat16)
            both = jnp.dot(values_at[pl.ds(h * wide, wide), :], weights, preferred_element_type=jnp.float32)
            mass = both[HD : HD + 1]
            fits = mass < GUARD
            acc[cols, at] = jnp.where(fits, acc[cols, at] + both[:HD], acc[cols, at])
            stat[8 + h : 9 + h, at] += jnp.where(fits, mass, 0.0)
            fit = jnp.where(fits, 1.0, 0.0)
            fine[h : h + 1, :] = fit
            lowest = jnp.minimum(lowest, fit)
            scores = following

        @pl.when(jnp.min(lowest) < 0.5)
        def _():
            lax.fori_loop(0, STRETCH // HD, lambda w, c: (again(start, w * HD, twice), c)[1], 0)

    def again(start, w, twice):
        at = pl.ds(pl.multiple_of(start + w, HD), HD)
        for h in range(heads):
            cols = pl.ds(h * HD, HD)
            scores = score(keys_at[:, cols], queries, h, at)
            before = stat[h : h + 1, at]
            peak = jnp.maximum(jnp.max(scores, axis=0, keepdims=True), before)
            keep = jnp.exp2(before - peak)
            weights = jnp.exp2(scores - (peak - twice)).astype(jnp.bfloat16)
            both = jnp.dot(values_at[pl.ds(h * wide, wide), :], weights, preferred_element_type=jnp.float32)
            miss = fine[h : h + 1, pl.ds(pl.multiple_of(w, HD), HD)] < 0.5
            mass = both[HD : HD + 1] + stat[8 + h : 9 + h, at] * keep
            acc[cols, at] = jnp.where(miss, both[:HD] + acc[cols, at] * keep, acc[cols, at])
            stat[8 + h : 9 + h, at] = jnp.where(miss, mass, stat[8 + h : 9 + h, at])
            stat[h : h + 1, at] = jnp.where(miss, peak, before)

    def visit(b, c):
        place, stride = jnp.int32(0), jnp.int32(0)
        for number, (_, (first, second)) in enumerate(blocks):
            place = jnp.where(b == number, first, place)
            stride = jnp.where(b == number, second, stride)
        place = base + place

        @pl.when(plan[place] + plan[place + stride] > 0)
        def _():
            for number, (start, _) in enumerate(blocks):
                @pl.when(b == number)
                def _(start=start, number=number):
                    part = pl.ds(start, STRETCH)
                    keys_at[...] = block_refs[number][0][part, :]
                    for h in range(heads):
                        values_at[pl.ds(h * wide, HD), :] = block_refs[number][1][pl.ds(h * HD, HD), part]

            def stretch(t, c):
                times = plan[place + t * stride]

                @pl.when(times > 0)
                def _():
                    step(t * STRETCH, jnp.where(times > 1, 1.0, 0.0))

                return c

            lax.fori_loop(0, rows // STRETCH, stretch, 0)

        return c

    lax.fori_loop(0, len(blocks), visit, 0)

    if last:
        for h in range(heads):
            cols = pl.ds(h * HD, HD)
            for t in range(rows // TURN):
                at = pl.ds(t * TURN, TURN)
                share = 1.0 / stat[8 + h : 9 + h, at]
                out[at, cols] = jnp.transpose(acc[cols, at] * share).astype(out.dtype)


def attend(plan, row, queries, blocks, state, last):
    columns, rows = queries.shape[0] // 2, queries.shape[1]
    acc = jax.ShapeDtypeStruct((columns, rows), jnp.float32)
    stat = jax.ShapeDtypeStruct((16, rows), jnp.float32)
    scratch, outs = [], [acc, stat]
    if last:
        scratch = [pltpu.VMEM(acc.shape, acc.dtype), pltpu.VMEM(stat.shape, stat.dtype)]
        outs = [jax.ShapeDtypeStruct((rows, columns), queries.dtype)]
    scratch += [
        pltpu.VMEM((STRETCH, columns), queries.dtype),
        pltpu.VMEM((columns // HD * (HD + ONES), STRETCH), queries.dtype),
        pltpu.VMEM((8, STRETCH), jnp.float32),
    ]
    operands = [plan] + ([] if row is None else [row])
    smem = len(operands)
    operands.append(queries)
    for b in blocks:
        operands += [b[0], b[1]]
    operands += list(state)
    keys = len(blocks) * STRETCH
    result = pl.pallas_call(
        functools.partial(attend_kernel, [tuple(b[2:]) for b in blocks], row is not None, last),
        out_shape=outs,
        in_specs=[SMEM] * smem + [VMEM] * (len(operands) - smem),
        out_specs=[VMEM] * len(outs),
        scratch_shapes=scratch,
        compiler_params=room(24),
        cost_estimate=pl.CostEstimate(
            flops=4 * rows * columns * keys, bytes_accessed=8 * rows * columns,
            transcendentals=rows * columns // HD * keys,
        ),
        name="attend",
    )(*operands)
    return result[0] if last else tuple(result)


def own_blocks(keys, values):
    return [(keys, values, j * STRETCH, (1 + j, 2)) for j in range(STRETCH_DEV)]


def came_blocks(base, key_came, value_came):
    return [(key_came[d], value_came[d], 0, (base + 2 + 2 * d, 1)) for d in range(2)]


def send(up, down):
    last = lax.axis_size("seq") - 1
    return (
        lax.ppermute(up, "seq", [(i, i + 1) for i in range(last)]),
        lax.ppermute(down, "seq", [(i + 1, i) for i in range(last)]),
    )


def exchange(rounds, plan, queries, keys, values, text_keys, text_values, key_first):
    key_here = send(*key_first)
    values, text_values, *value_first = turn_values(plan, values, text_values)
    queries = turn_queries(queries)
    value_first, queries = lax.optimization_barrier((value_first, queries))
    value_here = send(*value_first)
    state = attend_text(queries, text_keys, text_values)
    key_came, value_came = ([], []), ([], [])
    waiting = []

    def before(blocks):
        nonlocal state
        blocks, state = lax.optimization_barrier((blocks, state))
        return blocks

    for r in range(rounds - 1):
        key_here = before(key_here)
        for d in range(2):
            key_came[d].append(key_here[d])
        key_next = send(*before(choose(plan, r + 1, keys, 0, *key_came)))
        if r > 0:
            state = attend(plan, None, queries, [waiting.pop(0)], state, False)
        value_here = before(value_here)
        for d in range(2):
            value_came[d].append(value_here[d])
        waiting += came_blocks(HEADER + r * ROW, key_here, value_here)
        key_here, value_here = key_next, send(*before(choose(plan, r + 1, values, 1, *value_came)))
    blocks = came_blocks(HEADER + (rounds - 1) * ROW, key_here, value_here)
    state = attend(plan, None, queries, own_blocks(keys, values) + waiting, state, False)
    return attend(plan, None, queries, blocks, state, True)


def long_exchange(plan, queries, keys, values, text_keys, text_values, key_first):
    values, text_values, *value_first = turn_values(plan, values, text_values)
    queries = turn_queries(queries)
    state = attend_text(queries, text_keys, text_values)
    state = attend(plan, None, queries, own_blocks(keys, values), state, False)

    def body(carry):
        r, key_here, value_here, state = carry
        row = r.reshape(1)
        key_here = send(*choose(plan, row, keys, 0, [key_here[0]], [key_here[1]]))
        value_here = send(*choose(plan, row, values, 1, [value_here[0]], [value_here[1]]))
        state = attend(plan, row, queries, came_blocks(0, key_here, value_here), state, False)
        return (r + 1, key_here, value_here, state)

    carry = (jnp.int32(0), tuple(key_first), tuple(value_first), state)
    _, _, _, (acc, stat) = lax.while_loop(lambda c: c[0] < plan[5], body, carry)
    heads = acc.shape[0] // HD
    share = jnp.repeat(1.0 / stat[8 : 8 + heads], HD, axis=0)
    return jnp.transpose(acc * share).astype(queries.dtype)


def shards(
    queries, key_rows, value_rows, text_keys, text_values,
    shot_of_stretch, anchor_stretch, context_count, context_ids,
):
    groups = lax.axis_size("seq")
    tables = (shot_of_stretch, anchor_stretch, context_count, context_ids.T)
    plan, branch, key_up, key_down = make_plan(groups, tables, key_rows)
    branches = [functools.partial(exchange, rounds) for rounds in ROUNDS] + [long_exchange]
    return lax.switch(
        branch[0], branches, plan, queries, key_rows, value_rows, text_keys, text_values,
        (key_up, key_down),
    )


def solution(mesh):
    return jax.shard_map(
        shards,
        mesh=mesh,
        in_specs=(
            P(("rep", "seq"), "shot"),
            P(("rep", "seq"), "shot"),
            P(("rep", "seq"), "shot"),
            P("rep", "shot"),
            P("rep", "shot"),
            P("rep"),
            P("rep"),
            P("rep"),
            P("rep", None),
        ),
        out_specs=P(("rep", "seq"), "shot"),
        check_vma=False,
    )
```

```python
import functools
import math

import jax
import jax.numpy as jnp
from jax import lax
from jax.experimental import pallas as pl
from jax.experimental.pallas import tpu as pltpu
from jax.sharding import PartitionSpec as P

HD = 128
STRETCH = 512
STRETCH_DEV = 2
ROUNDS = (3, 4)
ROW = 8
HEADER = 8
TURN = 256
GUARD = 2.0 ** 100
ONES = 16
EXPONENT = HD ** (-0.5) * math.log2(math.e)
SMEM = pl.BlockSpec(memory_space=pltpu.SMEM)
VMEM = pl.BlockSpec(memory_space=pltpu.VMEM)


def room(mebibytes):
    return pltpu.CompilerParams(vmem_limit_bytes=mebibytes * 1024 * 1024)


def quick_plan(groups, shot, anchor, count, ids, keys, plan, targets):
    total = STRETCH_DEV * groups
    slots = ids.shape[0]
    me = lax.axis_index("seq")
    one = jnp.int32(1)

    def listed(c):
        live = count[c]
        yield one << anchor[shot[c]]
        for s in range(slots):
            yield jnp.where(s < live, one << ids[s, c], 0)

    need = []
    for g in range(groups):
        mask = jnp.int32(0)
        for c in range(STRETCH_DEV * g, STRETCH_DEV * (g + 1)):
            for entry in listed(c):
                mask = mask | entry
        need.append(mask)

    once, twice = [], []
    for q in range(STRETCH_DEV):
        c = STRETCH_DEV * me + q
        seen, again = one << c, jnp.int32(0)
        for entry in listed(c):
            again = again | (seen & entry)
            seen = seen | entry
        once.append(seen)
        twice.append(again)

    def times(q, stretch):
        return jnp.where((once[q] & stretch) != 0, 1, 0) + jnp.where((twice[q] & stretch) != 0, 1, 0)

    first_own = one << (STRETCH_DEV * me)
    second_own = first_own << 1
    for q in range(STRETCH_DEV):
        plan[1 + 2 * q] = times(q, first_own)
        plan[2 + 2 * q] = times(q, second_own)

    ways = []
    for d in range(2):
        order = list(range(groups))[:: 1 - 2 * d]
        own = [((1 << STRETCH_DEV) - 1) << (STRETCH_DEV * g) for g in order]
        before = [sum(own[:k]) for k in range(groups)]
        beyond = _beyond(need, order, before)
        ways.append((own, beyond, [own[k] & beyond[k] for k in range(groups)]))

    rounds = jnp.int32(0)
    arrived = [[], []]
    for r in range(ROUNDS[-1]):
        pending = jnp.int32(0)
        for d in range(2):
            _, beyond, onward = ways[d]
            at = me if d == 0 else groups - 1 - me
            picks = []
            for k in range(groups - 1):
                pending = pending | onward[k]
                pick = onward[k] & beyond[groups - 2]
                for g in reversed(range(k, groups - 2)):
                    pick = jnp.where(pick != 0, pick, onward[k] & beyond[g])
                picks.append(pick & -pick)
            for k in range(groups - 1):
                onward[k] = onward[k] & ~picks[k]
            for k in range(1, groups - 1):
                onward[k] = onward[k] | (picks[k - 1] & beyond[k])
            sent, came = jnp.int32(0), jnp.int32(0)
            for k in range(groups - 1):
                sent = jnp.where(at == k, picks[k], sent)
                came = jnp.where(at == k + 1, picks[k], came)
            choice = jnp.where(sent == second_own, 1, 0)
            for i, earlier in enumerate(arrived[d]):
                choice = jnp.where((sent == earlier) & (sent != 0), STRETCH_DEV + i, choice)
            arrived[d].append(came)
            plan[HEADER + r * ROW + d] = choice
            for q in range(STRETCH_DEV):
                plan[HEADER + r * ROW + 2 + 2 * d + q] = times(q, came)
            if r == 0:
                start = pl.multiple_of(choice * STRETCH, STRETCH)
                targets[d][...] = keys[pl.ds(start, STRETCH), :]
        rounds = rounds + jnp.where(pending != 0, 1, 0)
    pending = jnp.int32(0)
    for _, _, onward in ways:
        for left in onward[: groups - 1]:
            pending = pending | left
    return rounds + jnp.where(pending != 0, 1, 0)


def _beyond(need, order, before):
    beyond = []
    for k in range(len(order)):
        mask = jnp.int32(0)
        held = before[k + 1] if k + 1 < len(order) else 0
        for g in order[k + 1 :]:
            mask = mask | need[g]
        beyond.append(mask & held)
    return beyond


def plan_kernel(
    groups, cap, shot, anchor, count, ids, keys,
    plan, branch, key_up, key_down, *scratch,
):
    def list_plan():
        return long_plan(groups, cap, shot, anchor, count, ids, plan, *scratch)

    if STRETCH_DEV * groups <= 16:
        rounds = quick_plan(groups, shot, anchor, count, ids, keys, plan, (key_up, key_down))
        plan[0] = rounds

        @pl.when(rounds > ROUNDS[-1])
        def _():
            list_plan()
    else:
        rounds = list_plan()
        for d, target in enumerate((key_up, key_down)):
            start = pl.multiple_of(plan[HEADER + d] * STRETCH, STRETCH)
            target[...] = keys[pl.ds(start, STRETCH), :]
    branch[0] = sum(jnp.where(rounds > length, 1, 0) for length in ROUNDS)


def long_plan(groups, cap, shot, anchor, count, ids, plan, dest, place, hold, stamp, times, best):
    total = STRETCH_DEV * groups
    slots = ids.shape[0]
    small = total <= 16
    bits = total.bit_length()
    me = lax.axis_index("seq")
    mine = (me, groups - 1 - me)

    def each(length, body):
        if small:
            for i in range(length):
                body(i)
        else:
            lax.fori_loop(0, length, lambda i, c: (body(i), c)[1], 0)

    def clear(e):
        g = e >> 1
        dest[e] = g
        dest[total + e] = groups - 1 - g
        times[e] = 0
        times[total + e] = 0

    each(total, clear)

    def stand(e):
        g = e >> 1
        for d, at in enumerate((g, groups - 1 - g)):
            place[d * total + e] = at
            hold[d * total + e] = e & 1
            stamp[d * total + e] = -1

    each(total, stand)

    def read(c):
        g = c >> 1

        def entry(e):
            dest[e] = jnp.maximum(dest[e], g)
            dest[total + e] = jnp.maximum(dest[total + e], groups - 1 - g)

        entry(anchor[shot[c]])
        live = count[c]
        for s in range(slots):
            entry(jnp.where(s < live, ids[s, c], c))

    each(total, read)

    for q in range(STRETCH_DEV):
        c = STRETCH_DEV * me + q

        def one(e, amount, q=q):
            times[q * total + e] = times[q * total + e] + amount

        one(c, 1)
        one(anchor[shot[c]], 1)
        live = count[c]
        for s in range(slots):
            alive = s < live
            one(jnp.where(alive, ids[s, c], c), jnp.where(alive, 1, 0))

    for q in range(STRETCH_DEV):
        for j in range(STRETCH_DEV):
            plan[1 + 2 * q + j] = times[q * total + STRETCH_DEV * me + j]
    for i in range(ROW * ROUNDS[-1]):
        plan[HEADER + i] = 0

    def remaining():
        return lax.fori_loop(
            0, 2 * total, lambda e, s: s + dest[e] - place[e], jnp.int32(0), unroll=small
        )

    def a_round(r, transit):
        moves = jnp.int32(0)
        for d in range(2):
            base = d * total
            for k in range(groups) if small else ():
                best[k] = -1
            if not small:
                each(groups, lambda k: best.__setitem__(k, jnp.int32(-1)))

            def rank(e, base=base):
                at = place[base + e]
                to = dest[base + e]
                key = (to << bits) | e
                if transit:
                    key = jnp.where(stamp[base + e] == r, key + (groups << bits), key)
                best[at] = jnp.maximum(best[at], jnp.where(to > at, key, -1))

            each(total, rank)
            sent = best[mine[d]]
            mask = (1 << bits) - 1
            plan[HEADER + r * ROW + d] = jnp.where(sent < 0, 0, hold[base + (jnp.maximum(sent, 0) & mask)])
            came = jnp.where(mine[d] > 0, best[jnp.maximum(mine[d] - 1, 0)], -1)
            come = jnp.maximum(came, 0) & mask
            for q in range(STRETCH_DEV):
                plan[HEADER + r * ROW + 2 + 2 * d + q] = jnp.where(came < 0, 0, times[q * total + come])

            @pl.when(came >= 0)
            def _(come=come, base=base):
                hold[base + come] = 2 + r

            def move(k, base=base):
                key = best[k]

                @pl.when(key >= 0)
                def _():
                    e = key & mask
                    place[base + e] = k + 1
                    stamp[base + e] = r + 1

                return jnp.where(key >= 0, 1, 0)

            if small:
                for k in range(groups - 1):
                    moves += move(k)
            else:
                moves += lax.fori_loop(0, groups - 1, lambda k, s: s + move(k), jnp.int32(0))
        return moves

    hops = remaining()

    def go_on(carry):
        return (carry[1] > 0) & (carry[0] < cap)

    rounds, _ = lax.while_loop(
        go_on, lambda c: (c[0] + 1, c[1] - a_round(c[0], False)), (jnp.int32(0), hops)
    )
    plan[0] = rounds

    @pl.when(rounds > ROUNDS[-1])
    def _():
        each(total, stand)
        again, _ = lax.while_loop(
            go_on, lambda c: (c[0] + 1, c[1] - a_round(c[0], True)), (jnp.int32(0), hops)
        )
        plan[5] = again

    return rounds


def make_plan(groups, tables, keys):
    total = STRETCH_DEV * groups
    cap = 2 * groups + 16
    block = jax.ShapeDtypeStruct((STRETCH, keys.shape[1]), keys.dtype)
    return pl.pallas_call(
        functools.partial(plan_kernel, groups, cap),
        out_shape=[
            jax.ShapeDtypeStruct((HEADER + cap * ROW,), jnp.int32),
            jax.ShapeDtypeStruct((1,), jnp.int32),
            block,
            block,
        ],
        in_specs=[SMEM] * 4 + [VMEM],
        out_specs=[SMEM] * 2 + [VMEM] * 2,
        scratch_shapes=[pltpu.SMEM((2 * total,), jnp.int32) for _ in range(5)]
        + [pltpu.SMEM((groups,), jnp.int32)],
        name="plan",
    )(*tables, keys)


def choose_kernel(row, arrivals, axis, plan, *refs):
    if row is None:
        at, own, *refs = refs
        base = HEADER + at[0] * ROW
    else:
        own, *refs = refs
        base = HEADER + row * ROW
    came, outs = refs[: 2 * arrivals], refs[2 * arrivals :]
    for d in range(2):
        choice = plan[base + d]

        @pl.when(choice < STRETCH_DEV)
        def _(d=d, choice=choice):
            part = pl.ds(pl.multiple_of(choice * STRETCH, STRETCH), STRETCH)
            outs[d][...] = own[part, :] if axis == 0 else own[:, part]

        for i in range(arrivals):
            picked = choice == STRETCH_DEV + i if row is not None else choice >= STRETCH_DEV

            @pl.when(picked)
            def _(d=d, i=i):
                outs[d][...] = came[d * arrivals + i][...]


def choose(plan, row, own, axis, up, down):
    static = isinstance(row, int)
    shape = list(own.shape)
    shape[axis] = STRETCH
    block = jax.ShapeDtypeStruct(tuple(shape), own.dtype)
    return pl.pallas_call(
        functools.partial(choose_kernel, row if static else None, len(up), axis),
        out_shape=[block] * 2,
        in_specs=[SMEM] + ([] if static else [SMEM]) + [VMEM] * (1 + 2 * len(up)),
        out_specs=[VMEM] * 2,
        compiler_params=room(8),
        cost_estimate=pl.CostEstimate(flops=0, bytes_accessed=8 * block.size, transcendentals=0),
        name="choose",
    )(plan, *(() if static else (row,)), own, *up, *down)


def score(keys, queries, h, at):
    return jnp.dot(
        jnp.concatenate([keys, keys], axis=1), queries[pl.ds(2 * h * HD, 2 * HD), at],
        preferred_element_type=jnp.float32,
    )


def turn_queries_kernel(queries, split):
    for h in range(queries.shape[1] // HD):
        cols = pl.ds(h * HD, HD)
        for t in range(queries.shape[0] // TURN):
            at = pl.ds(t * TURN, TURN)
            turned = jnp.transpose(queries[at, cols].astype(jnp.float32) * EXPONENT)
            high = turned.astype(jnp.bfloat16)
            split[pl.ds(2 * h * HD, HD), at] = high
            split[pl.ds((2 * h + 1) * HD, HD), at] = (turned - high.astype(jnp.float32)).astype(jnp.bfloat16)


def turn_queries(queries):
    rows, columns = queries.shape
    return pl.pallas_call(
        turn_queries_kernel,
        out_shape=jax.ShapeDtypeStruct((2 * columns, rows), queries.dtype),
        in_specs=[VMEM],
        out_specs=VMEM,
        compiler_params=room(10),
        name="turn_queries",
    )(queries)


def text_kernel(queries, text_keys, text_values, acc, stat):
    ones = jnp.ones((ONES, text_keys.shape[0]), jnp.bfloat16)

    def stretch(t, c):
        at = pl.ds(pl.multiple_of(t * STRETCH, STRETCH), STRETCH)
        for h in range(text_keys.shape[1] // HD):
            cols = pl.ds(h * HD, HD)
            scores = score(text_keys[:, cols], queries, h, at)
            peak = jnp.max(scores, axis=0, keepdims=True)
            both = jnp.dot(
                jnp.concatenate([text_values[cols, :], ones], axis=0),
                jnp.exp2(scores - peak).astype(jnp.bfloat16), preferred_element_type=jnp.float32,
            )
            acc[cols, at] = both[:HD]
            stat[h : h + 1, at] = peak
            stat[8 + h : 9 + h, at] = both[HD : HD + 1]
        return c

    lax.fori_loop(0, queries.shape[1] // STRETCH, stretch, 0)


def attend_text(queries, text_keys, text_values):
    columns, rows = queries.shape[0] // 2, queries.shape[1]
    return pl.pallas_call(
        text_kernel,
        out_shape=[
            jax.ShapeDtypeStruct((columns, rows), jnp.float32),
            jax.ShapeDtypeStruct((16, rows), jnp.float32),
        ],
        in_specs=[VMEM] * 3,
        out_specs=[VMEM] * 2,
        compiler_params=room(16),
        name="attend_text",
    )(queries, text_keys, text_values)


def turn_values_kernel(plan, values, text_values, values_out, text_out, up, down):
    for h in range(values.shape[1] // HD):
        cols = pl.ds(h * HD, HD)
        for source, target in ((values, values_out), (text_values, text_out)):
            for t in range(source.shape[0] // TURN):
                at = pl.ds(t * TURN, TURN)
                target[cols, at] = jnp.transpose(source[at, cols])
    for d, target in enumerate((up, down)):
        start = pl.multiple_of(plan[HEADER + d] * STRETCH, STRETCH)
        target[...] = values_out[:, pl.ds(start, STRETCH)]


def turn_values(plan, values, text_values):
    rows, columns = values.shape
    outs = [(columns, rows), (columns, text_values.shape[0]), (columns, STRETCH), (columns, STRETCH)]
    return pl.pallas_call(
        turn_values_kernel,
        out_shape=[jax.ShapeDtypeStruct(shape, values.dtype) for shape in outs],
        in_specs=[SMEM, VMEM, VMEM],
        out_specs=[VMEM] * 4,
        compiler_params=room(10),
        name="turn_values",
    )(plan, values, text_values)


def attend_kernel(blocks, rowed, last, *refs):
    refs = list(refs)
    plan = refs.pop(0)
    base = HEADER + refs.pop(0)[0] * ROW if rowed else 0
    queries = refs.pop(0)
    block_refs = [(refs.pop(0), refs.pop(0)) for _ in blocks]
    acc_in, stat_in, *refs = refs
    *refs, keys_at, values_at, fine = refs
    if last:
        out, acc, stat = refs
    else:
        acc, stat = refs
    rows = queries.shape[1]
    heads = queries.shape[0] // (2 * HD)
    wide = HD + ONES

    acc[...] = acc_in[...]
    stat[...] = stat_in[...]
    for h in range(heads):
        values_at[pl.ds(h * wide + HD, ONES), :] = jnp.ones((ONES, STRETCH), jnp.bfloat16)

    def step(start, twice):
        at = pl.ds(pl.multiple_of(start, STRETCH), STRETCH)
        lowest = jnp.ones((1, STRETCH), jnp.float32)
        scores = score(keys_at[:, pl.ds(0, HD)], queries, 0, at)
        for h in range(heads):
            following = score(keys_at[:, pl.ds((h + 1) * HD, HD)], queries, h + 1, at) if h + 1 < heads else None
            cols = pl.ds(h * HD, HD)
            weights = jnp.exp2(scores - (stat[h : h + 1, at] - twice)).astype(jnp.bfloat16)
            both = jnp.dot(values_at[pl.ds(h * wide, wide), :], weights, preferred_element_type=jnp.float32)
            mass = both[HD : HD + 1]
            fits = mass < GUARD
            acc[cols, at] = jnp.where(fits, acc[cols, at] + both[:HD], acc[cols, at])
            stat[8 + h : 9 + h, at] += jnp.where(fits, mass, 0.0)
            fit = jnp.where(fits, 1.0, 0.0)
            fine[h : h + 1, :] = fit
            lowest = jnp.minimum(lowest, fit)
            scores = following

        @pl.when(jnp.min(lowest) < 0.5)
        def _():
            lax.fori_loop(0, STRETCH // HD, lambda w, c: (again(start, w * HD, twice), c)[1], 0)

    def again(start, w, twice):
        at = pl.ds(pl.multiple_of(start + w, HD), HD)
        for h in range(heads):
            cols = pl.ds(h * HD, HD)
            scores = score(keys_at[:, cols], queries, h, at)
            before = stat[h : h + 1, at]
            peak = jnp.maximum(jnp.max(scores, axis=0, keepdims=True), before)
            keep = jnp.exp2(before - peak)
            weights = jnp.exp2(scores - (peak - twice)).astype(jnp.bfloat16)
            both = jnp.dot(values_at[pl.ds(h * wide, wide), :], weights, preferred_element_type=jnp.float32)
            miss = fine[h : h + 1, pl.ds(pl.multiple_of(w, HD), HD)] < 0.5
            mass = both[HD : HD + 1] + stat[8 + h : 9 + h, at] * keep
            acc[cols, at] = jnp.where(miss, both[:HD] + acc[cols, at] * keep, acc[cols, at])
            stat[8 + h : 9 + h, at] = jnp.where(miss, mass, stat[8 + h : 9 + h, at])
            stat[h : h + 1, at] = jnp.where(miss, peak, before)

    def visit(b, c):
        place, stride = jnp.int32(0), jnp.int32(0)
        for number, (_, (first, second)) in enumerate(blocks):
            place = jnp.where(b == number, first, place)
            stride = jnp.where(b == number, second, stride)
        place = base + place

        @pl.when(plan[place] + plan[place + stride] > 0)
        def _():
            for number, (start, _) in enumerate(blocks):
                @pl.when(b == number)
                def _(start=start, number=number):
                    part = pl.ds(start, STRETCH)
                    keys_at[...] = block_refs[number][0][part, :]
                    for h in range(heads):
                        values_at[pl.ds(h * wide, HD), :] = block_refs[number][1][pl.ds(h * HD, HD), part]

            def stretch(t, c):
                times = plan[place + t * stride]

                @pl.when(times > 0)
                def _():
                    step(t * STRETCH, jnp.where(times > 1, 1.0, 0.0))

                return c

            lax.fori_loop(0, rows // STRETCH, stretch, 0)

        return c

    lax.fori_loop(0, len(blocks), visit, 0)

    if last:
        for h in range(heads):
            cols = pl.ds(h * HD, HD)
            for t in range(rows // TURN):
                at = pl.ds(t * TURN, TURN)
                share = 1.0 / stat[8 + h : 9 + h, at]
                out[at, cols] = jnp.transpose(acc[cols, at] * share).astype(out.dtype)


def attend(plan, row, queries, blocks, state, last):
    columns, rows = queries.shape[0] // 2, queries.shape[1]
    acc = jax.ShapeDtypeStruct((columns, rows), jnp.float32)
    stat = jax.ShapeDtypeStruct((16, rows), jnp.float32)
    scratch, outs = [], [acc, stat]
    if last:
        scratch = [pltpu.VMEM(acc.shape, acc.dtype), pltpu.VMEM(stat.shape, stat.dtype)]
        outs = [jax.ShapeDtypeStruct((rows, columns), queries.dtype)]
    scratch += [
        pltpu.VMEM((STRETCH, columns), queries.dtype),
        pltpu.VMEM((columns // HD * (HD + ONES), STRETCH), queries.dtype),
        pltpu.VMEM((8, STRETCH), jnp.float32),
    ]
    operands = [plan] + ([] if row is None else [row])
    smem = len(operands)
    operands.append(queries)
    for b in blocks:
        operands += [b[0], b[1]]
    operands += list(state)
    keys = len(blocks) * STRETCH
    result = pl.pallas_call(
        functools.partial(attend_kernel, [tuple(b[2:]) for b in blocks], row is not None, last),
        out_shape=outs,
        in_specs=[SMEM] * smem + [VMEM] * (len(operands) - smem),
        out_specs=[VMEM] * len(outs),
        scratch_shapes=scratch,
        compiler_params=room(24),
        cost_estimate=pl.CostEstimate(
            flops=4 * rows * columns * keys, bytes_accessed=8 * rows * columns,
            transcendentals=rows * columns // HD * keys,
        ),
        name="attend",
    )(*operands)
    return result[0] if last else tuple(result)


def own_blocks(keys, values):
    return [(keys, values, j * STRETCH, (1 + j, 2)) for j in range(STRETCH_DEV)]


def came_blocks(base, key_came, value_came):
    return [(key_came[d], value_came[d], 0, (base + 2 + 2 * d, 1)) for d in range(2)]


def send(up, down):
    last = lax.axis_size("seq") - 1
    return (
        lax.ppermute(up, "seq", [(i, i + 1) for i in range(last)]),
        lax.ppermute(down, "seq", [(i + 1, i) for i in range(last)]),
    )


def exchange(rounds, plan, queries, keys, values, text_keys, text_values, key_first):
    key_here = send(*key_first)
    values, text_values, *value_first = turn_values(plan, values, text_values)
    queries = turn_queries(queries)
    value_first, queries = lax.optimization_barrier((value_first, queries))
    value_here = send(*value_first)
    state = attend_text(queries, text_keys, text_values)
    key_came, value_came = ([], []), ([], [])
    waiting = []

    def before(blocks):
        nonlocal state
        blocks, state = lax.optimization_barrier((blocks, state))
        return blocks

    for r in range(rounds - 1):
        key_here = before(key_here)
        for d in range(2):
            key_came[d].append(key_here[d])
        key_next = send(*before(choose(plan, r + 1, keys, 0, *key_came)))
        if r > 0:
            state = attend(plan, None, queries, [waiting.pop(0)], state, False)
        value_here = before(value_here)
        for d in range(2):
            value_came[d].append(value_here[d])
        waiting += came_blocks(HEADER + r * ROW, key_here, value_here)
        key_here, value_here = key_next, send(*before(choose(plan, r + 1, values, 1, *value_came)))
        if r + 2 < rounds:
            state = attend(plan, None, queries, [waiting.pop(0)], state, False)
    blocks = came_blocks(HEADER + (rounds - 1) * ROW, key_here, value_here)
    state = attend(plan, None, queries, own_blocks(keys, values) + waiting, state, False)
    return attend(plan, None, queries, blocks, state, True)


def long_exchange(plan, queries, keys, values, text_keys, text_values, key_first):
    values, text_values, *value_first = turn_values(plan, values, text_values)
    queries = turn_queries(queries)
    state = attend_text(queries, text_keys, text_values)
    state = attend(plan, None, queries, own_blocks(keys, values), state, False)

    def body(carry):
        r, key_here, value_here, state = carry
        row = r.reshape(1)
        key_here = send(*choose(plan, row, keys, 0, [key_here[0]], [key_here[1]]))
        value_here = send(*choose(plan, row, values, 1, [value_here[0]], [value_here[1]]))
        state = attend(plan, row, queries, came_blocks(0, key_here, value_here), state, False)
        return (r + 1, key_here, value_here, state)

    carry = (jnp.int32(0), tuple(key_first), tuple(value_first), state)
    _, _, _, (acc, stat) = lax.while_loop(lambda c: c[0] < plan[5], body, carry)
    heads = acc.shape[0] // HD
    share = jnp.repeat(1.0 / stat[8 : 8 + heads], HD, axis=0)
    return jnp.transpose(acc * share).astype(queries.dtype)


def shards(
    queries, key_rows, value_rows, text_keys, text_values,
    shot_of_stretch, anchor_stretch, context_count, context_ids,
):
    groups = lax.axis_size("seq")
    tables = (shot_of_stretch, anchor_stretch, context_count, context_ids.T)
    plan, branch, key_up, key_down = make_plan(groups, tables, key_rows)
    branches = [functools.partial(exchange, rounds) for rounds in ROUNDS] + [long_exchange]
    return lax.switch(
        branch[0], branches, plan, queries, key_rows, value_rows, text_keys, text_values,
        (key_up, key_down),
    )


def solution(mesh):
    return jax.shard_map(
        shards,
        mesh=mesh,
        in_specs=(
            P(("rep", "seq"), "shot"),
            P(("rep", "seq"), "shot"),
            P(("rep", "seq"), "shot"),
            P("rep", "shot"),
            P("rep", "shot"),
            P("rep"),
            P("rep"),
            P("rep"),
            P("rep", None),
        ),
        out_specs=P(("rep", "seq"), "shot"),
        check_vma=False,
    )
```

```python
import functools
import math

import jax
import jax.numpy as jnp
from jax import lax
from jax.experimental import pallas as pl
from jax.experimental.pallas import tpu as pltpu
from jax.sharding import PartitionSpec as P

HD = 128
STRETCH = 512
STRETCH_DEV = 2
ROUNDS = (3, 4)
ROW = 8
HEADER = 8
TURN = 256
GUARD = 2.0 ** 100
ONES = 16
EXPONENT = HD ** (-0.5) * math.log2(math.e)
SMEM = pl.BlockSpec(memory_space=pltpu.SMEM)
VMEM = pl.BlockSpec(memory_space=pltpu.VMEM)


def room(mebibytes):
    return pltpu.CompilerParams(vmem_limit_bytes=mebibytes * 1024 * 1024)


def quick_plan(groups, shot, anchor, count, ids, keys, plan, targets):
    total = STRETCH_DEV * groups
    slots = ids.shape[0]
    me = lax.axis_index("seq")
    one = jnp.int32(1)

    def listed(c):
        live = count[c]
        yield one << anchor[shot[c]]
        for s in range(slots):
            yield jnp.where(s < live, one << ids[s, c], 0)

    need = []
    for g in range(groups):
        mask = jnp.int32(0)
        for c in range(STRETCH_DEV * g, STRETCH_DEV * (g + 1)):
            for entry in listed(c):
                mask = mask | entry
        need.append(mask)

    once, twice = [], []
    for q in range(STRETCH_DEV):
        c = STRETCH_DEV * me + q
        seen, again = one << c, jnp.int32(0)
        for entry in listed(c):
            again = again | (seen & entry)
            seen = seen | entry
        once.append(seen)
        twice.append(again)

    def times(q, stretch):
        return jnp.where((once[q] & stretch) != 0, 1, 0) + jnp.where((twice[q] & stretch) != 0, 1, 0)

    first_own = one << (STRETCH_DEV * me)
    second_own = first_own << 1
    for q in range(STRETCH_DEV):
        plan[1 + 2 * q] = times(q, first_own)
        plan[2 + 2 * q] = times(q, second_own)

    ways = []
    for d in range(2):
        order = list(range(groups))[:: 1 - 2 * d]
        own = [((1 << STRETCH_DEV) - 1) << (STRETCH_DEV * g) for g in order]
        before = [sum(own[:k]) for k in range(groups)]
        beyond = _beyond(need, order, before)
        ways.append((own, beyond, [own[k] & beyond[k] for k in range(groups)]))

    rounds = jnp.int32(0)
    arrived = [[], []]
    for r in range(ROUNDS[-1]):
        pending = jnp.int32(0)
        for d in range(2):
            _, beyond, onward = ways[d]
            at = me if d == 0 else groups - 1 - me
            picks = []
            for k in range(groups - 1):
                pending = pending | onward[k]
                pick = onward[k] & beyond[groups - 2]
                for g in reversed(range(k, groups - 2)):
                    pick = jnp.where(pick != 0, pick, onward[k] & beyond[g])
                picks.append(pick & -pick)
            for k in range(groups - 1):
                onward[k] = onward[k] & ~picks[k]
            for k in range(1, groups - 1):
                onward[k] = onward[k] | (picks[k - 1] & beyond[k])
            sent, came = jnp.int32(0), jnp.int32(0)
            for k in range(groups - 1):
                sent = jnp.where(at == k, picks[k], sent)
                came = jnp.where(at == k + 1, picks[k], came)
            choice = jnp.where(sent == second_own, 1, 0)
            for i, earlier in enumerate(arrived[d]):
                choice = jnp.where((sent == earlier) & (sent != 0), STRETCH_DEV + i, choice)
            arrived[d].append(came)
            plan[HEADER + r * ROW + d] = choice
            for q in range(STRETCH_DEV):
                plan[HEADER + r * ROW + 2 + 2 * d + q] = times(q, came)
            if r == 0:
                start = pl.multiple_of(choice * STRETCH, STRETCH)
                targets[d][...] = keys[pl.ds(start, STRETCH), :]
        rounds = rounds + jnp.where(pending != 0, 1, 0)
    pending = jnp.int32(0)
    for _, _, onward in ways:
        for left in onward[: groups - 1]:
            pending = pending | left
    return rounds + jnp.where(pending != 0, 1, 0)


def _beyond(need, order, before):
    beyond = []
    for k in range(len(order)):
        mask = jnp.int32(0)
        held = before[k + 1] if k + 1 < len(order) else 0
        for g in order[k + 1 :]:
            mask = mask | need[g]
        beyond.append(mask & held)
    return beyond


def plan_kernel(
    groups, cap, shot, anchor, count, ids, keys,
    plan, branch, key_up, key_down, *scratch,
):
    def list_plan():
        return long_plan(groups, cap, shot, anchor, count, ids, plan, *scratch)

    if STRETCH_DEV * groups <= 16:
        rounds = quick_plan(groups, shot, anchor, count, ids, keys, plan, (key_up, key_down))
        plan[0] = rounds

        @pl.when(rounds > ROUNDS[-1])
        def _():
            list_plan()
    else:
        rounds = list_plan()
        for d, target in enumerate((key_up, key_down)):
            start = pl.multiple_of(plan[HEADER + d] * STRETCH, STRETCH)
            target[...] = keys[pl.ds(start, STRETCH), :]
    branch[0] = sum(jnp.where(rounds > length, 1, 0) for length in ROUNDS)


def long_plan(groups, cap, shot, anchor, count, ids, plan, dest, place, hold, stamp, times, best):
    total = STRETCH_DEV * groups
    slots = ids.shape[0]
    small = total <= 16
    bits = total.bit_length()
    me = lax.axis_index("seq")
    mine = (me, groups - 1 - me)

    def each(length, body):
        if small:
            for i in range(length):
                body(i)
        else:
            lax.fori_loop(0, length, lambda i, c: (body(i), c)[1], 0)

    def clear(e):
        g = e >> 1
        dest[e] = g
        dest[total + e] = groups - 1 - g
        times[e] = 0
        times[total + e] = 0

    each(total, clear)

    def stand(e):
        g = e >> 1
        for d, at in enumerate((g, groups - 1 - g)):
            place[d * total + e] = at
            hold[d * total + e] = e & 1
            stamp[d * total + e] = -1

    each(total, stand)

    def read(c):
        g = c >> 1

        def entry(e):
            dest[e] = jnp.maximum(dest[e], g)
            dest[total + e] = jnp.maximum(dest[total + e], groups - 1 - g)

        entry(anchor[shot[c]])
        live = count[c]
        for s in range(slots):
            entry(jnp.where(s < live, ids[s, c], c))

    each(total, read)

    for q in range(STRETCH_DEV):
        c = STRETCH_DEV * me + q

        def one(e, amount, q=q):
            times[q * total + e] = times[q * total + e] + amount

        one(c, 1)
        one(anchor[shot[c]], 1)
        live = count[c]
        for s in range(slots):
            alive = s < live
            one(jnp.where(alive, ids[s, c], c), jnp.where(alive, 1, 0))

    for q in range(STRETCH_DEV):
        for j in range(STRETCH_DEV):
            plan[1 + 2 * q + j] = times[q * total + STRETCH_DEV * me + j]
    for i in range(ROW * ROUNDS[-1]):
        plan[HEADER + i] = 0

    def remaining():
        return lax.fori_loop(
            0, 2 * total, lambda e, s: s + dest[e] - place[e], jnp.int32(0), unroll=small
        )

    def a_round(r, transit):
        moves = jnp.int32(0)
        for d in range(2):
            base = d * total
            for k in range(groups) if small else ():
                best[k] = -1
            if not small:
                each(groups, lambda k: best.__setitem__(k, jnp.int32(-1)))

            def rank(e, base=base):
                at = place[base + e]
                to = dest[base + e]
                key = (to << bits) | e
                if transit:
                    key = jnp.where(stamp[base + e] == r, key + (groups << bits), key)
                best[at] = jnp.maximum(best[at], jnp.where(to > at, key, -1))

            each(total, rank)
            sent = best[mine[d]]
            mask = (1 << bits) - 1
            plan[HEADER + r * ROW + d] = jnp.where(sent < 0, 0, hold[base + (jnp.maximum(sent, 0) & mask)])
            came = jnp.where(mine[d] > 0, best[jnp.maximum(mine[d] - 1, 0)], -1)
            come = jnp.maximum(came, 0) & mask
            for q in range(STRETCH_DEV):
                plan[HEADER + r * ROW + 2 + 2 * d + q] = jnp.where(came < 0, 0, times[q * total + come])

            @pl.when(came >= 0)
            def _(come=come, base=base):
                hold[base + come] = 2 + r

            def move(k, base=base):
                key = best[k]

                @pl.when(key >= 0)
                def _():
                    e = key & mask
                    place[base + e] = k + 1
                    stamp[base + e] = r + 1

                return jnp.where(key >= 0, 1, 0)

            if small:
                for k in range(groups - 1):
                    moves += move(k)
            else:
                moves += lax.fori_loop(0, groups - 1, lambda k, s: s + move(k), jnp.int32(0))
        return moves

    hops = remaining()

    def go_on(carry):
        return (carry[1] > 0) & (carry[0] < cap)

    rounds, _ = lax.while_loop(
        go_on, lambda c: (c[0] + 1, c[1] - a_round(c[0], False)), (jnp.int32(0), hops)
    )
    plan[0] = rounds

    @pl.when(rounds > ROUNDS[-1])
    def _():
        each(total, stand)
        again, _ = lax.while_loop(
            go_on, lambda c: (c[0] + 1, c[1] - a_round(c[0], True)), (jnp.int32(0), hops)
        )
        plan[5] = again

    return rounds


def make_plan(groups, tables, keys):
    total = STRETCH_DEV * groups
    cap = 2 * groups + 16
    block = jax.ShapeDtypeStruct((STRETCH, keys.shape[1]), keys.dtype)
    return pl.pallas_call(
        functools.partial(plan_kernel, groups, cap),
        out_shape=[
            jax.ShapeDtypeStruct((HEADER + cap * ROW,), jnp.int32),
            jax.ShapeDtypeStruct((1,), jnp.int32),
            block,
            block,
        ],
        in_specs=[SMEM] * 4 + [VMEM],
        out_specs=[SMEM] * 2 + [VMEM] * 2,
        scratch_shapes=[pltpu.SMEM((2 * total,), jnp.int32) for _ in range(5)]
        + [pltpu.SMEM((groups,), jnp.int32)],
        name="plan",
    )(*tables, keys)


def choose_kernel(row, arrivals, axis, plan, *refs):
    if row is None:
        at, own, *refs = refs
        base = HEADER + at[0] * ROW
    else:
        own, *refs = refs
        base = HEADER + row * ROW
    came, outs = refs[: 2 * arrivals], refs[2 * arrivals :]
    for d in range(2):
        choice = plan[base + d]

        @pl.when(choice < STRETCH_DEV)
        def _(d=d, choice=choice):
            part = pl.ds(pl.multiple_of(choice * STRETCH, STRETCH), STRETCH)
            outs[d][...] = own[part, :] if axis == 0 else own[:, part]

        for i in range(arrivals):
            picked = choice == STRETCH_DEV + i if row is not None else choice >= STRETCH_DEV

            @pl.when(picked)
            def _(d=d, i=i):
                outs[d][...] = came[d * arrivals + i][...]


def choose(plan, row, own, axis, up, down):
    static = isinstance(row, int)
    shape = list(own.shape)
    shape[axis] = STRETCH
    block = jax.ShapeDtypeStruct(tuple(shape), own.dtype)
    return pl.pallas_call(
        functools.partial(choose_kernel, row if static else None, len(up), axis),
        out_shape=[block] * 2,
        in_specs=[SMEM] + ([] if static else [SMEM]) + [VMEM] * (1 + 2 * len(up)),
        out_specs=[VMEM] * 2,
        compiler_params=room(8),
        cost_estimate=pl.CostEstimate(flops=0, bytes_accessed=8 * block.size, transcendentals=0),
        name="choose",
    )(plan, *(() if static else (row,)), own, *up, *down)


def score(keys, queries):
    return jnp.dot(jnp.concatenate([keys, keys], axis=1), queries, preferred_element_type=jnp.float32)


def turn_queries_kernel(queries, split):
    for h in range(queries.shape[1] // HD):
        cols = pl.ds(h * HD, HD)
        for t in range(queries.shape[0] // TURN):
            at = pl.ds(t * TURN, TURN)
            turned = jnp.transpose(queries[at, cols].astype(jnp.float32) * EXPONENT)
            high = turned.astype(jnp.bfloat16)
            split[pl.ds(2 * h * HD, HD), at] = high
            split[pl.ds((2 * h + 1) * HD, HD), at] = (turned - high.astype(jnp.float32)).astype(jnp.bfloat16)


def turn_queries(queries):
    rows, columns = queries.shape
    return pl.pallas_call(
        turn_queries_kernel,
        out_shape=jax.ShapeDtypeStruct((2 * columns, rows), queries.dtype),
        in_specs=[VMEM],
        out_specs=VMEM,
        compiler_params=room(10),
        name="turn_queries",
    )(queries)


def text_kernel(queries, text_keys, text_values, acc, stat):
    ones = jnp.ones((ONES, text_keys.shape[0]), jnp.bfloat16)

    def stretch(t, c):
        at = pl.ds(pl.multiple_of(t * STRETCH, STRETCH), STRETCH)
        for h in range(text_keys.shape[1] // HD):
            cols = pl.ds(h * HD, HD)
            scores = score(text_keys[:, cols], queries[pl.ds(2 * h * HD, 2 * HD), at])
            peak = jnp.max(scores, axis=0, keepdims=True)
            both = jnp.dot(
                jnp.concatenate([text_values[cols, :], ones], axis=0),
                jnp.exp2(scores - peak).astype(jnp.bfloat16), preferred_element_type=jnp.float32,
            )
            acc[cols, at] = both[:HD]
            stat[16 * h : 16 * h + 1, at] = peak
            stat[16 * h + 8 : 16 * h + 9, at] = both[HD : HD + 1]
        return c

    lax.fori_loop(0, queries.shape[1] // STRETCH, stretch, 0)


def attend_text(queries, text_keys, text_values):
    columns, rows = queries.shape[0] // 2, queries.shape[1]
    return pl.pallas_call(
        text_kernel,
        out_shape=[
            jax.ShapeDtypeStruct((columns, rows), jnp.float32),
            jax.ShapeDtypeStruct((16 * (columns // HD), rows), jnp.float32),
        ],
        in_specs=[VMEM] * 3,
        out_specs=[VMEM] * 2,
        compiler_params=room(16),
        name="attend_text",
    )(queries, text_keys, text_values)


def turn_values_kernel(plan, values, text_values, values_out, text_out, up, down):
    for h in range(values.shape[1] // HD):
        cols = pl.ds(h * HD, HD)
        for source, target in ((values, values_out), (text_values, text_out)):
            for t in range(source.shape[0] // TURN):
                at = pl.ds(t * TURN, TURN)
                target[cols, at] = jnp.transpose(source[at, cols])
    for d, target in enumerate((up, down)):
        start = pl.multiple_of(plan[HEADER + d] * STRETCH, STRETCH)
        target[...] = values_out[:, pl.ds(start, STRETCH)]


def turn_values(plan, values, text_values):
    rows, columns = values.shape
    outs = [(columns, rows), (columns, text_values.shape[0]), (columns, STRETCH), (columns, STRETCH)]
    return pl.pallas_call(
        turn_values_kernel,
        out_shape=[jax.ShapeDtypeStruct(shape, values.dtype) for shape in outs],
        in_specs=[SMEM, VMEM, VMEM],
        out_specs=[VMEM] * 4,
        compiler_params=room(10),
        name="turn_values",
    )(plan, values, text_values)


def attend_kernel(blocks, rowed, last, *refs):
    refs = list(refs)
    plan = refs.pop(0)
    base = HEADER + refs.pop(0)[0] * ROW if rowed else 0
    queries = refs.pop(0)
    block_refs = [(refs.pop(0), refs.pop(0)) for _ in blocks]
    acc_in, stat_in, *refs = refs
    *refs, keys_at, values_at, fine = refs
    if last:
        out, acc, stat = refs
    else:
        acc, stat = refs
    rows = queries.shape[1]
    heads = queries.shape[0] // (2 * HD)
    wide = HD + ONES

    acc[...] = acc_in[...]
    stat[...] = stat_in[...]
    for h in range(heads):
        values_at[pl.ds(h * wide + HD, ONES), :] = jnp.ones((ONES, STRETCH), jnp.bfloat16)

    def head(h):
        cols = pl.ds(pl.multiple_of(h * HD, HD), HD)
        both = pl.ds(pl.multiple_of(2 * h * HD, 2 * HD), 2 * HD)
        mixed = pl.ds(pl.multiple_of(h * wide, ONES), wide)
        return cols, both, mixed, pl.ds(pl.multiple_of(16 * h, 8), 1), pl.ds(pl.multiple_of(16 * h + 8, 8), 1)

    def step(start, twice):
        at = pl.ds(pl.multiple_of(start, STRETCH), STRETCH)

        def one(h, lowest):
            cols, both, mixed, refer, total = head(h)
            scores = score(keys_at[:, cols], queries[both, at])
            weights = jnp.exp2(scores - (stat[refer, at] - twice)).astype(jnp.bfloat16)
            product = jnp.dot(values_at[mixed, :], weights, preferred_element_type=jnp.float32)
            mass = product[HD : HD + 1]
            fits = mass < GUARD
            acc[cols, at] = jnp.where(fits, acc[cols, at] + product[:HD], acc[cols, at])
            stat[total, at] += jnp.where(fits, mass, 0.0)
            fit = jnp.where(fits, 1.0, 0.0)
            fine[pl.ds(pl.multiple_of(8 * h, 8), 1), :] = fit
            return jnp.minimum(lowest, fit)

        lowest = lax.fori_loop(0, heads, one, jnp.ones((1, STRETCH), jnp.float32))

        @pl.when(jnp.min(lowest) < 0.5)
        def _():
            parts = STRETCH // HD
            lax.fori_loop(
                0, heads * parts, lambda i, c: (again(start, i // parts, i % parts * HD, twice), c)[1], 0
            )

    def again(start, h, w, twice):
        at = pl.ds(pl.multiple_of(start + w, HD), HD)
        cols, both, mixed, refer, total = head(h)
        scores = score(keys_at[:, cols], queries[both, at])
        before = stat[refer, at]
        peak = jnp.maximum(jnp.max(scores, axis=0, keepdims=True), before)
        keep = jnp.exp2(before - peak)
        weights = jnp.exp2(scores - (peak - twice)).astype(jnp.bfloat16)
        product = jnp.dot(values_at[mixed, :], weights, preferred_element_type=jnp.float32)
        miss = fine[pl.ds(pl.multiple_of(8 * h, 8), 1), pl.ds(pl.multiple_of(w, HD), HD)] < 0.5
        mass = product[HD : HD + 1] + stat[total, at] * keep
        acc[cols, at] = jnp.where(miss, product[:HD] + acc[cols, at] * keep, acc[cols, at])
        stat[total, at] = jnp.where(miss, mass, stat[total, at])
        stat[refer, at] = jnp.where(miss, peak, before)

    def visit(b, c):
        place, stride = jnp.int32(0), jnp.int32(0)
        for number, (_, (first, second)) in enumerate(blocks):
            place = jnp.where(b == number, first, place)
            stride = jnp.where(b == number, second, stride)
        place = base + place

        @pl.when(plan[place] + plan[place + stride] > 0)
        def _():
            for number, (start, _) in enumerate(blocks):
                @pl.when(b == number)
                def _(start=start, number=number):
                    part = pl.ds(start, STRETCH)
                    keys_at[...] = block_refs[number][0][part, :]
                    for h in range(heads):
                        values_at[pl.ds(h * wide, HD), :] = block_refs[number][1][pl.ds(h * HD, HD), part]

            def stretch(t, c):
                times = plan[place + t * stride]

                @pl.when(times > 0)
                def _():
                    step(t * STRETCH, jnp.where(times > 1, 1.0, 0.0))

                return c

            lax.fori_loop(0, rows // STRETCH, stretch, 0)

        return c

    lax.fori_loop(0, len(blocks), visit, 0)

    if last:
        for h in range(heads):
            cols = pl.ds(h * HD, HD)
            for t in range(rows // TURN):
                at = pl.ds(t * TURN, TURN)
                share = 1.0 / stat[16 * h + 8 : 16 * h + 9, at]
                out[at, cols] = jnp.transpose((acc[cols, at] * share).astype(out.dtype))


def attend(plan, row, queries, blocks, state, last):
    columns, rows = queries.shape[0] // 2, queries.shape[1]
    acc = jax.ShapeDtypeStruct((columns, rows), jnp.float32)
    stat = jax.ShapeDtypeStruct((16 * (columns // HD), rows), jnp.float32)
    scratch, outs = [], [acc, stat]
    if last:
        scratch = [pltpu.VMEM(acc.shape, acc.dtype), pltpu.VMEM(stat.shape, stat.dtype)]
        outs = [jax.ShapeDtypeStruct((rows, columns), queries.dtype)]
    scratch += [
        pltpu.VMEM((STRETCH, columns), queries.dtype),
        pltpu.VMEM((columns // HD * (HD + ONES), STRETCH), queries.dtype),
        pltpu.VMEM((8 * (columns // HD), STRETCH), jnp.float32),
    ]
    operands = [plan] + ([] if row is None else [row])
    smem = len(operands)
    operands.append(queries)
    for b in blocks:
        operands += [b[0], b[1]]
    operands += list(state)
    keys = len(blocks) * STRETCH
    result = pl.pallas_call(
        functools.partial(attend_kernel, [tuple(b[2:]) for b in blocks], row is not None, last),
        out_shape=outs,
        in_specs=[SMEM] * smem + [VMEM] * (len(operands) - smem),
        out_specs=[VMEM] * len(outs),
        scratch_shapes=scratch,
        compiler_params=room(24),
        cost_estimate=pl.CostEstimate(
            flops=4 * rows * columns * keys, bytes_accessed=8 * rows * columns,
            transcendentals=rows * columns // HD * keys,
        ),
        name="attend",
    )(*operands)
    return result[0] if last else tuple(result)


def own_blocks(keys, values):
    return [(keys, values, j * STRETCH, (1 + j, 2)) for j in range(STRETCH_DEV)]


def came_blocks(base, key_came, value_came):
    return [(key_came[d], value_came[d], 0, (base + 2 + 2 * d, 1)) for d in range(2)]


def send(up, down):
    last = lax.axis_size("seq") - 1
    return (
        lax.ppermute(up, "seq", [(i, i + 1) for i in range(last)]),
        lax.ppermute(down, "seq", [(i + 1, i) for i in range(last)]),
    )


def exchange(rounds, plan, queries, keys, values, text_keys, text_values, key_first):
    key_here = send(*key_first)
    values, text_values, *value_first = turn_values(plan, values, text_values)
    queries = turn_queries(queries)
    value_first, queries = lax.optimization_barrier((value_first, queries))
    value_here = send(*value_first)
    state = attend_text(queries, text_keys, text_values)
    key_came, value_came = ([], []), ([], [])
    waiting = []

    def before(blocks):
        nonlocal state
        blocks, state = lax.optimization_barrier((blocks, state))
        return blocks

    for r in range(rounds - 1):
        key_here = before(key_here)
        for d in range(2):
            key_came[d].append(key_here[d])
        key_next = send(*before(choose(plan, r + 1, keys, 0, *key_came)))
        if r > 0:
            state = attend(plan, None, queries, [waiting.pop(0)], state, False)
        value_here = before(value_here)
        for d in range(2):
            value_came[d].append(value_here[d])
        waiting += came_blocks(HEADER + r * ROW, key_here, value_here)
        key_here, value_here = key_next, send(*before(choose(plan, r + 1, values, 1, *value_came)))
        if r + 2 < rounds:
            state = attend(plan, None, queries, [waiting.pop(0)], state, False)
    blocks = came_blocks(HEADER + (rounds - 1) * ROW, key_here, value_here)
    state = attend(plan, None, queries, own_blocks(keys, values) + waiting, state, False)
    return attend(plan, None, queries, blocks, state, True)


def long_exchange(plan, queries, keys, values, text_keys, text_values, key_first):
    values, text_values, *value_first = turn_values(plan, values, text_values)
    queries = turn_queries(queries)
    state = attend_text(queries, text_keys, text_values)
    state = attend(plan, None, queries, own_blocks(keys, values), state, False)

    def body(carry):
        r, key_here, value_here, state = carry
        row = r.reshape(1)
        key_here = send(*choose(plan, row, keys, 0, [key_here[0]], [key_here[1]]))
        value_here = send(*choose(plan, row, values, 1, [value_here[0]], [value_here[1]]))
        state = attend(plan, row, queries, came_blocks(0, key_here, value_here), state, False)
        return (r + 1, key_here, value_here, state)

    carry = (jnp.int32(0), tuple(key_first), tuple(value_first), state)
    _, _, _, (acc, stat) = lax.while_loop(lambda c: c[0] < plan[5], body, carry)
    share = jnp.repeat(1.0 / stat[8::16], HD, axis=0)
    return jnp.transpose(acc * share).astype(queries.dtype)


def shards(
    queries, key_rows, value_rows, text_keys, text_values,
    shot_of_stretch, anchor_stretch, context_count, context_ids,
):
    groups = lax.axis_size("seq")
    tables = (shot_of_stretch, anchor_stretch, context_count, context_ids.T)
    plan, branch, key_up, key_down = make_plan(groups, tables, key_rows)
    branches = [functools.partial(exchange, rounds) for rounds in ROUNDS] + [long_exchange]
    return lax.switch(
        branch[0], branches, plan, queries, key_rows, value_rows, text_keys, text_values,
        (key_up, key_down),
    )


def solution(mesh):
    return jax.shard_map(
        shards,
        mesh=mesh,
        in_specs=(
            P(("rep", "seq"), "shot"),
            P(("rep", "seq"), "shot"),
            P(("rep", "seq"), "shot"),
            P("rep", "shot"),
            P("rep", "shot"),
            P("rep"),
            P("rep"),
            P("rep"),
            P("rep", None),
        ),
        out_specs=P(("rep", "seq"), "shot"),
        check_vma=False,
    )
```

```python
import functools
import math

import jax
import jax.numpy as jnp
from jax import lax
from jax.experimental import pallas as pl
from jax.experimental.pallas import tpu as pltpu
from jax.sharding import PartitionSpec as P

HD = 128
STRETCH = 512
STRETCH_DEV = 2
ROUNDS = (3, 4)
ROW = 8
HEADER = 8
TURN = 256
GUARD = 2.0 ** 100
ONES = 16
EXPONENT = HD ** (-0.5) * math.log2(math.e)
SMEM = pl.BlockSpec(memory_space=pltpu.SMEM)
VMEM = pl.BlockSpec(memory_space=pltpu.VMEM)


def room(mebibytes):
    return pltpu.CompilerParams(vmem_limit_bytes=mebibytes * 1024 * 1024)


def quick_plan(groups, shot, anchor, count, ids, keys, plan, targets):
    total = STRETCH_DEV * groups
    slots = ids.shape[0]
    me = lax.axis_index("seq")
    one = jnp.int32(1)

    def listed(c):
        live = count[c]
        yield one << anchor[shot[c]]
        for s in range(slots):
            yield jnp.where(s < live, one << ids[s, c], 0)

    need = []
    for g in range(groups):
        mask = jnp.int32(0)
        for c in range(STRETCH_DEV * g, STRETCH_DEV * (g + 1)):
            for entry in listed(c):
                mask = mask | entry
        need.append(mask)

    once, twice = [], []
    for q in range(STRETCH_DEV):
        c = STRETCH_DEV * me + q
        seen, again = one << c, jnp.int32(0)
        for entry in listed(c):
            again = again | (seen & entry)
            seen = seen | entry
        once.append(seen)
        twice.append(again)

    def times(q, stretch):
        return jnp.where((once[q] & stretch) != 0, 1, 0) + jnp.where((twice[q] & stretch) != 0, 1, 0)

    first_own = one << (STRETCH_DEV * me)
    second_own = first_own << 1
    for q in range(STRETCH_DEV):
        plan[1 + 2 * q] = times(q, first_own)
        plan[2 + 2 * q] = times(q, second_own)

    ways = []
    for d in range(2):
        order = list(range(groups))[:: 2 * d - 1]
        own = [((1 << STRETCH_DEV) - 1) << (STRETCH_DEV * g) for g in order]
        before = [sum(own[:k]) for k in range(groups)]
        beyond = _beyond(need, order, before)
        ways.append((own, beyond, [own[k] & beyond[k] for k in range(groups)]))

    rounds = jnp.int32(0)
    arrived = [[], []]
    for r in range(ROUNDS[-1]):
        pending = jnp.int32(0)
        for d in range(2):
            _, beyond, onward = ways[d]
            at = groups - 1 - me if d == 0 else me
            picks = []
            for k in range(groups - 1):
                pending = pending | onward[k]
                pick = onward[k] & beyond[groups - 2]
                for g in reversed(range(k, groups - 2)):
                    pick = jnp.where(pick != 0, pick, onward[k] & beyond[g])
                picks.append(pick & -pick)
            for k in range(groups - 1):
                onward[k] = onward[k] & ~picks[k]
            for k in range(1, groups - 1):
                onward[k] = onward[k] | (picks[k - 1] & beyond[k])
            sent, came = jnp.int32(0), jnp.int32(0)
            for k in range(groups - 1):
                sent = jnp.where(at == k, picks[k], sent)
                came = jnp.where(at == k + 1, picks[k], came)
            choice = jnp.where(sent == second_own, 1, 0)
            for i, earlier in enumerate(arrived[d]):
                choice = jnp.where((sent == earlier) & (sent != 0), STRETCH_DEV + i, choice)
            arrived[d].append(came)
            plan[HEADER + r * ROW + d] = choice
            for q in range(STRETCH_DEV):
                plan[HEADER + r * ROW + 2 + 2 * d + q] = times(q, came)
            if r == 0:
                start = pl.multiple_of(choice * STRETCH, STRETCH)
                targets[d][...] = keys[pl.ds(start, STRETCH), :]
        rounds = rounds + jnp.where(pending != 0, 1, 0)
    pending = jnp.int32(0)
    for _, _, onward in ways:
        for left in onward[: groups - 1]:
            pending = pending | left
    return rounds + jnp.where(pending != 0, 1, 0)


def _beyond(need, order, before):
    beyond = []
    for k in range(len(order)):
        mask = jnp.int32(0)
        held = before[k + 1] if k + 1 < len(order) else 0
        for g in order[k + 1 :]:
            mask = mask | need[g]
        beyond.append(mask & held)
    return beyond


def plan_kernel(
    groups, cap, shot, anchor, count, ids, keys,
    plan, branch, key_down, key_up, *scratch,
):
    def list_plan():
        return long_plan(groups, cap, shot, anchor, count, ids, plan, *scratch)

    if STRETCH_DEV * groups <= 16:
        rounds = quick_plan(groups, shot, anchor, count, ids, keys, plan, (key_down, key_up))
        plan[0] = rounds

        @pl.when(rounds > ROUNDS[-1])
        def _():
            list_plan()
    else:
        rounds = list_plan()
        for d, target in enumerate((key_down, key_up)):
            start = pl.multiple_of(plan[HEADER + d] * STRETCH, STRETCH)
            target[...] = keys[pl.ds(start, STRETCH), :]
    branch[0] = sum(jnp.where(rounds > length, 1, 0) for length in ROUNDS)


def long_plan(groups, cap, shot, anchor, count, ids, plan, dest, place, hold, stamp, times, best):
    total = STRETCH_DEV * groups
    slots = ids.shape[0]
    small = total <= 16
    bits = total.bit_length()
    me = lax.axis_index("seq")
    mine = (groups - 1 - me, me)

    def each(length, body):
        if small:
            for i in range(length):
                body(i)
        else:
            lax.fori_loop(0, length, lambda i, c: (body(i), c)[1], 0)

    def clear(e):
        g = e >> 1
        dest[e] = groups - 1 - g
        dest[total + e] = g
        times[e] = 0
        times[total + e] = 0

    each(total, clear)

    def stand(e):
        g = e >> 1
        for d, at in enumerate((groups - 1 - g, g)):
            place[d * total + e] = at
            hold[d * total + e] = e & 1
            stamp[d * total + e] = -1

    each(total, stand)

    def read(c):
        g = c >> 1

        def entry(e):
            dest[e] = jnp.maximum(dest[e], groups - 1 - g)
            dest[total + e] = jnp.maximum(dest[total + e], g)

        entry(anchor[shot[c]])
        live = count[c]
        for s in range(slots):
            entry(jnp.where(s < live, ids[s, c], c))

    each(total, read)

    for q in range(STRETCH_DEV):
        c = STRETCH_DEV * me + q

        def one(e, amount, q=q):
            times[q * total + e] = times[q * total + e] + amount

        one(c, 1)
        one(anchor[shot[c]], 1)
        live = count[c]
        for s in range(slots):
            alive = s < live
            one(jnp.where(alive, ids[s, c], c), jnp.where(alive, 1, 0))

    for q in range(STRETCH_DEV):
        for j in range(STRETCH_DEV):
            plan[1 + 2 * q + j] = times[q * total + STRETCH_DEV * me + j]
    for i in range(ROW * ROUNDS[-1]):
        plan[HEADER + i] = 0

    def remaining():
        return lax.fori_loop(
            0, 2 * total, lambda e, s: s + dest[e] - place[e], jnp.int32(0), unroll=small
        )

    def a_round(r, transit):
        moves = jnp.int32(0)
        for d in range(2):
            base = d * total
            for k in range(groups) if small else ():
                best[k] = -1
            if not small:
                each(groups, lambda k: best.__setitem__(k, jnp.int32(-1)))

            def rank(e, base=base):
                at = place[base + e]
                to = dest[base + e]
                key = (to << bits) | e
                if transit:
                    key = jnp.where(stamp[base + e] == r, key + (groups << bits), key)
                best[at] = jnp.maximum(best[at], jnp.where(to > at, key, -1))

            each(total, rank)
            sent = best[mine[d]]
            mask = (1 << bits) - 1
            plan[HEADER + r * ROW + d] = jnp.where(sent < 0, 0, hold[base + (jnp.maximum(sent, 0) & mask)])
            came = jnp.where(mine[d] > 0, best[jnp.maximum(mine[d] - 1, 0)], -1)
            come = jnp.maximum(came, 0) & mask
            for q in range(STRETCH_DEV):
                plan[HEADER + r * ROW + 2 + 2 * d + q] = jnp.where(came < 0, 0, times[q * total + come])

            @pl.when(came >= 0)
            def _(come=come, base=base):
                hold[base + come] = 2 + r

            def move(k, base=base):
                key = best[k]

                @pl.when(key >= 0)
                def _():
                    e = key & mask
                    place[base + e] = k + 1
                    stamp[base + e] = r + 1

                return jnp.where(key >= 0, 1, 0)

            if small:
                for k in range(groups - 1):
                    moves += move(k)
            else:
                moves += lax.fori_loop(0, groups - 1, lambda k, s: s + move(k), jnp.int32(0))
        return moves

    hops = remaining()

    def go_on(carry):
        return (carry[1] > 0) & (carry[0] < cap)

    rounds, _ = lax.while_loop(
        go_on, lambda c: (c[0] + 1, c[1] - a_round(c[0], False)), (jnp.int32(0), hops)
    )
    plan[0] = rounds

    @pl.when(rounds > ROUNDS[-1])
    def _():
        each(total, stand)
        again, _ = lax.while_loop(
            go_on, lambda c: (c[0] + 1, c[1] - a_round(c[0], True)), (jnp.int32(0), hops)
        )
        plan[5] = again

    return rounds


def make_plan(groups, tables, keys):
    total = STRETCH_DEV * groups
    cap = 2 * groups + 16
    block = jax.ShapeDtypeStruct((STRETCH, keys.shape[1]), keys.dtype)
    return pl.pallas_call(
        functools.partial(plan_kernel, groups, cap),
        out_shape=[
            jax.ShapeDtypeStruct((HEADER + cap * ROW,), jnp.int32),
            jax.ShapeDtypeStruct((1,), jnp.int32),
            block,
            block,
        ],
        in_specs=[SMEM] * 4 + [VMEM],
        out_specs=[SMEM] * 2 + [VMEM] * 2,
        scratch_shapes=[pltpu.SMEM((2 * total,), jnp.int32) for _ in range(5)]
        + [pltpu.SMEM((groups,), jnp.int32)],
        name="plan",
    )(*tables, keys)


def choose_kernel(row, arrivals, axis, plan, *refs):
    if row is None:
        at, own, *refs = refs
        base = HEADER + at[0] * ROW
    else:
        own, *refs = refs
        base = HEADER + row * ROW
    came, outs = refs[: 2 * arrivals], refs[2 * arrivals :]
    for d in range(2):
        choice = plan[base + d]

        @pl.when(choice < STRETCH_DEV)
        def _(d=d, choice=choice):
            part = pl.ds(pl.multiple_of(choice * STRETCH, STRETCH), STRETCH)
            outs[d][...] = own[part, :] if axis == 0 else own[:, part]

        for i in range(arrivals):
            picked = choice == STRETCH_DEV + i if row is not None else choice >= STRETCH_DEV

            @pl.when(picked)
            def _(d=d, i=i):
                outs[d][...] = came[d * arrivals + i][...]


def choose(plan, row, own, axis, down, up):
    static = isinstance(row, int)
    shape = list(own.shape)
    shape[axis] = STRETCH
    block = jax.ShapeDtypeStruct(tuple(shape), own.dtype)
    return pl.pallas_call(
        functools.partial(choose_kernel, row if static else None, len(down), axis),
        out_shape=[block] * 2,
        in_specs=[SMEM] + ([] if static else [SMEM]) + [VMEM] * (1 + 2 * len(down)),
        out_specs=[VMEM] * 2,
        compiler_params=room(8),
        cost_estimate=pl.CostEstimate(flops=0, bytes_accessed=8 * block.size, transcendentals=0),
        name="choose",
    )(plan, *(() if static else (row,)), own, *down, *up)


def score(keys, queries):
    return jnp.dot(jnp.concatenate([keys, keys], axis=1), queries, preferred_element_type=jnp.float32)


def turn_queries_kernel(queries, split):
    for h in range(queries.shape[1] // HD):
        cols = pl.ds(h * HD, HD)
        for t in range(queries.shape[0] // TURN):
            at = pl.ds(t * TURN, TURN)
            turned = jnp.transpose(queries[at, cols].astype(jnp.float32) * EXPONENT)
            high = turned.astype(jnp.bfloat16)
            split[pl.ds(2 * h * HD, HD), at] = high
            split[pl.ds((2 * h + 1) * HD, HD), at] = (turned - high.astype(jnp.float32)).astype(jnp.bfloat16)


def turn_queries(queries):
    rows, columns = queries.shape
    return pl.pallas_call(
        turn_queries_kernel,
        out_shape=jax.ShapeDtypeStruct((2 * columns, rows), queries.dtype),
        in_specs=[VMEM],
        out_specs=VMEM,
        compiler_params=room(10),
        name="turn_queries",
    )(queries)


def text_kernel(queries, text_keys, text_values, acc, stat):
    ones = jnp.ones((ONES, text_keys.shape[0]), jnp.bfloat16)

    def stretch(t, c):
        at = pl.ds(pl.multiple_of(t * STRETCH, STRETCH), STRETCH)
        for h in range(text_keys.shape[1] // HD):
            cols = pl.ds(h * HD, HD)
            scores = score(text_keys[:, cols], queries[pl.ds(2 * h * HD, 2 * HD), at])
            peak = jnp.max(scores, axis=0, keepdims=True)
            both = jnp.dot(
                jnp.concatenate([text_values[cols, :], ones], axis=0),
                jnp.exp2(scores - peak).astype(jnp.bfloat16), preferred_element_type=jnp.float32,
            )
            acc[cols, at] = both[:HD]
            stat[16 * h : 16 * h + 1, at] = peak
            stat[16 * h + 8 : 16 * h + 9, at] = both[HD : HD + 1]
        return c

    lax.fori_loop(0, queries.shape[1] // STRETCH, stretch, 0)


def attend_text(queries, text_keys, text_values):
    columns, rows = queries.shape[0] // 2, queries.shape[1]
    return pl.pallas_call(
        text_kernel,
        out_shape=[
            jax.ShapeDtypeStruct((columns, rows), jnp.float32),
            jax.ShapeDtypeStruct((16 * (columns // HD), rows), jnp.float32),
        ],
        in_specs=[VMEM] * 3,
        out_specs=[VMEM] * 2,
        compiler_params=room(16),
        name="attend_text",
    )(queries, text_keys, text_values)


def turn_values_kernel(plan, values, text_values, values_out, text_out, down, up):
    for h in range(values.shape[1] // HD):
        cols = pl.ds(h * HD, HD)
        for source, target in ((values, values_out), (text_values, text_out)):
            for t in range(source.shape[0] // TURN):
                at = pl.ds(t * TURN, TURN)
                target[cols, at] = jnp.transpose(source[at, cols])
    for d, target in enumerate((down, up)):
        start = pl.multiple_of(plan[HEADER + d] * STRETCH, STRETCH)
        target[...] = values_out[:, pl.ds(start, STRETCH)]


def turn_values(plan, values, text_values):
    rows, columns = values.shape
    outs = [(columns, rows), (columns, text_values.shape[0]), (columns, STRETCH), (columns, STRETCH)]
    return pl.pallas_call(
        turn_values_kernel,
        out_shape=[jax.ShapeDtypeStruct(shape, values.dtype) for shape in outs],
        in_specs=[SMEM, VMEM, VMEM],
        out_specs=[VMEM] * 4,
        compiler_params=room(10),
        name="turn_values",
    )(plan, values, text_values)


def attend_kernel(blocks, rowed, last, *refs):
    refs = list(refs)
    plan = refs.pop(0)
    base = HEADER + refs.pop(0)[0] * ROW if rowed else 0
    queries = refs.pop(0)
    block_refs = [(refs.pop(0), refs.pop(0)) for _ in blocks]
    acc_in, stat_in, *refs = refs
    *refs, keys_at, values_at, fine = refs
    if last:
        out, acc, stat = refs
    else:
        acc, stat = refs
    rows = queries.shape[1]
    heads = queries.shape[0] // (2 * HD)
    wide = HD + ONES

    acc[...] = acc_in[...]
    stat[...] = stat_in[...]
    for h in range(heads):
        values_at[pl.ds(h * wide + HD, ONES), :] = jnp.ones((ONES, STRETCH), jnp.bfloat16)

    def head(h):
        def part(start, size, by):
            return pl.ds(start if isinstance(h, int) else pl.multiple_of(start, by), size)

        return (
            part(h * HD, HD, HD), part(2 * h * HD, 2 * HD, 2 * HD), part(h * wide, wide, ONES),
            part(16 * h, 1, 8), part(16 * h + 8, 1, 8),
        )

    def step(start, twice):
        at = pl.ds(pl.multiple_of(start, STRETCH), STRETCH)

        lowest = jnp.ones((1, STRETCH), jnp.float32)
        scores = score(keys_at[:, head(0)[0]], queries[head(0)[1], at])
        for h in range(heads):
            cols, _, mixed, refer, total = head(h)
            if h + 1 < heads:
                following = score(keys_at[:, head(h + 1)[0]], queries[head(h + 1)[1], at])
            weights = jnp.exp2(scores - (stat[refer, at] - twice)).astype(jnp.bfloat16)
            product = jnp.dot(values_at[mixed, :], weights, preferred_element_type=jnp.float32)
            mass = product[HD : HD + 1]
            fits = mass < GUARD
            acc[cols, at] = jnp.where(fits, acc[cols, at] + product[:HD], acc[cols, at])
            stat[total, at] += jnp.where(fits, mass, 0.0)
            fit = jnp.where(fits, 1.0, 0.0)
            fine[pl.ds(8 * h, 1), :] = fit
            lowest = jnp.minimum(lowest, fit)
            scores = following

        @pl.when(jnp.min(lowest) < 0.5)
        def _():
            parts = STRETCH // HD
            lax.fori_loop(
                0, heads * parts, lambda i, c: (again(start, i // parts, i % parts * HD, twice), c)[1], 0
            )

    def again(start, h, w, twice):
        at = pl.ds(pl.multiple_of(start + w, HD), HD)
        cols, both, mixed, refer, total = head(h)
        scores = score(keys_at[:, cols], queries[both, at])
        before = stat[refer, at]
        peak = jnp.maximum(jnp.max(scores, axis=0, keepdims=True), before)
        keep = jnp.exp2(before - peak)
        weights = jnp.exp2(scores - (peak - twice)).astype(jnp.bfloat16)
        product = jnp.dot(values_at[mixed, :], weights, preferred_element_type=jnp.float32)
        miss = fine[pl.ds(pl.multiple_of(8 * h, 8), 1), pl.ds(pl.multiple_of(w, HD), HD)] < 0.5
        mass = product[HD : HD + 1] + stat[total, at] * keep
        acc[cols, at] = jnp.where(miss, product[:HD] + acc[cols, at] * keep, acc[cols, at])
        stat[total, at] = jnp.where(miss, mass, stat[total, at])
        stat[refer, at] = jnp.where(miss, peak, before)

    def visit(b, c):
        place, stride = jnp.int32(0), jnp.int32(0)
        for number, (_, (first, second)) in enumerate(blocks):
            place = jnp.where(b == number, first, place)
            stride = jnp.where(b == number, second, stride)
        place = base + place

        @pl.when(plan[place] + plan[place + stride] > 0)
        def _():
            for number, (start, _) in enumerate(blocks):
                @pl.when(b == number)
                def _(start=start, number=number):
                    part = pl.ds(start, STRETCH)
                    keys_at[...] = block_refs[number][0][part, :]
                    for h in range(heads):
                        values_at[pl.ds(h * wide, HD), :] = block_refs[number][1][pl.ds(h * HD, HD), part]

            def stretch(t, c):
                times = plan[place + t * stride]

                @pl.when(times > 0)
                def _():
                    step(t * STRETCH, jnp.where(times > 1, 1.0, 0.0))

                return c

            lax.fori_loop(0, rows // STRETCH, stretch, 0)

        return c

    lax.fori_loop(0, len(blocks), visit, 0)

    if last:
        for h in range(heads):
            cols = pl.ds(h * HD, HD)
            for t in range(rows // TURN):
                at = pl.ds(t * TURN, TURN)
                share = 1.0 / stat[16 * h + 8 : 16 * h + 9, at]
                out[at, cols] = jnp.transpose((acc[cols, at] * share).astype(out.dtype))


def attend(plan, row, queries, blocks, state, last):
    columns, rows = queries.shape[0] // 2, queries.shape[1]
    acc = jax.ShapeDtypeStruct((columns, rows), jnp.float32)
    stat = jax.ShapeDtypeStruct((16 * (columns // HD), rows), jnp.float32)
    scratch, outs = [], [acc, stat]
    if last:
        scratch = [pltpu.VMEM(acc.shape, acc.dtype), pltpu.VMEM(stat.shape, stat.dtype)]
        outs = [jax.ShapeDtypeStruct((rows, columns), queries.dtype)]
    scratch += [
        pltpu.VMEM((STRETCH, columns), queries.dtype),
        pltpu.VMEM((columns // HD * (HD + ONES), STRETCH), queries.dtype),
        pltpu.VMEM((8 * (columns // HD), STRETCH), jnp.float32),
    ]
    operands = [plan] + ([] if row is None else [row])
    smem = len(operands)
    operands.append(queries)
    for b in blocks:
        operands += [b[0], b[1]]
    operands += list(state)
    keys = len(blocks) * STRETCH
    result = pl.pallas_call(
        functools.partial(attend_kernel, [tuple(b[2:]) for b in blocks], row is not None, last),
        out_shape=outs,
        in_specs=[SMEM] * smem + [VMEM] * (len(operands) - smem),
        out_specs=[VMEM] * len(outs),
        scratch_shapes=scratch,
        compiler_params=room(24),
        cost_estimate=pl.CostEstimate(
            flops=4 * rows * columns * keys, bytes_accessed=8 * rows * columns,
            transcendentals=rows * columns // HD * keys,
        ),
        name="attend",
    )(*operands)
    return result[0] if last else tuple(result)


def own_blocks(keys, values):
    return [(keys, values, j * STRETCH, (1 + j, 2)) for j in range(STRETCH_DEV)]


def came_blocks(base, key_came, value_came):
    return [(key_came[d], value_came[d], 0, (base + 2 + 2 * d, 1)) for d in range(2)]


def send(down, up):
    last = lax.axis_size("seq") - 1
    from_above = lax.ppermute(down, "seq", [(i + 1, i) for i in range(last)])
    from_below = lax.ppermute(up, "seq", [(i, i + 1) for i in range(last)])
    return from_above, from_below


def exchange(rounds, plan, queries, keys, values, text_keys, text_values, key_first):
    key_here = send(*key_first)
    values, text_values, *value_first = turn_values(plan, values, text_values)
    queries = turn_queries(queries)
    value_first, queries = lax.optimization_barrier((value_first, queries))
    value_here = send(*value_first)
    state = attend_text(queries, text_keys, text_values)
    key_came, value_came = ([], []), ([], [])
    waiting = []

    def before(blocks):
        nonlocal state
        blocks, state = lax.optimization_barrier((blocks, state))
        return blocks

    for r in range(rounds - 1):
        key_here = before(key_here)
        for d in range(2):
            key_came[d].append(key_here[d])
        key_next = send(*before(choose(plan, r + 1, keys, 0, *key_came)))
        if r > 0:
            state = attend(plan, None, queries, [waiting.pop(0)], state, False)
        value_here = before(value_here)
        for d in range(2):
            value_came[d].append(value_here[d])
        waiting += came_blocks(HEADER + r * ROW, key_here, value_here)
        key_here, value_here = key_next, send(*before(choose(plan, r + 1, values, 1, *value_came)))
        if r + 2 < rounds:
            state = attend(plan, None, queries, [waiting.pop(0)], state, False)
    blocks = came_blocks(HEADER + (rounds - 1) * ROW, key_here, value_here)
    state = attend(plan, None, queries, own_blocks(keys, values) + waiting, state, False)
    return attend(plan, None, queries, blocks, state, True)


def long_exchange(plan, queries, keys, values, text_keys, text_values, key_first):
    values, text_values, *value_first = turn_values(plan, values, text_values)
    queries = turn_queries(queries)
    state = attend_text(queries, text_keys, text_values)
    state = attend(plan, None, queries, own_blocks(keys, values), state, False)

    def body(carry):
        r, key_here, value_here, state = carry
        row = r.reshape(1)
        key_here = send(*choose(plan, row, keys, 0, [key_here[0]], [key_here[1]]))
        value_here = send(*choose(plan, row, values, 1, [value_here[0]], [value_here[1]]))
        state = attend(plan, row, queries, came_blocks(0, key_here, value_here), state, False)
        return (r + 1, key_here, value_here, state)

    carry = (jnp.int32(0), tuple(key_first), tuple(value_first), state)
    _, _, _, (acc, stat) = lax.while_loop(lambda c: c[0] < plan[5], body, carry)
    share = jnp.repeat(1.0 / stat[8::16], HD, axis=0)
    return jnp.transpose(acc * share).astype(queries.dtype)


def shards(
    queries, key_rows, value_rows, text_keys, text_values,
    shot_of_stretch, anchor_stretch, context_count, context_ids,
):
    groups = lax.axis_size("seq")
    tables = (shot_of_stretch, anchor_stretch, context_count, context_ids.T)
    plan, branch, key_down, key_up = make_plan(groups, tables, key_rows)
    branches = [functools.partial(exchange, rounds) for rounds in ROUNDS] + [long_exchange]
    return lax.switch(
        branch[0], branches, plan, queries, key_rows, value_rows, text_keys, text_values,
        (key_down, key_up),
    )


def solution(mesh):
    return jax.shard_map(
        shards,
        mesh=mesh,
        in_specs=(
            P(("rep", "seq"), "shot"),
            P(("rep", "seq"), "shot"),
            P(("rep", "seq"), "shot"),
            P("rep", "shot"),
            P("rep", "shot"),
            P("rep"),
            P("rep"),
            P("rep"),
            P("rep", None),
        ),
        out_specs=P(("rep", "seq"), "shot"),
        check_vma=False,
    )
```

```python
import functools
import math

import jax
import jax.numpy as jnp
from jax import lax
from jax.experimental import pallas as pl
from jax.experimental.pallas import tpu as pltpu
from jax.sharding import PartitionSpec as P

HD = 128
STRETCH = 512
STRETCH_DEV = 2
ROUNDS = (3, 4)
ROW = 8
HEADER = 8
TURN = 256
GUARD = 2.0 ** 100
ONES = 16
EXPONENT = HD ** (-0.5) * math.log2(math.e)
SMEM = pl.BlockSpec(memory_space=pltpu.SMEM)
VMEM = pl.BlockSpec(memory_space=pltpu.VMEM)


def room(mebibytes):
    return pltpu.CompilerParams(vmem_limit_bytes=mebibytes * 1024 * 1024)


def quick_plan(groups, shot, anchor, count, ids, keys, plan, targets):
    total = STRETCH_DEV * groups
    slots = ids.shape[0]
    me = lax.axis_index("seq")
    one = jnp.int32(1)

    def listed(c):
        live = count[c]
        yield one << anchor[shot[c]]
        for s in range(slots):
            yield jnp.where(s < live, one << ids[s, c], 0)

    need = []
    for g in range(groups):
        mask = jnp.int32(0)
        for c in range(STRETCH_DEV * g, STRETCH_DEV * (g + 1)):
            for entry in listed(c):
                mask = mask | entry
        need.append(mask)

    once, twice = [], []
    for q in range(STRETCH_DEV):
        c = STRETCH_DEV * me + q
        seen, again = one << c, jnp.int32(0)
        for entry in listed(c):
            again = again | (seen & entry)
            seen = seen | entry
        once.append(seen)
        twice.append(again)

    def times(q, stretch):
        return jnp.where((once[q] & stretch) != 0, 1, 0) + jnp.where((twice[q] & stretch) != 0, 1, 0)

    first_own = one << (STRETCH_DEV * me)
    second_own = first_own << 1
    for q in range(STRETCH_DEV):
        plan[1 + 2 * q] = times(q, first_own)
        plan[2 + 2 * q] = times(q, second_own)

    ways = []
    for d in range(2):
        order = list(range(groups))[:: 2 * d - 1]
        own = [((1 << STRETCH_DEV) - 1) << (STRETCH_DEV * g) for g in order]
        before = [sum(own[:k]) for k in range(groups)]
        beyond = _beyond(need, order, before)
        ways.append((own, beyond, [own[k] & beyond[k] for k in range(groups)]))

    rounds = jnp.int32(0)
    arrived = [[], []]
    for r in range(ROUNDS[-1]):
        pending = jnp.int32(0)
        for d in range(2):
            _, beyond, onward = ways[d]
            at = groups - 1 - me if d == 0 else me
            picks = []
            for k in range(groups - 1):
                pending = pending | onward[k]
                pick = onward[k] & beyond[groups - 2]
                for g in reversed(range(k, groups - 2)):
                    pick = jnp.where(pick != 0, pick, onward[k] & beyond[g])
                picks.append(pick & -pick)
            for k in range(groups - 1):
                onward[k] = onward[k] & ~picks[k]
            for k in range(1, groups - 1):
                onward[k] = onward[k] | (picks[k - 1] & beyond[k])
            sent, came = jnp.int32(0), jnp.int32(0)
            for k in range(groups - 1):
                sent = jnp.where(at == k, picks[k], sent)
                came = jnp.where(at == k + 1, picks[k], came)
            choice = jnp.where(sent == second_own, 1, 0)
            for i, earlier in enumerate(arrived[d]):
                choice = jnp.where((sent == earlier) & (sent != 0), STRETCH_DEV + i, choice)
            arrived[d].append(came)
            plan[HEADER + r * ROW + d] = choice
            for q in range(STRETCH_DEV):
                plan[HEADER + r * ROW + 2 + 2 * d + q] = times(q, came)
            if r == 0:
                start = pl.multiple_of(choice * STRETCH, STRETCH)
                targets[d][...] = keys[pl.ds(start, STRETCH), :]
        rounds = rounds + jnp.where(pending != 0, 1, 0)
    pending = jnp.int32(0)
    for _, _, onward in ways:
        for left in onward[: groups - 1]:
            pending = pending | left
    return rounds + jnp.where(pending != 0, 1, 0)


def _beyond(need, order, before):
    beyond = []
    for k in range(len(order)):
        mask = jnp.int32(0)
        held = before[k + 1] if k + 1 < len(order) else 0
        for g in order[k + 1 :]:
            mask = mask | need[g]
        beyond.append(mask & held)
    return beyond


def plan_kernel(
    groups, cap, shot, anchor, count, ids, keys,
    plan, branch, key_down, key_up, *scratch,
):
    def list_plan():
        return long_plan(groups, cap, shot, anchor, count, ids, plan, *scratch)

    if STRETCH_DEV * groups <= 16:
        rounds = quick_plan(groups, shot, anchor, count, ids, keys, plan, (key_down, key_up))
        plan[0] = rounds

        @pl.when(rounds > ROUNDS[-1])
        def _():
            list_plan()
    else:
        rounds = list_plan()
        for d, target in enumerate((key_down, key_up)):
            start = pl.multiple_of(plan[HEADER + d] * STRETCH, STRETCH)
            target[...] = keys[pl.ds(start, STRETCH), :]
    branch[0] = sum(jnp.where(rounds > length, 1, 0) for length in ROUNDS)


def long_plan(groups, cap, shot, anchor, count, ids, plan, dest, place, hold, stamp, times, best):
    total = STRETCH_DEV * groups
    slots = ids.shape[0]
    small = total <= 16
    bits = total.bit_length()
    me = lax.axis_index("seq")
    mine = (groups - 1 - me, me)

    def each(length, body):
        if small:
            for i in range(length):
                body(i)
        else:
            lax.fori_loop(0, length, lambda i, c: (body(i), c)[1], 0)

    def clear(e):
        g = e >> 1
        dest[e] = groups - 1 - g
        dest[total + e] = g
        times[e] = 0
        times[total + e] = 0

    each(total, clear)

    def stand(e):
        g = e >> 1
        for d, at in enumerate((groups - 1 - g, g)):
            place[d * total + e] = at
            hold[d * total + e] = e & 1
            stamp[d * total + e] = -1

    each(total, stand)

    def read(c):
        g = c >> 1

        def entry(e):
            dest[e] = jnp.maximum(dest[e], groups - 1 - g)
            dest[total + e] = jnp.maximum(dest[total + e], g)

        entry(anchor[shot[c]])
        live = count[c]
        for s in range(slots):
            entry(jnp.where(s < live, ids[s, c], c))

    each(total, read)

    for q in range(STRETCH_DEV):
        c = STRETCH_DEV * me + q

        def one(e, amount, q=q):
            times[q * total + e] = times[q * total + e] + amount

        one(c, 1)
        one(anchor[shot[c]], 1)
        live = count[c]
        for s in range(slots):
            alive = s < live
            one(jnp.where(alive, ids[s, c], c), jnp.where(alive, 1, 0))

    for q in range(STRETCH_DEV):
        for j in range(STRETCH_DEV):
            plan[1 + 2 * q + j] = times[q * total + STRETCH_DEV * me + j]
    for i in range(ROW * ROUNDS[-1]):
        plan[HEADER + i] = 0

    def remaining():
        return lax.fori_loop(
            0, 2 * total, lambda e, s: s + dest[e] - place[e], jnp.int32(0), unroll=small
        )

    def a_round(r, transit):
        moves = jnp.int32(0)
        for d in range(2):
            base = d * total
            for k in range(groups) if small else ():
                best[k] = -1
            if not small:
                each(groups, lambda k: best.__setitem__(k, jnp.int32(-1)))

            def rank(e, base=base):
                at = place[base + e]
                to = dest[base + e]
                key = (to << bits) | e
                if transit:
                    key = jnp.where(stamp[base + e] == r, key + (groups << bits), key)
                best[at] = jnp.maximum(best[at], jnp.where(to > at, key, -1))

            each(total, rank)
            sent = best[mine[d]]
            mask = (1 << bits) - 1
            plan[HEADER + r * ROW + d] = jnp.where(sent < 0, 0, hold[base + (jnp.maximum(sent, 0) & mask)])
            came = jnp.where(mine[d] > 0, best[jnp.maximum(mine[d] - 1, 0)], -1)
            come = jnp.maximum(came, 0) & mask
            for q in range(STRETCH_DEV):
                plan[HEADER + r * ROW + 2 + 2 * d + q] = jnp.where(came < 0, 0, times[q * total + come])

            @pl.when(came >= 0)
            def _(come=come, base=base):
                hold[base + come] = 2 + r

            def move(k, base=base):
                key = best[k]

                @pl.when(key >= 0)
                def _():
                    e = key & mask
                    place[base + e] = k + 1
                    stamp[base + e] = r + 1

                return jnp.where(key >= 0, 1, 0)

            if small:
                for k in range(groups - 1):
                    moves += move(k)
            else:
                moves += lax.fori_loop(0, groups - 1, lambda k, s: s + move(k), jnp.int32(0))
        return moves

    hops = remaining()

    def go_on(carry):
        return (carry[1] > 0) & (carry[0] < cap)

    rounds, _ = lax.while_loop(
        go_on, lambda c: (c[0] + 1, c[1] - a_round(c[0], False)), (jnp.int32(0), hops)
    )
    plan[0] = rounds

    @pl.when(rounds > ROUNDS[-1])
    def _():
        each(total, stand)
        again, _ = lax.while_loop(
            go_on, lambda c: (c[0] + 1, c[1] - a_round(c[0], True)), (jnp.int32(0), hops)
        )
        plan[5] = again

    return rounds


def make_plan(groups, tables, keys):
    total = STRETCH_DEV * groups
    cap = 2 * groups + 16
    block = jax.ShapeDtypeStruct((STRETCH, keys.shape[1]), keys.dtype)
    return pl.pallas_call(
        functools.partial(plan_kernel, groups, cap),
        out_shape=[
            jax.ShapeDtypeStruct((HEADER + cap * ROW,), jnp.int32),
            jax.ShapeDtypeStruct((1,), jnp.int32),
            block,
            block,
        ],
        in_specs=[SMEM] * 4 + [VMEM],
        out_specs=[SMEM] * 2 + [VMEM] * 2,
        scratch_shapes=[pltpu.SMEM((2 * total,), jnp.int32) for _ in range(5)]
        + [pltpu.SMEM((groups,), jnp.int32)],
        name="plan",
    )(*tables, keys)


def choose_kernel(row, arrivals, axis, plan, *refs):
    if row is None:
        at, own, *refs = refs
        base = HEADER + at[0] * ROW
    else:
        own, *refs = refs
        base = HEADER + row * ROW
    came, outs = refs[: 2 * arrivals], refs[2 * arrivals :]
    for d in range(2):
        choice = plan[base + d]

        @pl.when(choice < STRETCH_DEV)
        def _(d=d, choice=choice):
            part = pl.ds(pl.multiple_of(choice * STRETCH, STRETCH), STRETCH)
            outs[d][...] = own[part, :] if axis == 0 else own[:, part]

        for i in range(arrivals):
            picked = choice == STRETCH_DEV + i if row is not None else choice >= STRETCH_DEV

            @pl.when(picked)
            def _(d=d, i=i):
                outs[d][...] = came[d * arrivals + i][...]


def choose(plan, row, own, axis, down, up):
    static = isinstance(row, int)
    shape = list(own.shape)
    shape[axis] = STRETCH
    block = jax.ShapeDtypeStruct(tuple(shape), own.dtype)
    return pl.pallas_call(
        functools.partial(choose_kernel, row if static else None, len(down), axis),
        out_shape=[block] * 2,
        in_specs=[SMEM] + ([] if static else [SMEM]) + [VMEM] * (1 + 2 * len(down)),
        out_specs=[VMEM] * 2,
        compiler_params=room(8),
        cost_estimate=pl.CostEstimate(flops=0, bytes_accessed=8 * block.size, transcendentals=0),
        name="choose",
    )(plan, *(() if static else (row,)), own, *down, *up)


def score(keys, queries):
    return jnp.dot(jnp.concatenate([keys, keys], axis=1), queries, preferred_element_type=jnp.float32)


def turn_queries_kernel(queries, split):
    for h in range(queries.shape[1] // HD):
        cols = pl.ds(h * HD, HD)
        for t in range(queries.shape[0] // TURN):
            at = pl.ds(t * TURN, TURN)
            turned = jnp.transpose(queries[at, cols].astype(jnp.float32) * EXPONENT)
            high = turned.astype(jnp.bfloat16)
            split[pl.ds(2 * h * HD, HD), at] = high
            split[pl.ds((2 * h + 1) * HD, HD), at] = (turned - high.astype(jnp.float32)).astype(jnp.bfloat16)


def turn_queries(queries):
    rows, columns = queries.shape
    return pl.pallas_call(
        turn_queries_kernel,
        out_shape=jax.ShapeDtypeStruct((2 * columns, rows), queries.dtype),
        in_specs=[VMEM],
        out_specs=VMEM,
        compiler_params=room(10),
        name="turn_queries",
    )(queries)


def text_kernel(queries, text_keys, text_values, acc, stat):
    ones = jnp.ones((ONES, text_keys.shape[0]), jnp.bfloat16)

    def stretch(t, c):
        at = pl.ds(pl.multiple_of(t * STRETCH, STRETCH), STRETCH)
        for h in range(text_keys.shape[1] // HD):
            cols = pl.ds(h * HD, HD)
            scores = score(text_keys[:, cols], queries[pl.ds(2 * h * HD, 2 * HD), at])
            peak = jnp.max(scores, axis=0, keepdims=True)
            both = jnp.dot(
                jnp.concatenate([text_values[cols, :], ones], axis=0),
                jnp.exp2(scores - peak).astype(jnp.bfloat16), preferred_element_type=jnp.float32,
            )
            acc[cols, at] = both[:HD]
            stat[16 * h : 16 * h + 1, at] = peak
            stat[16 * h + 8 : 16 * h + 9, at] = both[HD : HD + 1]
        return c

    lax.fori_loop(0, queries.shape[1] // STRETCH, stretch, 0)


def attend_text(queries, text_keys, text_values):
    columns, rows = queries.shape[0] // 2, queries.shape[1]
    return pl.pallas_call(
        text_kernel,
        out_shape=[
            jax.ShapeDtypeStruct((columns, rows), jnp.float32),
            jax.ShapeDtypeStruct((16 * (columns // HD), rows), jnp.float32),
        ],
        in_specs=[VMEM] * 3,
        out_specs=[VMEM] * 2,
        compiler_params=room(16),
        name="attend_text",
    )(queries, text_keys, text_values)


def turn_values_kernel(plan, values, text_values, values_out, text_out, down, up):
    for h in range(values.shape[1] // HD):
        cols = pl.ds(h * HD, HD)
        for source, target in ((values, values_out), (text_values, text_out)):
            for t in range(source.shape[0] // TURN):
                at = pl.ds(t * TURN, TURN)
                target[cols, at] = jnp.transpose(source[at, cols])
    for d, target in enumerate((down, up)):
        start = pl.multiple_of(plan[HEADER + d] * STRETCH, STRETCH)
        target[...] = values_out[:, pl.ds(start, STRETCH)]


def turn_values(plan, values, text_values):
    rows, columns = values.shape
    outs = [(columns, rows), (columns, text_values.shape[0]), (columns, STRETCH), (columns, STRETCH)]
    return pl.pallas_call(
        turn_values_kernel,
        out_shape=[jax.ShapeDtypeStruct(shape, values.dtype) for shape in outs],
        in_specs=[SMEM, VMEM, VMEM],
        out_specs=[VMEM] * 4,
        compiler_params=room(10),
        name="turn_values",
    )(plan, values, text_values)


def attend_kernel(blocks, rowed, last, *refs):
    refs = list(refs)
    plan = refs.pop(0)
    base = HEADER + refs.pop(0)[0] * ROW if rowed else 0
    queries = refs.pop(0)
    block_refs = [(refs.pop(0), refs.pop(0)) for _ in blocks]
    acc_in, stat_in, *refs = refs
    *refs, keys_at, values_at, fine = refs
    if last:
        out, acc, stat = refs
    else:
        acc, stat = refs
    rows = queries.shape[1]
    heads = queries.shape[0] // (2 * HD)
    wide = HD + ONES

    acc[...] = acc_in[...]
    stat[...] = stat_in[...]
    for h in range(heads):
        values_at[pl.ds(h * wide + HD, ONES), :] = jnp.ones((ONES, STRETCH), jnp.bfloat16)

    def head(h):
        def part(start, size, by):
            return pl.ds(start if isinstance(h, int) else pl.multiple_of(start, by), size)

        return (
            part(h * HD, HD, HD), part(2 * h * HD, 2 * HD, 2 * HD), part(h * wide, wide, ONES),
            part(16 * h, 1, 8), part(16 * h + 8, 1, 8),
        )

    def step(start, twice):
        at = pl.ds(pl.multiple_of(start, STRETCH), STRETCH)

        lowest = jnp.ones((1, STRETCH), jnp.float32)
        scores = score(keys_at[:, head(0)[0]], queries[head(0)[1], at])
        for h in range(heads):
            cols, _, mixed, refer, total = head(h)
            following = None
            if h + 1 < heads:
                following = score(keys_at[:, head(h + 1)[0]], queries[head(h + 1)[1], at])
            weights = jnp.exp2(scores - (stat[refer, at] - twice)).astype(jnp.bfloat16)
            product = jnp.dot(values_at[mixed, :], weights, preferred_element_type=jnp.float32)
            mass = product[HD : HD + 1]
            fits = mass < GUARD
            acc[cols, at] = jnp.where(fits, acc[cols, at] + product[:HD], acc[cols, at])
            stat[total, at] += jnp.where(fits, mass, 0.0)
            fit = jnp.where(fits, 1.0, 0.0)
            fine[pl.ds(8 * h, 1), :] = fit
            lowest = jnp.minimum(lowest, fit)
            scores = following

        @pl.when(jnp.min(lowest) < 0.5)
        def _():
            parts = STRETCH // HD
            lax.fori_loop(
                0, heads * parts, lambda i, c: (again(start, i // parts, i % parts * HD, twice), c)[1], 0
            )

    def again(start, h, w, twice):
        at = pl.ds(pl.multiple_of(start + w, HD), HD)
        cols, both, mixed, refer, total = head(h)
        scores = score(keys_at[:, cols], queries[both, at])
        before = stat[refer, at]
        peak = jnp.maximum(jnp.max(scores, axis=0, keepdims=True), before)
        keep = jnp.exp2(before - peak)
        weights = jnp.exp2(scores - (peak - twice)).astype(jnp.bfloat16)
        product = jnp.dot(values_at[mixed, :], weights, preferred_element_type=jnp.float32)
        miss = fine[pl.ds(pl.multiple_of(8 * h, 8), 1), pl.ds(pl.multiple_of(w, HD), HD)] < 0.5
        mass = product[HD : HD + 1] + stat[total, at] * keep
        acc[cols, at] = jnp.where(miss, product[:HD] + acc[cols, at] * keep, acc[cols, at])
        stat[total, at] = jnp.where(miss, mass, stat[total, at])
        stat[refer, at] = jnp.where(miss, peak, before)

    def visit(b, c):
        place, stride = jnp.int32(0), jnp.int32(0)
        for number, (_, (first, second)) in enumerate(blocks):
            place = jnp.where(b == number, first, place)
            stride = jnp.where(b == number, second, stride)
        place = base + place

        @pl.when(plan[place] + plan[place + stride] > 0)
        def _():
            for number, (start, _) in enumerate(blocks):
                @pl.when(b == number)
                def _(start=start, number=number):
                    part = pl.ds(start, STRETCH)
                    keys_at[...] = block_refs[number][0][part, :]
                    for h in range(heads):
                        values_at[pl.ds(h * wide, HD), :] = block_refs[number][1][pl.ds(h * HD, HD), part]

            def stretch(t, c):
                times = plan[place + t * stride]

                @pl.when(times > 0)
                def _():
                    step(t * STRETCH, jnp.where(times > 1, 1.0, 0.0))

                return c

            lax.fori_loop(0, rows // STRETCH, stretch, 0)

        return c

    lax.fori_loop(0, len(blocks), visit, 0)

    if last:
        for h in range(heads):
            cols = pl.ds(h * HD, HD)
            for t in range(rows // TURN):
                at = pl.ds(t * TURN, TURN)
                share = 1.0 / stat[16 * h + 8 : 16 * h + 9, at]
                out[at, cols] = jnp.transpose((acc[cols, at] * share).astype(out.dtype))


def attend(plan, row, queries, blocks, state, last):
    columns, rows = queries.shape[0] // 2, queries.shape[1]
    acc = jax.ShapeDtypeStruct((columns, rows), jnp.float32)
    stat = jax.ShapeDtypeStruct((16 * (columns // HD), rows), jnp.float32)
    scratch, outs = [], [acc, stat]
    if last:
        scratch = [pltpu.VMEM(acc.shape, acc.dtype), pltpu.VMEM(stat.shape, stat.dtype)]
        outs = [jax.ShapeDtypeStruct((rows, columns), queries.dtype)]
    scratch += [
        pltpu.VMEM((STRETCH, columns), queries.dtype),
        pltpu.VMEM((columns // HD * (HD + ONES), STRETCH), queries.dtype),
        pltpu.VMEM((8 * (columns // HD), STRETCH), jnp.float32),
    ]
    operands = [plan] + ([] if row is None else [row])
    smem = len(operands)
    operands.append(queries)
    for b in blocks:
        operands += [b[0], b[1]]
    operands += list(state)
    keys = len(blocks) * STRETCH
    result = pl.pallas_call(
        functools.partial(attend_kernel, [tuple(b[2:]) for b in blocks], row is not None, last),
        out_shape=outs,
        in_specs=[SMEM] * smem + [VMEM] * (len(operands) - smem),
        out_specs=[VMEM] * len(outs),
        scratch_shapes=scratch,
        compiler_params=room(24),
        cost_estimate=pl.CostEstimate(
            flops=4 * rows * columns * keys, bytes_accessed=8 * rows * columns,
            transcendentals=rows * columns // HD * keys,
        ),
        name="attend",
    )(*operands)
    return result[0] if last else tuple(result)


def own_blocks(keys, values):
    return [(keys, values, j * STRETCH, (1 + j, 2)) for j in range(STRETCH_DEV)]


def came_blocks(base, key_came, value_came):
    return [(key_came[d], value_came[d], 0, (base + 2 + 2 * d, 1)) for d in range(2)]


def send(down, up):
    last = lax.axis_size("seq") - 1
    from_above = lax.ppermute(down, "seq", [(i + 1, i) for i in range(last)])
    from_below = lax.ppermute(up, "seq", [(i, i + 1) for i in range(last)])
    return from_above, from_below


def exchange(rounds, plan, queries, keys, values, text_keys, text_values, key_first):
    key_here = send(*key_first)
    values, text_values, *value_first = turn_values(plan, values, text_values)
    queries = turn_queries(queries)
    value_first, queries = lax.optimization_barrier((value_first, queries))
    value_here = send(*value_first)
    state = attend_text(queries, text_keys, text_values)
    first_own, second_own = own_blocks(keys, values)
    key_came, value_came = ([], []), ([], [])

    def before(blocks):
        nonlocal state
        blocks, state = lax.optimization_barrier((blocks, state))
        return blocks

    for r in range(rounds - 1):
        key_here = before(key_here)
        for d in range(2):
            key_came[d].append(key_here[d])
        key_next = send(*before(choose(plan, r + 1, keys, 0, *key_came)))
        if r == 1:
            state = attend(plan, None, queries, [first_own], state, False)
        value_here = before(value_here)
        for d in range(2):
            value_came[d].append(value_here[d])
        came = came_blocks(HEADER + r * ROW, key_here, value_here)
        key_here, value_here = key_next, send(*before(choose(plan, r + 1, values, 1, *value_came)))
        blocks = came if r + 2 < rounds else [second_own] + came
        state = attend(plan, None, queries, blocks, state, False)
    blocks = came_blocks(HEADER + (rounds - 1) * ROW, key_here, value_here)
    return attend(plan, None, queries, blocks, state, True)


def long_exchange(plan, queries, keys, values, text_keys, text_values, key_first):
    values, text_values, *value_first = turn_values(plan, values, text_values)
    queries = turn_queries(queries)
    state = attend_text(queries, text_keys, text_values)
    state = attend(plan, None, queries, own_blocks(keys, values), state, False)

    def body(carry):
        r, key_here, value_here, state = carry
        row = r.reshape(1)
        key_here = send(*choose(plan, row, keys, 0, [key_here[0]], [key_here[1]]))
        value_here = send(*choose(plan, row, values, 1, [value_here[0]], [value_here[1]]))
        state = attend(plan, row, queries, came_blocks(0, key_here, value_here), state, False)
        return (r + 1, key_here, value_here, state)

    carry = (jnp.int32(0), tuple(key_first), tuple(value_first), state)
    _, _, _, (acc, stat) = lax.while_loop(lambda c: c[0] < plan[5], body, carry)
    share = jnp.repeat(1.0 / stat[8::16], HD, axis=0)
    return jnp.transpose(acc * share).astype(queries.dtype)


def shards(
    queries, key_rows, value_rows, text_keys, text_values,
    shot_of_stretch, anchor_stretch, context_count, context_ids,
):
    groups = lax.axis_size("seq")
    tables = (shot_of_stretch, anchor_stretch, context_count, context_ids.T)
    plan, branch, key_down, key_up = make_plan(groups, tables, key_rows)
    branches = [functools.partial(exchange, rounds) for rounds in ROUNDS] + [long_exchange]
    return lax.switch(
        branch[0], branches, plan, queries, key_rows, value_rows, text_keys, text_values,
        (key_down, key_up),
    )


def solution(mesh):
    return jax.shard_map(
        shards,
        mesh=mesh,
        in_specs=(
            P(("rep", "seq"), "shot"),
            P(("rep", "seq"), "shot"),
            P(("rep", "seq"), "shot"),
            P("rep", "shot"),
            P("rep", "shot"),
            P("rep"),
            P("rep"),
            P("rep"),
            P("rep", None),
        ),
        out_specs=P(("rep", "seq"), "shot"),
        check_vma=False,
    )
```

```python
import functools
import math

import jax
import jax.numpy as jnp
from jax import lax
from jax.experimental import pallas as pl
from jax.experimental.pallas import tpu as pltpu
from jax.sharding import PartitionSpec as P

HD = 128
STRETCH = 512
STRETCH_DEV = 2
ROUNDS = (3, 4)
ROW = 8
HEADER = 8
TURN = 256
GUARD = 2.0 ** 100
ONES = 16
EXPONENT = HD ** (-0.5) * math.log2(math.e)
SMEM = pl.BlockSpec(memory_space=pltpu.SMEM)
VMEM = pl.BlockSpec(memory_space=pltpu.VMEM)


def room(mebibytes):
    return pltpu.CompilerParams(vmem_limit_bytes=mebibytes * 1024 * 1024)


def quick_plan(groups, shot, anchor, count, ids, keys, plan, targets):
    total = STRETCH_DEV * groups
    slots = ids.shape[0]
    me = lax.axis_index("seq")
    one = jnp.int32(1)

    def listed(c):
        live = count[c]
        yield one << anchor[shot[c]]
        for s in range(slots):
            yield jnp.where(s < live, one << ids[s, c], 0)

    need = []
    for g in range(groups):
        mask = jnp.int32(0)
        for c in range(STRETCH_DEV * g, STRETCH_DEV * (g + 1)):
            for entry in listed(c):
                mask = mask | entry
        need.append(mask)

    once, twice = [], []
    for q in range(STRETCH_DEV):
        c = STRETCH_DEV * me + q
        seen, again = one << c, jnp.int32(0)
        for entry in listed(c):
            again = again | (seen & entry)
            seen = seen | entry
        once.append(seen)
        twice.append(again)

    def times(q, stretch):
        return jnp.where((once[q] & stretch) != 0, 1, 0) + jnp.where((twice[q] & stretch) != 0, 1, 0)

    first_own = one << (STRETCH_DEV * me)
    second_own = first_own << 1
    for q in range(STRETCH_DEV):
        plan[1 + 2 * q] = times(q, first_own)
        plan[2 + 2 * q] = times(q, second_own)

    ways = []
    for d in range(2):
        order = list(range(groups))[:: 2 * d - 1]
        own = [((1 << STRETCH_DEV) - 1) << (STRETCH_DEV * g) for g in order]
        before = [sum(own[:k]) for k in range(groups)]
        beyond = _beyond(need, order, before)
        ways.append((own, beyond, [own[k] & beyond[k] for k in range(groups)]))

    rounds = jnp.int32(0)
    arrived = [[], []]
    for r in range(ROUNDS[-1]):
        pending = jnp.int32(0)
        for d in range(2):
            _, beyond, onward = ways[d]
            at = groups - 1 - me if d == 0 else me
            picks = []
            for k in range(groups - 1):
                pending = pending | onward[k]
                pick = onward[k] & beyond[groups - 2]
                for g in reversed(range(k, groups - 2)):
                    pick = jnp.where(pick != 0, pick, onward[k] & beyond[g])
                picks.append(pick & -pick)
            for k in range(groups - 1):
                onward[k] = onward[k] & ~picks[k]
            for k in range(1, groups - 1):
                onward[k] = onward[k] | (picks[k - 1] & beyond[k])
            sent, came = jnp.int32(0), jnp.int32(0)
            for k in range(groups - 1):
                sent = jnp.where(at == k, picks[k], sent)
                came = jnp.where(at == k + 1, picks[k], came)
            choice = jnp.where(sent == second_own, 1, 0)
            for i, earlier in enumerate(arrived[d]):
                choice = jnp.where((sent == earlier) & (sent != 0), STRETCH_DEV + i, choice)
            arrived[d].append(came)
            plan[HEADER + r * ROW + d] = choice
            for q in range(STRETCH_DEV):
                plan[HEADER + r * ROW + 2 + 2 * d + q] = times(q, came)
            if r == 0:
                start = pl.multiple_of(choice * STRETCH, STRETCH)
                targets[d][...] = keys[pl.ds(start, STRETCH), :]
        rounds = rounds + jnp.where(pending != 0, 1, 0)
    pending = jnp.int32(0)
    for _, _, onward in ways:
        for left in onward[: groups - 1]:
            pending = pending | left
    return rounds + jnp.where(pending != 0, 1, 0)


def _beyond(need, order, before):
    beyond = []
    for k in range(len(order)):
        mask = jnp.int32(0)
        held = before[k + 1] if k + 1 < len(order) else 0
        for g in order[k + 1 :]:
            mask = mask | need[g]
        beyond.append(mask & held)
    return beyond


def plan_kernel(
    groups, cap, shot, anchor, count, ids, keys,
    plan, branch, key_down, key_up, *scratch,
):
    def list_plan():
        return long_plan(groups, cap, shot, anchor, count, ids, plan, *scratch)

    if STRETCH_DEV * groups <= 16:
        rounds = quick_plan(groups, shot, anchor, count, ids, keys, plan, (key_down, key_up))
        plan[0] = rounds

        @pl.when(rounds > ROUNDS[-1])
        def _():
            list_plan()
    else:
        rounds = list_plan()
        for d, target in enumerate((key_down, key_up)):
            start = pl.multiple_of(plan[HEADER + d] * STRETCH, STRETCH)
            target[...] = keys[pl.ds(start, STRETCH), :]
    branch[0] = sum(jnp.where(rounds > length, 1, 0) for length in ROUNDS)


def long_plan(groups, cap, shot, anchor, count, ids, plan, dest, place, hold, stamp, times, best):
    total = STRETCH_DEV * groups
    slots = ids.shape[0]
    small = total <= 16
    bits = total.bit_length()
    me = lax.axis_index("seq")
    mine = (groups - 1 - me, me)

    def each(length, body):
        if small:
            for i in range(length):
                body(i)
        else:
            lax.fori_loop(0, length, lambda i, c: (body(i), c)[1], 0)

    def clear(e):
        g = e >> 1
        dest[e] = groups - 1 - g
        dest[total + e] = g
        times[e] = 0
        times[total + e] = 0

    each(total, clear)

    def stand(e):
        g = e >> 1
        for d, at in enumerate((groups - 1 - g, g)):
            place[d * total + e] = at
            hold[d * total + e] = e & 1
            stamp[d * total + e] = -1

    each(total, stand)

    def read(c):
        g = c >> 1

        def entry(e):
            dest[e] = jnp.maximum(dest[e], groups - 1 - g)
            dest[total + e] = jnp.maximum(dest[total + e], g)

        entry(anchor[shot[c]])
        live = count[c]
        for s in range(slots):
            entry(jnp.where(s < live, ids[s, c], c))

    each(total, read)

    for q in range(STRETCH_DEV):
        c = STRETCH_DEV * me + q

        def one(e, amount, q=q):
            times[q * total + e] = times[q * total + e] + amount

        one(c, 1)
        one(anchor[shot[c]], 1)
        live = count[c]
        for s in range(slots):
            alive = s < live
            one(jnp.where(alive, ids[s, c], c), jnp.where(alive, 1, 0))

    for q in range(STRETCH_DEV):
        for j in range(STRETCH_DEV):
            plan[1 + 2 * q + j] = times[q * total + STRETCH_DEV * me + j]
    for i in range(ROW * ROUNDS[-1]):
        plan[HEADER + i] = 0

    def remaining():
        return lax.fori_loop(
            0, 2 * total, lambda e, s: s + dest[e] - place[e], jnp.int32(0), unroll=small
        )

    def a_round(r, transit):
        moves = jnp.int32(0)
        for d in range(2):
            base = d * total
            for k in range(groups) if small else ():
                best[k] = -1
            if not small:
                each(groups, lambda k: best.__setitem__(k, jnp.int32(-1)))

            def rank(e, base=base):
                at = place[base + e]
                to = dest[base + e]
                key = (to << bits) | e
                if transit:
                    key = jnp.where(stamp[base + e] == r, key + (groups << bits), key)
                best[at] = jnp.maximum(best[at], jnp.where(to > at, key, -1))

            each(total, rank)
            sent = best[mine[d]]
            mask = (1 << bits) - 1
            plan[HEADER + r * ROW + d] = jnp.where(sent < 0, 0, hold[base + (jnp.maximum(sent, 0) & mask)])
            came = jnp.where(mine[d] > 0, best[jnp.maximum(mine[d] - 1, 0)], -1)
            come = jnp.maximum(came, 0) & mask
            for q in range(STRETCH_DEV):
                plan[HEADER + r * ROW + 2 + 2 * d + q] = jnp.where(came < 0, 0, times[q * total + come])

            @pl.when(came >= 0)
            def _(come=come, base=base):
                hold[base + come] = 2 + r

            def move(k, base=base):
                key = best[k]

                @pl.when(key >= 0)
                def _():
                    e = key & mask
                    place[base + e] = k + 1
                    stamp[base + e] = r + 1

                return jnp.where(key >= 0, 1, 0)

            if small:
                for k in range(groups - 1):
                    moves += move(k)
            else:
                moves += lax.fori_loop(0, groups - 1, lambda k, s: s + move(k), jnp.int32(0))
        return moves

    hops = remaining()

    def go_on(carry):
        return (carry[1] > 0) & (carry[0] < cap)

    rounds, _ = lax.while_loop(
        go_on, lambda c: (c[0] + 1, c[1] - a_round(c[0], False)), (jnp.int32(0), hops)
    )
    plan[0] = rounds

    @pl.when(rounds > ROUNDS[-1])
    def _():
        each(total, stand)
        again, _ = lax.while_loop(
            go_on, lambda c: (c[0] + 1, c[1] - a_round(c[0], True)), (jnp.int32(0), hops)
        )
        plan[5] = again

    return rounds


def make_plan(groups, tables, keys):
    total = STRETCH_DEV * groups
    cap = 2 * groups + 16
    block = jax.ShapeDtypeStruct((STRETCH, keys.shape[1]), keys.dtype)
    return pl.pallas_call(
        functools.partial(plan_kernel, groups, cap),
        out_shape=[
            jax.ShapeDtypeStruct((HEADER + cap * ROW,), jnp.int32),
            jax.ShapeDtypeStruct((1,), jnp.int32),
            block,
            block,
        ],
        in_specs=[SMEM] * 4 + [VMEM],
        out_specs=[SMEM] * 2 + [VMEM] * 2,
        scratch_shapes=[pltpu.SMEM((2 * total,), jnp.int32) for _ in range(5)]
        + [pltpu.SMEM((groups,), jnp.int32)],
        name="plan",
    )(*tables, keys)


def choose_kernel(row, arrivals, axis, plan, *refs):
    if row is None:
        at, own, *refs = refs
        base = HEADER + at[0] * ROW
    else:
        own, *refs = refs
        base = HEADER + row * ROW
    came, outs = refs[: 2 * arrivals], refs[2 * arrivals :]
    for d in range(2):
        choice = plan[base + d]

        @pl.when(choice < STRETCH_DEV)
        def _(d=d, choice=choice):
            part = pl.ds(pl.multiple_of(choice * STRETCH, STRETCH), STRETCH)
            outs[d][...] = own[part, :] if axis == 0 else own[:, part]

        for i in range(arrivals):
            picked = choice == STRETCH_DEV + i if row is not None else choice >= STRETCH_DEV

            @pl.when(picked)
            def _(d=d, i=i):
                outs[d][...] = came[d * arrivals + i][...]


def choose(plan, row, own, axis, down, up):
    static = isinstance(row, int)
    shape = list(own.shape)
    shape[axis] = STRETCH
    block = jax.ShapeDtypeStruct(tuple(shape), own.dtype)
    return pl.pallas_call(
        functools.partial(choose_kernel, row if static else None, len(down), axis),
        out_shape=[block] * 2,
        in_specs=[SMEM] + ([] if static else [SMEM]) + [VMEM] * (1 + 2 * len(down)),
        out_specs=[VMEM] * 2,
        compiler_params=room(8),
        cost_estimate=pl.CostEstimate(flops=0, bytes_accessed=8 * block.size, transcendentals=0),
        name="choose",
    )(plan, *(() if static else (row,)), own, *down, *up)


def score(keys, queries):
    return jnp.dot(jnp.concatenate([keys, keys], axis=1), queries, preferred_element_type=jnp.float32)


def turn_queries_kernel(queries, split):
    for h in range(queries.shape[1] // HD):
        cols = pl.ds(h * HD, HD)
        for t in range(queries.shape[0] // TURN):
            at = pl.ds(t * TURN, TURN)
            turned = jnp.transpose(queries[at, cols].astype(jnp.float32) * EXPONENT)
            high = turned.astype(jnp.bfloat16)
            split[pl.ds(2 * h * HD, HD), at] = high
            split[pl.ds((2 * h + 1) * HD, HD), at] = (turned - high.astype(jnp.float32)).astype(jnp.bfloat16)


def turn_queries(queries):
    rows, columns = queries.shape
    return pl.pallas_call(
        turn_queries_kernel,
        out_shape=jax.ShapeDtypeStruct((2 * columns, rows), queries.dtype),
        in_specs=[VMEM],
        out_specs=VMEM,
        compiler_params=room(10),
        name="turn_queries",
    )(queries)


def text_kernel(queries, text_keys, text_values, acc, stat):
    ones = jnp.ones((ONES, text_keys.shape[0]), jnp.bfloat16)

    def stretch(t, c):
        at = pl.ds(pl.multiple_of(t * STRETCH, STRETCH), STRETCH)
        for h in range(text_keys.shape[1] // HD):
            cols = pl.ds(h * HD, HD)
            scores = score(text_keys[:, cols], queries[pl.ds(2 * h * HD, 2 * HD), at])
            peak = jnp.max(scores, axis=0, keepdims=True)
            both = jnp.dot(
                jnp.concatenate([text_values[cols, :], ones], axis=0),
                jnp.exp2(scores - peak).astype(jnp.bfloat16), preferred_element_type=jnp.float32,
            )
            acc[cols, at] = both[:HD]
            stat[16 * h : 16 * h + 1, at] = peak
            stat[16 * h + 8 : 16 * h + 9, at] = both[HD : HD + 1]
        return c

    lax.fori_loop(0, queries.shape[1] // STRETCH, stretch, 0)


def attend_text(queries, text_keys, text_values):
    columns, rows = queries.shape[0] // 2, queries.shape[1]
    return pl.pallas_call(
        text_kernel,
        out_shape=[
            jax.ShapeDtypeStruct((columns, rows), jnp.float32),
            jax.ShapeDtypeStruct((16 * (columns // HD), rows), jnp.float32),
        ],
        in_specs=[VMEM] * 3,
        out_specs=[VMEM] * 2,
        compiler_params=room(16),
        name="attend_text",
    )(queries, text_keys, text_values)


def turn_values_kernel(plan, values, text_values, values_out, text_out, down, up):
    for h in range(values.shape[1] // HD):
        cols = pl.ds(h * HD, HD)
        for source, target in ((values, values_out), (text_values, text_out)):
            for t in range(source.shape[0] // TURN):
                at = pl.ds(t * TURN, TURN)
                target[cols, at] = jnp.transpose(source[at, cols])
    for d, target in enumerate((down, up)):
        start = pl.multiple_of(plan[HEADER + d] * STRETCH, STRETCH)
        target[...] = values_out[:, pl.ds(start, STRETCH)]


def turn_values(plan, values, text_values):
    rows, columns = values.shape
    outs = [(columns, rows), (columns, text_values.shape[0]), (columns, STRETCH), (columns, STRETCH)]
    return pl.pallas_call(
        turn_values_kernel,
        out_shape=[jax.ShapeDtypeStruct(shape, values.dtype) for shape in outs],
        in_specs=[SMEM, VMEM, VMEM],
        out_specs=[VMEM] * 4,
        compiler_params=room(10),
        name="turn_values",
    )(plan, values, text_values)


def head(h):
    def part(start, size, by):
        return pl.ds(start if isinstance(h, int) else pl.multiple_of(start, by), size)

    return (
        part(h * HD, HD, HD), part(2 * h * HD, 2 * HD, 2 * HD), part(h * (HD + ONES), HD + ONES, ONES),
        part(16 * h, 1, 8), part(16 * h + 8, 1, 8),
    )


def attend_kernel(blocks, rowed, *refs):
    refs = list(refs)
    plan = refs.pop(0)
    base = HEADER + refs.pop(0)[0] * ROW if rowed else 0
    queries = refs.pop(0)
    block_refs = [(refs.pop(0), refs.pop(0)) for _ in blocks]
    acc_in, stat_in, acc, stat, keys_at, values_at, fine = refs
    rows = queries.shape[1]
    heads = queries.shape[0] // (2 * HD)
    wide = HD + ONES

    acc[...] = acc_in[...]
    stat[...] = stat_in[...]
    for h in range(heads):
        values_at[pl.ds(h * wide + HD, ONES), :] = jnp.ones((ONES, STRETCH), jnp.bfloat16)

    def step(start, twice):
        at = pl.ds(pl.multiple_of(start, STRETCH), STRETCH)

        lowest = jnp.ones((1, STRETCH), jnp.float32)
        scores = score(keys_at[:, head(0)[0]], queries[head(0)[1], at])
        for h in range(heads):
            cols, _, mixed, refer, total = head(h)
            following = None
            if h + 1 < heads:
                following = score(keys_at[:, head(h + 1)[0]], queries[head(h + 1)[1], at])
            weights = jnp.exp2(scores - (stat[refer, at] - twice)).astype(jnp.bfloat16)
            product = jnp.dot(values_at[mixed, :], weights, preferred_element_type=jnp.float32)
            mass = product[HD : HD + 1]
            fits = mass < GUARD
            acc[cols, at] = jnp.where(fits, acc[cols, at] + product[:HD], acc[cols, at])
            stat[total, at] += jnp.where(fits, mass, 0.0)
            fit = jnp.where(fits, 1.0, 0.0)
            fine[pl.ds(8 * h, 1), :] = fit
            lowest = jnp.minimum(lowest, fit)
            scores = following

        @pl.when(jnp.min(lowest) < 0.5)
        def _():
            parts = STRETCH // HD
            lax.fori_loop(
                0, heads * parts, lambda i, c: (again(start, i // parts, i % parts * HD, twice), c)[1], 0
            )

    def again(start, h, w, twice):
        at = pl.ds(pl.multiple_of(start + w, HD), HD)
        cols, both, mixed, refer, total = head(h)
        scores = score(keys_at[:, cols], queries[both, at])
        before = stat[refer, at]
        peak = jnp.maximum(jnp.max(scores, axis=0, keepdims=True), before)
        keep = jnp.exp2(before - peak)
        weights = jnp.exp2(scores - (peak - twice)).astype(jnp.bfloat16)
        product = jnp.dot(values_at[mixed, :], weights, preferred_element_type=jnp.float32)
        miss = fine[pl.ds(pl.multiple_of(8 * h, 8), 1), pl.ds(pl.multiple_of(w, HD), HD)] < 0.5
        mass = product[HD : HD + 1] + stat[total, at] * keep
        acc[cols, at] = jnp.where(miss, product[:HD] + acc[cols, at] * keep, acc[cols, at])
        stat[total, at] = jnp.where(miss, mass, stat[total, at])
        stat[refer, at] = jnp.where(miss, peak, before)

    def visit(b, c):
        place, stride = jnp.int32(0), jnp.int32(0)
        for number, (_, (first, second)) in enumerate(blocks):
            place = jnp.where(b == number, first, place)
            stride = jnp.where(b == number, second, stride)
        place = base + place

        @pl.when(plan[place] + plan[place + stride] > 0)
        def _():
            for number, (start, _) in enumerate(blocks):
                @pl.when(b == number)
                def _(start=start, number=number):
                    part = pl.ds(start, STRETCH)
                    keys_at[...] = block_refs[number][0][part, :]
                    for h in range(heads):
                        values_at[pl.ds(h * wide, HD), :] = block_refs[number][1][pl.ds(h * HD, HD), part]

            def stretch(t, c):
                times = plan[place + t * stride]

                @pl.when(times > 0)
                def _():
                    step(t * STRETCH, jnp.where(times > 1, 1.0, 0.0))

                return c

            lax.fori_loop(0, rows // STRETCH, stretch, 0)

        return c

    lax.fori_loop(0, len(blocks), visit, 0)


def attend(plan, row, queries, blocks, state):
    columns, rows = queries.shape[0] // 2, queries.shape[1]
    acc = jax.ShapeDtypeStruct((columns, rows), jnp.float32)
    stat = jax.ShapeDtypeStruct((16 * (columns // HD), rows), jnp.float32)
    scratch = [
        pltpu.VMEM((STRETCH, columns), queries.dtype),
        pltpu.VMEM((columns // HD * (HD + ONES), STRETCH), queries.dtype),
        pltpu.VMEM((8 * (columns // HD), STRETCH), jnp.float32),
    ]
    operands = [plan] + ([] if row is None else [row])
    smem = len(operands)
    operands.append(queries)
    for b in blocks:
        operands += [b[0], b[1]]
    operands += list(state)
    keys = len(blocks) * STRETCH
    return pl.pallas_call(
        functools.partial(attend_kernel, [tuple(b[2:]) for b in blocks], row is not None),
        out_shape=[acc, stat],
        in_specs=[SMEM] * smem + [VMEM] * (len(operands) - smem),
        out_specs=[VMEM] * 2,
        scratch_shapes=scratch,
        compiler_params=room(24),
        cost_estimate=pl.CostEstimate(
            flops=4 * rows * columns * keys, bytes_accessed=8 * rows * columns,
            transcendentals=rows * columns // HD * keys,
        ),
        name="attend",
    )(*operands)


def weigh_kernel(row, plan, queries, *refs):
    *key_refs, acc_in, stat_in, kept, acc, stat, keys_at, fine = refs
    columns, rows = acc.shape
    heads = columns // HD
    base = HEADER + row * ROW + 2
    acc[...] = acc_in[...]
    stat[...] = stat_in[...]

    def rows_of(d, h):
        return pl.ds(pl.multiple_of((d * heads + h) * STRETCH, STRETCH), STRETCH)

    def step(d, t, twice):
        start = t * STRETCH
        at = pl.ds(pl.multiple_of(start, STRETCH), STRETCH)
        lowest = jnp.ones((1, STRETCH), jnp.float32)
        scores = score(keys_at[:, head(0)[0]], queries[head(0)[1], at])
        for h in range(heads):
            _, _, _, refer, total = head(h)
            following = None
            if h + 1 < heads:
                following = score(keys_at[:, head(h + 1)[0]], queries[head(h + 1)[1], at])
            weights = jnp.exp2(scores - (stat[refer, at] - twice))
            kept[rows_of(d, h), at] = weights.astype(jnp.bfloat16)
            mass = jnp.sum(weights, axis=0, keepdims=True)
            fits = mass < GUARD
            stat[total, at] += jnp.where(fits, mass, 0.0)
            fit = jnp.where(fits, 1.0, 0.0)
            fine[pl.ds(8 * h, 1), :] = fit
            lowest = jnp.minimum(lowest, fit)
            scores = following

        @pl.when(jnp.min(lowest) < 0.5)
        def _():
            parts = STRETCH // HD
            lax.fori_loop(
                0, heads * parts, lambda i, c: (again(d, t, i // parts, i % parts * HD, twice), c)[1], 0
            )

    def again(d, t, h, w, twice):
        at = pl.ds(pl.multiple_of(t * STRETCH + w, HD), HD)
        cols, both, _, refer, total = head(h)
        scores = score(keys_at[:, cols], queries[both, at])
        before = stat[refer, at]
        peak = jnp.maximum(jnp.max(scores, axis=0, keepdims=True), before)
        miss = fine[pl.ds(pl.multiple_of(8 * h, 8), 1), pl.ds(pl.multiple_of(w, HD), HD)] < 0.5
        keep = jnp.where(miss, jnp.exp2(before - peak), 1.0)
        weights = jnp.exp2(scores - (peak - twice))
        mass = stat[total, at] * keep + jnp.where(miss, jnp.sum(weights, axis=0, keepdims=True), 0.0)
        acc[cols, at] = acc[cols, at] * keep
        stat[total, at] = mass
        stat[refer, at] = jnp.where(miss, peak, before)
        old = kept[rows_of(d, h), at].astype(jnp.float32)
        kept[rows_of(d, h), at] = jnp.where(miss, weights, old).astype(jnp.bfloat16)

        @pl.when((d > 0) & (plan[base + t] > 0))
        def _():
            earlier = kept[rows_of(0, h), at].astype(jnp.float32)
            kept[rows_of(0, h), at] = (earlier * keep).astype(jnp.bfloat16)

    def visit(d, c):
        @pl.when(plan[base + 2 * d] + plan[base + 2 * d + 1] > 0)
        def _():
            for number, ref in enumerate(key_refs):
                @pl.when(d == number)
                def _(ref=ref):
                    keys_at[...] = ref[...]

            def stretch(t, c):
                times = plan[base + 2 * d + t]

                @pl.when(times > 0)
                def _():
                    step(d, t, jnp.where(times > 1, 1.0, 0.0))

                return c

            lax.fori_loop(0, rows // STRETCH, stretch, 0)

        return c

    lax.fori_loop(0, len(key_refs), visit, 0)


def weigh(plan, row, queries, key_came, state):
    columns, rows = queries.shape[0] // 2, queries.shape[1]
    acc, stat = state
    heads = columns // HD
    keys = len(key_came) * STRETCH
    return pl.pallas_call(
        functools.partial(weigh_kernel, row),
        out_shape=[
            jax.ShapeDtypeStruct((heads * keys, rows), queries.dtype),
            jax.ShapeDtypeStruct(acc.shape, acc.dtype),
            jax.ShapeDtypeStruct(stat.shape, stat.dtype),
        ],
        in_specs=[SMEM] + [VMEM] * (3 + len(key_came)),
        out_specs=[VMEM] * 3,
        scratch_shapes=[
            pltpu.VMEM((STRETCH, columns), queries.dtype),
            pltpu.VMEM((8 * heads, STRETCH), jnp.float32),
        ],
        compiler_params=room(24),
        cost_estimate=pl.CostEstimate(
            flops=2 * rows * columns * keys, bytes_accessed=8 * rows * columns,
            transcendentals=rows * heads * keys,
        ),
        name="weigh",
    )(plan, queries, *key_came, acc, stat)


def finish_kernel(row, plan, kept, *refs):
    *value_refs, acc_in, stat, out, acc = refs
    columns, rows = acc.shape
    heads = columns // HD
    base = HEADER + row * ROW + 2
    acc[...] = acc_in[...]

    def stretch(t, c):
        at = pl.ds(pl.multiple_of(t * STRETCH, STRETCH), STRETCH)
        for d, values in enumerate(value_refs):
            @pl.when(plan[base + 2 * d + t] > 0)
            def _(d=d, values=values):
                for h in range(heads):
                    cols = pl.ds(h * HD, HD)
                    acc[cols, at] += jnp.dot(
                        values[cols, :], kept[pl.ds((d * heads + h) * STRETCH, STRETCH), at],
                        preferred_element_type=jnp.float32,
                    )

        return c

    lax.fori_loop(0, rows // STRETCH, stretch, 0)
    for h in range(heads):
        cols = pl.ds(h * HD, HD)
        for t in range(rows // TURN):
            at = pl.ds(t * TURN, TURN)
            share = 1.0 / stat[16 * h + 8 : 16 * h + 9, at]
            out[at, cols] = jnp.transpose((acc[cols, at] * share).astype(out.dtype))


def finish(plan, row, kept, value_came, state):
    acc, stat = state
    columns, rows = acc.shape
    return pl.pallas_call(
        functools.partial(finish_kernel, row),
        out_shape=jax.ShapeDtypeStruct((rows, columns), kept.dtype),
        in_specs=[SMEM] + [VMEM] * (3 + len(value_came)),
        out_specs=VMEM,
        scratch_shapes=[pltpu.VMEM(acc.shape, acc.dtype)],
        compiler_params=room(24),
        cost_estimate=pl.CostEstimate(
            flops=2 * columns * rows * STRETCH * len(value_came), bytes_accessed=8 * rows * columns, transcendentals=0
        ),
        name="finish",
    )(plan, kept, *value_came, acc, stat)


def own_blocks(keys, values):
    return [(keys, values, j * STRETCH, (1 + j, 2)) for j in range(STRETCH_DEV)]


def came_blocks(base, key_came, value_came):
    return [(key_came[d], value_came[d], 0, (base + 2 + 2 * d, 1)) for d in range(2)]


def send(down, up):
    last = lax.axis_size("seq") - 1
    from_above = lax.ppermute(down, "seq", [(i + 1, i) for i in range(last)])
    from_below = lax.ppermute(up, "seq", [(i, i + 1) for i in range(last)])
    return from_above, from_below


def exchange(rounds, plan, queries, keys, values, text_keys, text_values, key_first):
    key_here = send(*key_first)
    values, text_values, *value_first = turn_values(plan, values, text_values)
    queries = turn_queries(queries)
    value_first, queries = lax.optimization_barrier((value_first, queries))
    value_here = send(*value_first)
    state = attend_text(queries, text_keys, text_values)
    first_own, second_own = own_blocks(keys, values)
    key_came, value_came = ([], []), ([], [])

    def before(blocks):
        nonlocal state
        blocks, state = lax.optimization_barrier((blocks, state))
        return blocks

    for r in range(rounds - 1):
        key_here = before(key_here)
        for d in range(2):
            key_came[d].append(key_here[d])
        key_next = send(*before(choose(plan, r + 1, keys, 0, *key_came)))
        if r == 1:
            state = attend(plan, None, queries, [first_own], state)
        value_here = before(value_here)
        for d in range(2):
            value_came[d].append(value_here[d])
        came = came_blocks(HEADER + r * ROW, key_here, value_here)
        key_here, value_here = key_next, send(*before(choose(plan, r + 1, values, 1, *value_came)))
        blocks = came if r + 2 < rounds else [second_own] + came
        state = attend(plan, None, queries, blocks, state)
    kept, *state = weigh(plan, rounds - 1, queries, key_here, state)
    value_here, kept, state = lax.optimization_barrier((value_here, kept, state))
    return finish(plan, rounds - 1, kept, value_here, state)


def long_exchange(plan, queries, keys, values, text_keys, text_values, key_first):
    values, text_values, *value_first = turn_values(plan, values, text_values)
    queries = turn_queries(queries)
    state = attend_text(queries, text_keys, text_values)
    state = attend(plan, None, queries, own_blocks(keys, values), state)

    def body(carry):
        r, key_here, value_here, state = carry
        row = r.reshape(1)
        key_here = send(*choose(plan, row, keys, 0, [key_here[0]], [key_here[1]]))
        value_here = send(*choose(plan, row, values, 1, [value_here[0]], [value_here[1]]))
        state = attend(plan, row, queries, came_blocks(0, key_here, value_here), state)
        return (r + 1, key_here, value_here, state)

    carry = (jnp.int32(0), tuple(key_first), tuple(value_first), state)
    _, _, _, (acc, stat) = lax.while_loop(lambda c: c[0] < plan[5], body, carry)
    share = jnp.repeat(1.0 / stat[8::16], HD, axis=0)
    return jnp.transpose(acc * share).astype(queries.dtype)


def shards(
    queries, key_rows, value_rows, text_keys, text_values,
    shot_of_stretch, anchor_stretch, context_count, context_ids,
):
    groups = lax.axis_size("seq")
    tables = (shot_of_stretch, anchor_stretch, context_count, context_ids.T)
    plan, branch, key_down, key_up = make_plan(groups, tables, key_rows)
    branches = [functools.partial(exchange, rounds) for rounds in ROUNDS] + [long_exchange]
    return lax.switch(
        branch[0], branches, plan, queries, key_rows, value_rows, text_keys, text_values,
        (key_down, key_up),
    )


def solution(mesh):
    return jax.shard_map(
        shards,
        mesh=mesh,
        in_specs=(
            P(("rep", "seq"), "shot"),
            P(("rep", "seq"), "shot"),
            P(("rep", "seq"), "shot"),
            P("rep", "shot"),
            P("rep", "shot"),
            P("rep"),
            P("rep"),
            P("rep"),
            P("rep", None),
        ),
        out_specs=P(("rep", "seq"), "shot"),
        check_vma=False,
    )
```

```python
import functools
import math

import jax
import jax.numpy as jnp
from jax import lax
from jax.experimental import pallas as pl
from jax.experimental.pallas import tpu as pltpu
from jax.sharding import PartitionSpec as P

HD = 128
STRETCH = 512
STRETCH_DEV = 2
ROUNDS = (3, 4)
ROW = 8
HEADER = 8
TURN = 256
GUARD = 2.0 ** 100
ONES = 16
EXPONENT = HD ** (-0.5) * math.log2(math.e)
SMEM = pl.BlockSpec(memory_space=pltpu.SMEM)
VMEM = pl.BlockSpec(memory_space=pltpu.VMEM)


def room(mebibytes):
    return pltpu.CompilerParams(vmem_limit_bytes=mebibytes * 1024 * 1024)


def quick_plan(groups, shot, anchor, count, ids, keys, plan, targets):
    total = STRETCH_DEV * groups
    slots = ids.shape[0]
    me = lax.axis_index("seq")
    one = jnp.int32(1)

    def listed(c):
        live = count[c]
        yield one << anchor[shot[c]]
        for s in range(slots):
            yield jnp.where(s < live, one << ids[s, c], 0)

    need = []
    for g in range(groups):
        mask = jnp.int32(0)
        for c in range(STRETCH_DEV * g, STRETCH_DEV * (g + 1)):
            for entry in listed(c):
                mask = mask | entry
        need.append(mask)

    once, twice = [], []
    for q in range(STRETCH_DEV):
        c = STRETCH_DEV * me + q
        seen, again = one << c, jnp.int32(0)
        for entry in listed(c):
            again = again | (seen & entry)
            seen = seen | entry
        once.append(seen)
        twice.append(again)

    def times(q, stretch):
        return jnp.where((once[q] & stretch) != 0, 1, 0) + jnp.where((twice[q] & stretch) != 0, 1, 0)

    first_own = one << (STRETCH_DEV * me)
    second_own = first_own << 1
    for q in range(STRETCH_DEV):
        plan[1 + 2 * q] = times(q, first_own)
        plan[2 + 2 * q] = times(q, second_own)

    ways = []
    for d in range(2):
        order = list(range(groups))[:: 2 * d - 1]
        own = [((1 << STRETCH_DEV) - 1) << (STRETCH_DEV * g) for g in order]
        before = [sum(own[:k]) for k in range(groups)]
        beyond = _beyond(need, order, before)
        ways.append((own, beyond, [own[k] & beyond[k] for k in range(groups)]))

    rounds = jnp.int32(0)
    arrived = [[], []]
    for r in range(ROUNDS[-1]):
        pending = jnp.int32(0)
        for d in range(2):
            _, beyond, onward = ways[d]
            at = groups - 1 - me if d == 0 else me
            picks = []
            for k in range(groups - 1):
                pending = pending | onward[k]
                pick = onward[k] & beyond[groups - 2]
                for g in reversed(range(k, groups - 2)):
                    pick = jnp.where(pick != 0, pick, onward[k] & beyond[g])
                picks.append(pick & -pick)
            for k in range(groups - 1):
                onward[k] = onward[k] & ~picks[k]
            for k in range(1, groups - 1):
                onward[k] = onward[k] | (picks[k - 1] & beyond[k])
            sent, came = jnp.int32(0), jnp.int32(0)
            for k in range(groups - 1):
                sent = jnp.where(at == k, picks[k], sent)
                came = jnp.where(at == k + 1, picks[k], came)
            choice = jnp.where(sent == second_own, 1, 0)
            for i, earlier in enumerate(arrived[d]):
                choice = jnp.where((sent == earlier) & (sent != 0), STRETCH_DEV + i, choice)
            arrived[d].append(came)
            plan[HEADER + r * ROW + d] = choice
            for q in range(STRETCH_DEV):
                plan[HEADER + r * ROW + 2 + 2 * d + q] = times(q, came)
            if r == 0:
                start = pl.multiple_of(choice * STRETCH, STRETCH)
                targets[d][...] = keys[pl.ds(start, STRETCH), :]
        rounds = rounds + jnp.where(pending != 0, 1, 0)
    pending = jnp.int32(0)
    for _, _, onward in ways:
        for left in onward[: groups - 1]:
            pending = pending | left
    return rounds + jnp.where(pending != 0, 1, 0)


def _beyond(need, order, before):
    beyond = []
    for k in range(len(order)):
        mask = jnp.int32(0)
        held = before[k + 1] if k + 1 < len(order) else 0
        for g in order[k + 1 :]:
            mask = mask | need[g]
        beyond.append(mask & held)
    return beyond


def plan_kernel(
    groups, cap, shot, anchor, count, ids, keys,
    plan, branch, key_down, key_up, *scratch,
):
    def list_plan():
        return long_plan(groups, cap, shot, anchor, count, ids, plan, *scratch)

    if STRETCH_DEV * groups <= 16:
        rounds = quick_plan(groups, shot, anchor, count, ids, keys, plan, (key_down, key_up))
        plan[0] = rounds

        @pl.when(rounds > ROUNDS[-1])
        def _():
            list_plan()
    else:
        rounds = list_plan()
        for d, target in enumerate((key_down, key_up)):
            start = pl.multiple_of(plan[HEADER + d] * STRETCH, STRETCH)
            target[...] = keys[pl.ds(start, STRETCH), :]
    branch[0] = sum(jnp.where(rounds > length, 1, 0) for length in ROUNDS)


def long_plan(groups, cap, shot, anchor, count, ids, plan, dest, place, hold, stamp, times, best):
    total = STRETCH_DEV * groups
    slots = ids.shape[0]
    small = total <= 16
    bits = total.bit_length()
    me = lax.axis_index("seq")
    mine = (groups - 1 - me, me)

    def each(length, body):
        if small:
            for i in range(length):
                body(i)
        else:
            lax.fori_loop(0, length, lambda i, c: (body(i), c)[1], 0)

    def clear(e):
        g = e >> 1
        dest[e] = groups - 1 - g
        dest[total + e] = g
        times[e] = 0
        times[total + e] = 0

    each(total, clear)

    def stand(e):
        g = e >> 1
        for d, at in enumerate((groups - 1 - g, g)):
            place[d * total + e] = at
            hold[d * total + e] = e & 1
            stamp[d * total + e] = -1

    each(total, stand)

    def read(c):
        g = c >> 1

        def entry(e):
            dest[e] = jnp.maximum(dest[e], groups - 1 - g)
            dest[total + e] = jnp.maximum(dest[total + e], g)

        entry(anchor[shot[c]])
        live = count[c]
        for s in range(slots):
            entry(jnp.where(s < live, ids[s, c], c))

    each(total, read)

    for q in range(STRETCH_DEV):
        c = STRETCH_DEV * me + q

        def one(e, amount, q=q):
            times[q * total + e] = times[q * total + e] + amount

        one(c, 1)
        one(anchor[shot[c]], 1)
        live = count[c]
        for s in range(slots):
            alive = s < live
            one(jnp.where(alive, ids[s, c], c), jnp.where(alive, 1, 0))

    for q in range(STRETCH_DEV):
        for j in range(STRETCH_DEV):
            plan[1 + 2 * q + j] = times[q * total + STRETCH_DEV * me + j]
    for i in range(ROW * ROUNDS[-1]):
        plan[HEADER + i] = 0

    def remaining():
        return lax.fori_loop(
            0, 2 * total, lambda e, s: s + dest[e] - place[e], jnp.int32(0), unroll=small
        )

    def a_round(r, transit):
        moves = jnp.int32(0)
        for d in range(2):
            base = d * total
            for k in range(groups) if small else ():
                best[k] = -1
            if not small:
                each(groups, lambda k: best.__setitem__(k, jnp.int32(-1)))

            def rank(e, base=base):
                at = place[base + e]
                to = dest[base + e]
                key = (to << bits) | e
                if transit:
                    key = jnp.where(stamp[base + e] == r, key + (groups << bits), key)
                best[at] = jnp.maximum(best[at], jnp.where(to > at, key, -1))

            each(total, rank)
            sent = best[mine[d]]
            mask = (1 << bits) - 1
            plan[HEADER + r * ROW + d] = jnp.where(sent < 0, 0, hold[base + (jnp.maximum(sent, 0) & mask)])
            came = jnp.where(mine[d] > 0, best[jnp.maximum(mine[d] - 1, 0)], -1)
            come = jnp.maximum(came, 0) & mask
            for q in range(STRETCH_DEV):
                plan[HEADER + r * ROW + 2 + 2 * d + q] = jnp.where(came < 0, 0, times[q * total + come])

            @pl.when(came >= 0)
            def _(come=come, base=base):
                hold[base + come] = 2 + r

            def move(k, base=base):
                key = best[k]

                @pl.when(key >= 0)
                def _():
                    e = key & mask
                    place[base + e] = k + 1
                    stamp[base + e] = r + 1

                return jnp.where(key >= 0, 1, 0)

            if small:
                for k in range(groups - 1):
                    moves += move(k)
            else:
                moves += lax.fori_loop(0, groups - 1, lambda k, s: s + move(k), jnp.int32(0))
        return moves

    hops = remaining()

    def go_on(carry):
        return (carry[1] > 0) & (carry[0] < cap)

    rounds, _ = lax.while_loop(
        go_on, lambda c: (c[0] + 1, c[1] - a_round(c[0], False)), (jnp.int32(0), hops)
    )
    plan[0] = rounds

    @pl.when(rounds > ROUNDS[-1])
    def _():
        each(total, stand)
        again, _ = lax.while_loop(
            go_on, lambda c: (c[0] + 1, c[1] - a_round(c[0], True)), (jnp.int32(0), hops)
        )
        plan[5] = again

    return rounds


def make_plan(groups, tables, keys):
    total = STRETCH_DEV * groups
    cap = 2 * groups + 16
    block = jax.ShapeDtypeStruct((STRETCH, keys.shape[1]), keys.dtype)
    return pl.pallas_call(
        functools.partial(plan_kernel, groups, cap),
        out_shape=[
            jax.ShapeDtypeStruct((HEADER + cap * ROW,), jnp.int32),
            jax.ShapeDtypeStruct((1,), jnp.int32),
            block,
            block,
        ],
        in_specs=[SMEM] * 4 + [VMEM],
        out_specs=[SMEM] * 2 + [VMEM] * 2,
        scratch_shapes=[pltpu.SMEM((2 * total,), jnp.int32) for _ in range(5)]
        + [pltpu.SMEM((groups,), jnp.int32)],
        name="plan",
    )(*tables, keys)


def choose_kernel(row, arrivals, axis, plan, *refs):
    if row is None:
        at, own, *refs = refs
        base = HEADER + at[0] * ROW
    else:
        own, *refs = refs
        base = HEADER + row * ROW
    came, outs = refs[: 2 * arrivals], refs[2 * arrivals :]
    for d in range(2):
        choice = plan[base + d]

        @pl.when(choice < STRETCH_DEV)
        def _(d=d, choice=choice):
            part = pl.ds(pl.multiple_of(choice * STRETCH, STRETCH), STRETCH)
            outs[d][...] = own[part, :] if axis == 0 else own[:, part]

        for i in range(arrivals):
            picked = choice == STRETCH_DEV + i if row is not None else choice >= STRETCH_DEV

            @pl.when(picked)
            def _(d=d, i=i):
                outs[d][...] = came[d * arrivals + i][...]


def choose(plan, row, own, axis, down, up):
    static = isinstance(row, int)
    shape = list(own.shape)
    shape[axis] = STRETCH
    block = jax.ShapeDtypeStruct(tuple(shape), own.dtype)
    return pl.pallas_call(
        functools.partial(choose_kernel, row if static else None, len(down), axis),
        out_shape=[block] * 2,
        in_specs=[SMEM] + ([] if static else [SMEM]) + [VMEM] * (1 + 2 * len(down)),
        out_specs=[VMEM] * 2,
        compiler_params=room(8),
        cost_estimate=pl.CostEstimate(flops=0, bytes_accessed=8 * block.size, transcendentals=0),
        name="choose",
    )(plan, *(() if static else (row,)), own, *down, *up)


def score(keys, queries):
    return jnp.dot(jnp.concatenate([keys, keys], axis=1), queries, preferred_element_type=jnp.float32)


def turn_queries_kernel(queries, split):
    for h in range(queries.shape[1] // HD):
        cols = pl.ds(h * HD, HD)
        for t in range(queries.shape[0] // TURN):
            at = pl.ds(t * TURN, TURN)
            turned = jnp.transpose(queries[at, cols].astype(jnp.float32) * EXPONENT)
            high = turned.astype(jnp.bfloat16)
            split[pl.ds(2 * h * HD, HD), at] = high
            split[pl.ds((2 * h + 1) * HD, HD), at] = (turned - high.astype(jnp.float32)).astype(jnp.bfloat16)


def turn_queries(queries):
    rows, columns = queries.shape
    return pl.pallas_call(
        turn_queries_kernel,
        out_shape=jax.ShapeDtypeStruct((2 * columns, rows), queries.dtype),
        in_specs=[VMEM],
        out_specs=VMEM,
        compiler_params=room(10),
        name="turn_queries",
    )(queries)


def text_kernel(queries, text_keys, text_values, acc, stat):
    ones = jnp.ones((ONES, text_keys.shape[0]), jnp.bfloat16)

    def stretch(t, c):
        at = pl.ds(pl.multiple_of(t * STRETCH, STRETCH), STRETCH)
        for h in range(text_keys.shape[1] // HD):
            cols = pl.ds(h * HD, HD)
            scores = score(text_keys[:, cols], queries[pl.ds(2 * h * HD, 2 * HD), at])
            peak = jnp.max(scores, axis=0, keepdims=True)
            both = jnp.dot(
                jnp.concatenate([text_values[cols, :], ones], axis=0),
                jnp.exp2(scores - peak).astype(jnp.bfloat16), preferred_element_type=jnp.float32,
            )
            acc[cols, at] = both[:HD]
            stat[16 * h : 16 * h + 1, at] = peak
            stat[16 * h + 8 : 16 * h + 9, at] = both[HD : HD + 1]
        return c

    lax.fori_loop(0, queries.shape[1] // STRETCH, stretch, 0)


def attend_text(queries, text_keys, text_values):
    columns, rows = queries.shape[0] // 2, queries.shape[1]
    return pl.pallas_call(
        text_kernel,
        out_shape=[
            jax.ShapeDtypeStruct((columns, rows), jnp.float32),
            jax.ShapeDtypeStruct((16 * (columns // HD), rows), jnp.float32),
        ],
        in_specs=[VMEM] * 3,
        out_specs=[VMEM] * 2,
        compiler_params=room(16),
        name="attend_text",
    )(queries, text_keys, text_values)


def turn_values_kernel(plan, values, text_values, values_out, text_out, down, up):
    for h in range(values.shape[1] // HD):
        cols = pl.ds(h * HD, HD)
        for source, target in ((values, values_out), (text_values, text_out)):
            for t in range(source.shape[0] // TURN):
                at = pl.ds(t * TURN, TURN)
                target[cols, at] = jnp.transpose(source[at, cols])
    for d, target in enumerate((down, up)):
        start = pl.multiple_of(plan[HEADER + d] * STRETCH, STRETCH)
        target[...] = values_out[:, pl.ds(start, STRETCH)]


def turn_values(plan, values, text_values):
    rows, columns = values.shape
    outs = [(columns, rows), (columns, text_values.shape[0]), (columns, STRETCH), (columns, STRETCH)]
    return pl.pallas_call(
        turn_values_kernel,
        out_shape=[jax.ShapeDtypeStruct(shape, values.dtype) for shape in outs],
        in_specs=[SMEM, VMEM, VMEM],
        out_specs=[VMEM] * 4,
        compiler_params=room(10),
        name="turn_values",
    )(plan, values, text_values)


def head(h):
    def part(start, size, by):
        return pl.ds(start if isinstance(h, int) else pl.multiple_of(start, by), size)

    return (
        part(h * HD, HD, HD), part(2 * h * HD, 2 * HD, 2 * HD), part(h * (HD + ONES), HD + ONES, ONES),
        part(16 * h, 1, 8), part(16 * h + 8, 1, 8),
    )


def attend_kernel(blocks, rowed, *refs):
    refs = list(refs)
    plan = refs.pop(0)
    base = HEADER + refs.pop(0)[0] * ROW if rowed else 0
    queries = refs.pop(0)
    block_refs = [(refs.pop(0), refs.pop(0)) for _ in blocks]
    acc_in, stat_in, acc, stat, keys_at, values_at, fine = refs
    rows = queries.shape[1]
    heads = queries.shape[0] // (2 * HD)
    wide = HD + ONES

    acc[...] = acc_in[...]
    stat[...] = stat_in[...]
    for h in range(heads):
        values_at[pl.ds(h * wide + HD, ONES), :] = jnp.ones((ONES, STRETCH), jnp.bfloat16)

    def step(start, twice):
        at = pl.ds(pl.multiple_of(start, STRETCH), STRETCH)

        lowest = jnp.ones((1, STRETCH), jnp.float32)
        scores = score(keys_at[:, head(0)[0]], queries[head(0)[1], at])
        for h in range(heads):
            cols, _, mixed, refer, total = head(h)
            following = None
            if h + 1 < heads:
                following = score(keys_at[:, head(h + 1)[0]], queries[head(h + 1)[1], at])
            weights = jnp.exp2(scores - (stat[refer, at] - twice)).astype(jnp.bfloat16)
            product = jnp.dot(values_at[mixed, :], weights, preferred_element_type=jnp.float32)
            mass = product[HD : HD + 1]
            fits = mass < GUARD
            acc[cols, at] = jnp.where(fits, acc[cols, at] + product[:HD], acc[cols, at])
            stat[total, at] += jnp.where(fits, mass, 0.0)
            fit = jnp.where(fits, 1.0, 0.0)
            fine[pl.ds(8 * h, 1), :] = fit
            lowest = jnp.minimum(lowest, fit)
            scores = following

        @pl.when(jnp.min(lowest) < 0.5)
        def _():
            parts = STRETCH // HD
            lax.fori_loop(
                0, heads * parts, lambda i, c: (again(start, i // parts, i % parts * HD, twice), c)[1], 0
            )

    def again(start, h, w, twice):
        at = pl.ds(pl.multiple_of(start + w, HD), HD)
        cols, both, mixed, refer, total = head(h)
        scores = score(keys_at[:, cols], queries[both, at])
        before = stat[refer, at]
        peak = jnp.maximum(jnp.max(scores, axis=0, keepdims=True), before)
        keep = jnp.exp2(before - peak)
        weights = jnp.exp2(scores - (peak - twice)).astype(jnp.bfloat16)
        product = jnp.dot(values_at[mixed, :], weights, preferred_element_type=jnp.float32)
        miss = fine[pl.ds(pl.multiple_of(8 * h, 8), 1), pl.ds(pl.multiple_of(w, HD), HD)] < 0.5
        mass = product[HD : HD + 1] + stat[total, at] * keep
        acc[cols, at] = jnp.where(miss, product[:HD] + acc[cols, at] * keep, acc[cols, at])
        stat[total, at] = jnp.where(miss, mass, stat[total, at])
        stat[refer, at] = jnp.where(miss, peak, before)

    def visit(b, c):
        place, stride = jnp.int32(0), jnp.int32(0)
        for number, (_, (first, second)) in enumerate(blocks):
            place = jnp.where(b == number, first, place)
            stride = jnp.where(b == number, second, stride)
        place = base + place

        @pl.when(plan[place] + plan[place + stride] > 0)
        def _():
            for number, (start, _) in enumerate(blocks):
                @pl.when(b == number)
                def _(start=start, number=number):
                    part = pl.ds(start, STRETCH)
                    keys_at[...] = block_refs[number][0][part, :]
                    for h in range(heads):
                        values_at[pl.ds(h * wide, HD), :] = block_refs[number][1][pl.ds(h * HD, HD), part]

            def stretch(t, c):
                times = plan[place + t * stride]

                @pl.when(times > 0)
                def _():
                    step(t * STRETCH, jnp.where(times > 1, 1.0, 0.0))

                return c

            lax.fori_loop(0, rows // STRETCH, stretch, 0)

        return c

    lax.fori_loop(0, len(blocks), visit, 0)


def attend(plan, row, queries, blocks, state):
    columns, rows = queries.shape[0] // 2, queries.shape[1]
    acc = jax.ShapeDtypeStruct((columns, rows), jnp.float32)
    stat = jax.ShapeDtypeStruct((16 * (columns // HD), rows), jnp.float32)
    scratch = [
        pltpu.VMEM((STRETCH, columns), queries.dtype),
        pltpu.VMEM((columns // HD * (HD + ONES), STRETCH), queries.dtype),
        pltpu.VMEM((8 * (columns // HD), STRETCH), jnp.float32),
    ]
    operands = [plan] + ([] if row is None else [row])
    smem = len(operands)
    operands.append(queries)
    for b in blocks:
        operands += [b[0], b[1]]
    operands += list(state)
    keys = len(blocks) * STRETCH
    return pl.pallas_call(
        functools.partial(attend_kernel, [tuple(b[2:]) for b in blocks], row is not None),
        out_shape=[acc, stat],
        in_specs=[SMEM] * smem + [VMEM] * (len(operands) - smem),
        out_specs=[VMEM] * 2,
        scratch_shapes=scratch,
        compiler_params=room(24),
        cost_estimate=pl.CostEstimate(
            flops=4 * rows * columns * keys, bytes_accessed=8 * rows * columns,
            transcendentals=rows * columns // HD * keys,
        ),
        name="attend",
    )(*operands)


def weigh_kernel(row, plan, queries, *refs):
    *key_refs, acc_in, stat_in, kept, acc, stat, keys_at, fine = refs
    columns, rows = acc.shape
    heads = columns // HD
    base = HEADER + row * ROW + 2
    acc[...] = acc_in[...]
    stat[...] = stat_in[...]

    def rows_of(d, h):
        return pl.ds(pl.multiple_of((d * heads + h) * STRETCH, STRETCH), STRETCH)

    def step(d, t, twice):
        start = t * STRETCH
        at = pl.ds(pl.multiple_of(start, STRETCH), STRETCH)
        lowest = jnp.ones((1, STRETCH), jnp.float32)
        scores = score(keys_at[:, head(0)[0]], queries[head(0)[1], at])
        for h in range(heads):
            _, _, _, refer, total = head(h)
            following = None
            if h + 1 < heads:
                following = score(keys_at[:, head(h + 1)[0]], queries[head(h + 1)[1], at])
            weights = jnp.exp2(scores - (stat[refer, at] - twice))
            kept[rows_of(d, h), at] = weights.astype(jnp.bfloat16)
            mass = jnp.sum(weights, axis=0, keepdims=True)
            fits = mass < GUARD
            stat[total, at] += jnp.where(fits, mass, 0.0)
            fit = jnp.where(fits, 1.0, 0.0)
            fine[pl.ds(8 * h, 1), :] = fit
            lowest = jnp.minimum(lowest, fit)
            scores = following

        @pl.when(jnp.min(lowest) < 0.5)
        def _():
            parts = STRETCH // HD
            lax.fori_loop(
                0, heads * parts, lambda i, c: (again(d, t, i // parts, i % parts * HD, twice), c)[1], 0
            )

    def again(d, t, h, w, twice):
        at = pl.ds(pl.multiple_of(t * STRETCH + w, HD), HD)
        cols, both, _, refer, total = head(h)
        scores = score(keys_at[:, cols], queries[both, at])
        before = stat[refer, at]
        peak = jnp.maximum(jnp.max(scores, axis=0, keepdims=True), before)
        miss = fine[pl.ds(pl.multiple_of(8 * h, 8), 1), pl.ds(pl.multiple_of(w, HD), HD)] < 0.5
        keep = jnp.where(miss, jnp.exp2(before - peak), 1.0)
        weights = jnp.exp2(scores - (peak - twice))
        mass = stat[total, at] * keep + jnp.where(miss, jnp.sum(weights, axis=0, keepdims=True), 0.0)
        acc[cols, at] = acc[cols, at] * keep
        stat[total, at] = mass
        stat[refer, at] = jnp.where(miss, peak, before)
        old = kept[rows_of(d, h), at].astype(jnp.float32)
        kept[rows_of(d, h), at] = jnp.where(miss, weights, old).astype(jnp.bfloat16)

        @pl.when((d > 0) & (plan[base + t] > 0))
        def _():
            earlier = kept[rows_of(0, h), at].astype(jnp.float32)
            kept[rows_of(0, h), at] = (earlier * keep).astype(jnp.bfloat16)

    def visit(d, c):
        @pl.when(plan[base + 2 * d] + plan[base + 2 * d + 1] > 0)
        def _():
            for number, ref in enumerate(key_refs):
                @pl.when(d == number)
                def _(ref=ref):
                    keys_at[...] = ref[...]

            def stretch(t, c):
                times = plan[base + 2 * d + t]

                @pl.when(times > 0)
                def _():
                    step(d, t, jnp.where(times > 1, 1.0, 0.0))

                return c

            lax.fori_loop(0, rows // STRETCH, stretch, 0)

        return c

    lax.fori_loop(0, len(key_refs), visit, 0)


def weigh(plan, row, queries, key_came, state):
    columns, rows = queries.shape[0] // 2, queries.shape[1]
    acc, stat = state
    heads = columns // HD
    keys = len(key_came) * STRETCH
    return pl.pallas_call(
        functools.partial(weigh_kernel, row),
        out_shape=[
            jax.ShapeDtypeStruct((heads * keys, rows), queries.dtype),
            jax.ShapeDtypeStruct(acc.shape, acc.dtype),
            jax.ShapeDtypeStruct(stat.shape, stat.dtype),
        ],
        in_specs=[SMEM] + [VMEM] * (3 + len(key_came)),
        out_specs=[VMEM] * 3,
        scratch_shapes=[
            pltpu.VMEM((STRETCH, columns), queries.dtype),
            pltpu.VMEM((8 * heads, STRETCH), jnp.float32),
        ],
        compiler_params=room(24),
        cost_estimate=pl.CostEstimate(
            flops=2 * rows * columns * keys, bytes_accessed=8 * rows * columns,
            transcendentals=rows * heads * keys,
        ),
        name="weigh",
    )(plan, queries, *key_came, acc, stat)


def finish_kernel(row, plan, kept, *refs):
    *value_refs, acc_in, stat, out, acc = refs
    columns, rows = acc.shape
    heads = columns // HD
    base = HEADER + row * ROW + 2
    acc[...] = acc_in[...]

    def stretch(t, c):
        at = pl.ds(pl.multiple_of(t * STRETCH, STRETCH), STRETCH)
        for d, values in enumerate(value_refs):
            @pl.when(plan[base + 2 * d + t] > 0)
            def _(d=d, values=values):
                for h in range(heads):
                    cols = pl.ds(h * HD, HD)
                    acc[cols, at] += jnp.dot(
                        values[cols, :], kept[pl.ds((d * heads + h) * STRETCH, STRETCH), at],
                        preferred_element_type=jnp.float32,
                    )

        return c

    lax.fori_loop(0, rows // STRETCH, stretch, 0)
    for h in range(heads):
        cols = pl.ds(h * HD, HD)
        for t in range(rows // TURN):
            at = pl.ds(t * TURN, TURN)
            share = 1.0 / stat[16 * h + 8 : 16 * h + 9, at]
            out[at, cols] = jnp.transpose((acc[cols, at] * share).astype(out.dtype))


def finish(plan, row, kept, value_came, state):
    acc, stat = state
    columns, rows = acc.shape
    return pl.pallas_call(
        functools.partial(finish_kernel, row),
        out_shape=jax.ShapeDtypeStruct((rows, columns), kept.dtype),
        in_specs=[SMEM] + [VMEM] * (3 + len(value_came)),
        out_specs=VMEM,
        scratch_shapes=[pltpu.VMEM(acc.shape, acc.dtype)],
        compiler_params=room(24),
        cost_estimate=pl.CostEstimate(
            flops=2 * columns * rows * STRETCH * len(value_came), bytes_accessed=8 * rows * columns, transcendentals=0
        ),
        name="finish",
    )(plan, kept, *value_came, acc, stat)


def own_blocks(keys, values):
    return [(keys, values, j * STRETCH, (1 + j, 2)) for j in range(STRETCH_DEV)]


def came_blocks(base, key_came, value_came):
    return [(key_came[d], value_came[d], 0, (base + 2 + 2 * d, 1)) for d in range(2)]


def send(down, up):
    last = lax.axis_size("seq") - 1
    from_above = lax.ppermute(down, "seq", [(i + 1, i) for i in range(last)])
    from_below = lax.ppermute(up, "seq", [(i, i + 1) for i in range(last)])
    return from_above, from_below


def exchange(rounds, plan, queries, keys, values, text_keys, text_values, key_first):
    key_here = send(*key_first)
    values, text_values, *value_first = turn_values(plan, values, text_values)
    value_here = send(*value_first)
    value_first, queries = lax.optimization_barrier((value_first, queries))
    queries = turn_queries(queries)
    state = attend_text(queries, text_keys, text_values)
    first_own, second_own = own_blocks(keys, values)
    key_came, value_came = ([], []), ([], [])

    def before(blocks):
        nonlocal state
        blocks, state = lax.optimization_barrier((blocks, state))
        return blocks

    for r in range(rounds - 1):
        key_here = before(key_here)
        for d in range(2):
            key_came[d].append(key_here[d])
        key_next = send(*before(choose(plan, r + 1, keys, 0, *key_came)))
        if r == 1:
            state = attend(plan, None, queries, [first_own], state)
        value_here = before(value_here)
        for d in range(2):
            value_came[d].append(value_here[d])
        came = came_blocks(HEADER + r * ROW, key_here, value_here)
        key_here, value_here = key_next, send(*before(choose(plan, r + 1, values, 1, *value_came)))
        blocks = came if r + 2 < rounds else [second_own] + came
        state = attend(plan, None, queries, blocks, state)
    kept, *state = weigh(plan, rounds - 1, queries, key_here, state)
    value_here, kept, state = lax.optimization_barrier((value_here, kept, state))
    return finish(plan, rounds - 1, kept, value_here, state)


def long_exchange(plan, queries, keys, values, text_keys, text_values, key_first):
    values, text_values, *value_first = turn_values(plan, values, text_values)
    queries = turn_queries(queries)
    state = attend_text(queries, text_keys, text_values)
    state = attend(plan, None, queries, own_blocks(keys, values), state)

    def body(carry):
        r, key_here, value_here, state = carry
        row = r.reshape(1)
        key_here = send(*choose(plan, row, keys, 0, [key_here[0]], [key_here[1]]))
        value_here = send(*choose(plan, row, values, 1, [value_here[0]], [value_here[1]]))
        state = attend(plan, row, queries, came_blocks(0, key_here, value_here), state)
        return (r + 1, key_here, value_here, state)

    carry = (jnp.int32(0), tuple(key_first), tuple(value_first), state)
    _, _, _, (acc, stat) = lax.while_loop(lambda c: c[0] < plan[5], body, carry)
    share = jnp.repeat(1.0 / stat[8::16], HD, axis=0)
    return jnp.transpose(acc * share).astype(queries.dtype)


def shards(
    queries, key_rows, value_rows, text_keys, text_values,
    shot_of_stretch, anchor_stretch, context_count, context_ids,
):
    groups = lax.axis_size("seq")
    tables = (shot_of_stretch, anchor_stretch, context_count, context_ids.T)
    plan, branch, key_down, key_up = make_plan(groups, tables, key_rows)
    branches = [functools.partial(exchange, rounds) for rounds in ROUNDS] + [long_exchange]
    return lax.switch(
        branch[0], branches, plan, queries, key_rows, value_rows, text_keys, text_values,
        (key_down, key_up),
    )


def solution(mesh):
    return jax.shard_map(
        shards,
        mesh=mesh,
        in_specs=(
            P(("rep", "seq"), "shot"),
            P(("rep", "seq"), "shot"),
            P(("rep", "seq"), "shot"),
            P("rep", "shot"),
            P("rep", "shot"),
            P("rep"),
            P("rep"),
            P("rep"),
            P("rep", None),
        ),
        out_specs=P(("rep", "seq"), "shot"),
        check_vma=False,
    )
```

```python
import functools
import math

import jax
import jax.numpy as jnp
from jax import lax
from jax.experimental import pallas as pl
from jax.experimental.pallas import tpu as pltpu
from jax.sharding import PartitionSpec as P

HD = 128
STRETCH = 512
STRETCH_DEV = 2
ROUNDS = (3, 4)
ROW = 8
HEADER = 8
TURN = 256
GUARD = 2.0 ** 100
ONES = 16
EXPONENT = HD ** (-0.5) * math.log2(math.e)
SMEM = pl.BlockSpec(memory_space=pltpu.SMEM)
VMEM = pl.BlockSpec(memory_space=pltpu.VMEM)


def room(mebibytes):
    return pltpu.CompilerParams(vmem_limit_bytes=mebibytes * 1024 * 1024)


def quick_plan(groups, shot, anchor, count, ids, keys, plan, targets):
    total = STRETCH_DEV * groups
    slots = ids.shape[0]
    me = lax.axis_index("seq")
    one = jnp.int32(1)

    def listed(c):
        live = count[c]
        yield one << anchor[shot[c]]
        for s in range(slots):
            yield jnp.where(s < live, one << ids[s, c], 0)

    need = []
    for g in range(groups):
        mask = jnp.int32(0)
        for c in range(STRETCH_DEV * g, STRETCH_DEV * (g + 1)):
            for entry in listed(c):
                mask = mask | entry
        need.append(mask)

    once, twice = [], []
    for q in range(STRETCH_DEV):
        c = STRETCH_DEV * me + q
        seen, again = one << c, jnp.int32(0)
        for entry in listed(c):
            again = again | (seen & entry)
            seen = seen | entry
        once.append(seen)
        twice.append(again)

    def times(q, stretch):
        return jnp.where((once[q] & stretch) != 0, 1, 0) + jnp.where((twice[q] & stretch) != 0, 1, 0)

    first_own = one << (STRETCH_DEV * me)
    second_own = first_own << 1
    for q in range(STRETCH_DEV):
        plan[1 + 2 * q] = times(q, first_own)
        plan[2 + 2 * q] = times(q, second_own)

    ways = []
    for d in range(2):
        order = list(range(groups))[:: 2 * d - 1]
        own = [((1 << STRETCH_DEV) - 1) << (STRETCH_DEV * g) for g in order]
        before = [sum(own[:k]) for k in range(groups)]
        beyond = _beyond(need, order, before)
        ways.append((own, beyond, [own[k] & beyond[k] for k in range(groups)]))

    rounds = jnp.int32(0)
    arrived = [[], []]
    for r in range(ROUNDS[-1]):
        pending = jnp.int32(0)
        for d in range(2):
            _, beyond, onward = ways[d]
            at = groups - 1 - me if d == 0 else me
            picks = []
            for k in range(groups - 1):
                pending = pending | onward[k]
                pick = onward[k] & beyond[groups - 2]
                for g in reversed(range(k, groups - 2)):
                    pick = jnp.where(pick != 0, pick, onward[k] & beyond[g])
                picks.append(pick & -pick)
            for k in range(groups - 1):
                onward[k] = onward[k] & ~picks[k]
            for k in range(1, groups - 1):
                onward[k] = onward[k] | (picks[k - 1] & beyond[k])
            sent, came = jnp.int32(0), jnp.int32(0)
            for k in range(groups - 1):
                sent = jnp.where(at == k, picks[k], sent)
                came = jnp.where(at == k + 1, picks[k], came)
            choice = jnp.where(sent == second_own, 1, 0)
            for i, earlier in enumerate(arrived[d]):
                choice = jnp.where((sent == earlier) & (sent != 0), STRETCH_DEV + i, choice)
            arrived[d].append(came)
            plan[HEADER + r * ROW + d] = choice
            for q in range(STRETCH_DEV):
                plan[HEADER + r * ROW + 2 + 2 * d + q] = times(q, came)
            if r == 0:
                start = pl.multiple_of(choice * STRETCH, STRETCH)
                targets[d][...] = keys[pl.ds(start, STRETCH), :]
        rounds = rounds + jnp.where(pending != 0, 1, 0)
    pending = jnp.int32(0)
    for _, _, onward in ways:
        for left in onward[: groups - 1]:
            pending = pending | left
    return rounds + jnp.where(pending != 0, 1, 0)


def _beyond(need, order, before):
    beyond = []
    for k in range(len(order)):
        mask = jnp.int32(0)
        held = before[k + 1] if k + 1 < len(order) else 0
        for g in order[k + 1 :]:
            mask = mask | need[g]
        beyond.append(mask & held)
    return beyond


def plan_kernel(
    groups, cap, shot, anchor, count, ids, keys,
    plan, branch, key_down, key_up, *scratch,
):
    def list_plan():
        return long_plan(groups, cap, shot, anchor, count, ids, plan, *scratch)

    if STRETCH_DEV * groups <= 16:
        rounds = quick_plan(groups, shot, anchor, count, ids, keys, plan, (key_down, key_up))
        plan[0] = rounds

        @pl.when(rounds > ROUNDS[-1])
        def _():
            list_plan()
    else:
        rounds = list_plan()
        for d, target in enumerate((key_down, key_up)):
            start = pl.multiple_of(plan[HEADER + d] * STRETCH, STRETCH)
            target[...] = keys[pl.ds(start, STRETCH), :]
    branch[0] = sum(jnp.where(rounds > length, 1, 0) for length in ROUNDS)


def long_plan(groups, cap, shot, anchor, count, ids, plan, dest, place, hold, stamp, times, best):
    total = STRETCH_DEV * groups
    slots = ids.shape[0]
    small = total <= 16
    bits = total.bit_length()
    me = lax.axis_index("seq")
    mine = (groups - 1 - me, me)

    def each(length, body):
        if small:
            for i in range(length):
                body(i)
        else:
            lax.fori_loop(0, length, lambda i, c: (body(i), c)[1], 0)

    def clear(e):
        g = e >> 1
        dest[e] = groups - 1 - g
        dest[total + e] = g
        times[e] = 0
        times[total + e] = 0

    each(total, clear)

    def stand(e):
        g = e >> 1
        for d, at in enumerate((groups - 1 - g, g)):
            place[d * total + e] = at
            hold[d * total + e] = e & 1
            stamp[d * total + e] = -1

    each(total, stand)

    def read(c):
        g = c >> 1

        def entry(e):
            dest[e] = jnp.maximum(dest[e], groups - 1 - g)
            dest[total + e] = jnp.maximum(dest[total + e], g)

        entry(anchor[shot[c]])
        live = count[c]
        for s in range(slots):
            entry(jnp.where(s < live, ids[s, c], c))

    each(total, read)

    for q in range(STRETCH_DEV):
        c = STRETCH_DEV * me + q

        def one(e, amount, q=q):
            times[q * total + e] = times[q * total + e] + amount

        one(c, 1)
        one(anchor[shot[c]], 1)
        live = count[c]
        for s in range(slots):
            alive = s < live
            one(jnp.where(alive, ids[s, c], c), jnp.where(alive, 1, 0))

    for q in range(STRETCH_DEV):
        for j in range(STRETCH_DEV):
            plan[1 + 2 * q + j] = times[q * total + STRETCH_DEV * me + j]
    for i in range(ROW * ROUNDS[-1]):
        plan[HEADER + i] = 0

    def remaining():
        return lax.fori_loop(
            0, 2 * total, lambda e, s: s + dest[e] - place[e], jnp.int32(0), unroll=small
        )

    def a_round(r, transit):
        moves = jnp.int32(0)
        for d in range(2):
            base = d * total
            for k in range(groups) if small else ():
                best[k] = -1
            if not small:
                each(groups, lambda k: best.__setitem__(k, jnp.int32(-1)))

            def rank(e, base=base):
                at = place[base + e]
                to = dest[base + e]
                key = (to << bits) | e
                if transit:
                    key = jnp.where(stamp[base + e] == r, key + (groups << bits), key)
                best[at] = jnp.maximum(best[at], jnp.where(to > at, key, -1))

            each(total, rank)
            sent = best[mine[d]]
            mask = (1 << bits) - 1
            plan[HEADER + r * ROW + d] = jnp.where(sent < 0, 0, hold[base + (jnp.maximum(sent, 0) & mask)])
            came = jnp.where(mine[d] > 0, best[jnp.maximum(mine[d] - 1, 0)], -1)
            come = jnp.maximum(came, 0) & mask
            for q in range(STRETCH_DEV):
                plan[HEADER + r * ROW + 2 + 2 * d + q] = jnp.where(came < 0, 0, times[q * total + come])

            @pl.when(came >= 0)
            def _(come=come, base=base):
                hold[base + come] = 2 + r

            def move(k, base=base):
                key = best[k]

                @pl.when(key >= 0)
                def _():
                    e = key & mask
                    place[base + e] = k + 1
                    stamp[base + e] = r + 1

                return jnp.where(key >= 0, 1, 0)

            if small:
                for k in range(groups - 1):
                    moves += move(k)
            else:
                moves += lax.fori_loop(0, groups - 1, lambda k, s: s + move(k), jnp.int32(0))
        return moves

    hops = remaining()

    def go_on(carry):
        return (carry[1] > 0) & (carry[0] < cap)

    rounds, _ = lax.while_loop(
        go_on, lambda c: (c[0] + 1, c[1] - a_round(c[0], False)), (jnp.int32(0), hops)
    )
    plan[0] = rounds

    @pl.when(rounds > ROUNDS[-1])
    def _():
        each(total, stand)
        again, _ = lax.while_loop(
            go_on, lambda c: (c[0] + 1, c[1] - a_round(c[0], True)), (jnp.int32(0), hops)
        )
        plan[5] = again

    return rounds


def make_plan(groups, tables, keys):
    total = STRETCH_DEV * groups
    cap = 2 * groups + 16
    block = jax.ShapeDtypeStruct((STRETCH, keys.shape[1]), keys.dtype)
    return pl.pallas_call(
        functools.partial(plan_kernel, groups, cap),
        out_shape=[
            jax.ShapeDtypeStruct((HEADER + cap * ROW,), jnp.int32),
            jax.ShapeDtypeStruct((1,), jnp.int32),
            block,
            block,
        ],
        in_specs=[SMEM] * 4 + [VMEM],
        out_specs=[SMEM] * 2 + [VMEM] * 2,
        scratch_shapes=[pltpu.SMEM((2 * total,), jnp.int32) for _ in range(5)]
        + [pltpu.SMEM((groups,), jnp.int32)],
        name="plan",
    )(*tables, keys)


def choose_kernel(row, arrivals, axis, plan, *refs):
    if row is None:
        at, own, *refs = refs
        base = HEADER + at[0] * ROW
    else:
        own, *refs = refs
        base = HEADER + row * ROW
    came, outs = refs[: 2 * arrivals], refs[2 * arrivals :]
    for d in range(2):
        choice = plan[base + d]

        @pl.when(choice < STRETCH_DEV)
        def _(d=d, choice=choice):
            part = pl.ds(pl.multiple_of(choice * STRETCH, STRETCH), STRETCH)
            outs[d][...] = own[part, :] if axis == 0 else own[:, part]

        for i in range(arrivals):
            picked = choice == STRETCH_DEV + i if row is not None else choice >= STRETCH_DEV

            @pl.when(picked)
            def _(d=d, i=i):
                outs[d][...] = came[d * arrivals + i][...]


def choose(plan, row, own, axis, down, up):
    static = isinstance(row, int)
    shape = list(own.shape)
    shape[axis] = STRETCH
    block = jax.ShapeDtypeStruct(tuple(shape), own.dtype)
    return pl.pallas_call(
        functools.partial(choose_kernel, row if static else None, len(down), axis),
        out_shape=[block] * 2,
        in_specs=[SMEM] + ([] if static else [SMEM]) + [VMEM] * (1 + 2 * len(down)),
        out_specs=[VMEM] * 2,
        compiler_params=room(8),
        cost_estimate=pl.CostEstimate(flops=0, bytes_accessed=8 * block.size, transcendentals=0),
        name="choose",
    )(plan, *(() if static else (row,)), own, *down, *up)


def score(keys, queries):
    return jnp.dot(jnp.concatenate([keys, keys], axis=1), queries, preferred_element_type=jnp.float32)


def turn_queries_kernel(queries, split):
    for h in range(queries.shape[1] // HD):
        cols = pl.ds(h * HD, HD)
        for t in range(queries.shape[0] // TURN):
            at = pl.ds(t * TURN, TURN)
            turned = jnp.transpose(queries[at, cols].astype(jnp.float32) * EXPONENT)
            high = turned.astype(jnp.bfloat16)
            split[pl.ds(2 * h * HD, HD), at] = high
            split[pl.ds((2 * h + 1) * HD, HD), at] = (turned - high.astype(jnp.float32)).astype(jnp.bfloat16)


def turn_queries(queries):
    rows, columns = queries.shape
    return pl.pallas_call(
        turn_queries_kernel,
        out_shape=jax.ShapeDtypeStruct((2 * columns, rows), queries.dtype),
        in_specs=[VMEM],
        out_specs=VMEM,
        compiler_params=room(10),
        name="turn_queries",
    )(queries)


def text_kernel(queries, text_keys, text_values, acc, stat):
    ones = jnp.ones((ONES, text_keys.shape[0]), jnp.bfloat16)

    def stretch(t, c):
        at = pl.ds(pl.multiple_of(t * STRETCH, STRETCH), STRETCH)
        for h in range(text_keys.shape[1] // HD):
            cols = pl.ds(h * HD, HD)
            scores = score(text_keys[:, cols], queries[pl.ds(2 * h * HD, 2 * HD), at])
            peak = jnp.max(scores, axis=0, keepdims=True)
            both = jnp.dot(
                jnp.concatenate([text_values[cols, :], ones], axis=0),
                jnp.exp2(scores - peak).astype(jnp.bfloat16), preferred_element_type=jnp.float32,
            )
            acc[cols, at] = both[:HD]
            stat[16 * h : 16 * h + 1, at] = peak
            stat[16 * h + 8 : 16 * h + 9, at] = both[HD : HD + 1]
        return c

    lax.fori_loop(0, queries.shape[1] // STRETCH, stretch, 0)


def attend_text(queries, text_keys, text_values):
    columns, rows = queries.shape[0] // 2, queries.shape[1]
    return pl.pallas_call(
        text_kernel,
        out_shape=[
            jax.ShapeDtypeStruct((columns, rows), jnp.float32),
            jax.ShapeDtypeStruct((16 * (columns // HD), rows), jnp.float32),
        ],
        in_specs=[VMEM] * 3,
        out_specs=[VMEM] * 2,
        compiler_params=room(16),
        name="attend_text",
    )(queries, text_keys, text_values)


def turn_values_kernel(plan, values, text_values, values_out, text_out, down, up):
    for h in range(values.shape[1] // HD):
        cols = pl.ds(h * HD, HD)
        for source, target in ((values, values_out), (text_values, text_out)):
            for t in range(source.shape[0] // TURN):
                at = pl.ds(t * TURN, TURN)
                target[cols, at] = jnp.transpose(source[at, cols])
    for d, target in enumerate((down, up)):
        start = pl.multiple_of(plan[HEADER + d] * STRETCH, STRETCH)
        target[...] = values_out[:, pl.ds(start, STRETCH)]


def turn_values(plan, values, text_values):
    rows, columns = values.shape
    outs = [(columns, rows), (columns, text_values.shape[0]), (columns, STRETCH), (columns, STRETCH)]
    return pl.pallas_call(
        turn_values_kernel,
        out_shape=[jax.ShapeDtypeStruct(shape, values.dtype) for shape in outs],
        in_specs=[SMEM, VMEM, VMEM],
        out_specs=[VMEM] * 4,
        compiler_params=room(10),
        name="turn_values",
    )(plan, values, text_values)


def head(h):
    def part(start, size, by):
        return pl.ds(start if isinstance(h, int) else pl.multiple_of(start, by), size)

    return (
        part(h * HD, HD, HD), part(2 * h * HD, 2 * HD, 2 * HD), part(h * (HD + ONES), HD + ONES, ONES),
        part(16 * h, 1, 8), part(16 * h + 8, 1, 8),
    )


def attend_kernel(blocks, rowed, *refs):
    refs = list(refs)
    plan = refs.pop(0)
    base = HEADER + refs.pop(0)[0] * ROW if rowed else 0
    queries = refs.pop(0)
    block_refs = [(refs.pop(0), refs.pop(0)) for _ in blocks]
    acc_in, stat_in, acc, stat, keys_at, values_at, fine = refs
    rows = queries.shape[1]
    heads = queries.shape[0] // (2 * HD)
    wide = HD + ONES

    acc[...] = acc_in[...]
    stat[...] = stat_in[...]
    for h in range(heads):
        values_at[pl.ds(h * wide + HD, ONES), :] = jnp.ones((ONES, STRETCH), jnp.bfloat16)

    def step(start, twice):
        at = pl.ds(pl.multiple_of(start, STRETCH), STRETCH)

        lowest = jnp.ones((1, STRETCH), jnp.float32)
        scores = score(keys_at[:, head(0)[0]], queries[head(0)[1], at])
        for h in range(heads):
            cols, _, mixed, refer, total = head(h)
            following = None
            if h + 1 < heads:
                following = score(keys_at[:, head(h + 1)[0]], queries[head(h + 1)[1], at])
            weights = jnp.exp2(scores - (stat[refer, at] - twice)).astype(jnp.bfloat16)
            product = jnp.dot(values_at[mixed, :], weights, preferred_element_type=jnp.float32)
            mass = product[HD : HD + 1]
            fits = mass < GUARD
            acc[cols, at] = jnp.where(fits, acc[cols, at] + product[:HD], acc[cols, at])
            stat[total, at] += jnp.where(fits, mass, 0.0)
            fit = jnp.where(fits, 1.0, 0.0)
            fine[pl.ds(8 * h, 1), :] = fit
            lowest = jnp.minimum(lowest, fit)
            scores = following

        @pl.when(jnp.min(lowest) < 0.5)
        def _():
            parts = STRETCH // HD
            lax.fori_loop(
                0, heads * parts, lambda i, c: (again(start, i // parts, i % parts * HD, twice), c)[1], 0
            )

    def again(start, h, w, twice):
        at = pl.ds(pl.multiple_of(start + w, HD), HD)
        cols, both, mixed, refer, total = head(h)
        scores = score(keys_at[:, cols], queries[both, at])
        before = stat[refer, at]
        peak = jnp.maximum(jnp.max(scores, axis=0, keepdims=True), before)
        keep = jnp.exp2(before - peak)
        weights = jnp.exp2(scores - (peak - twice)).astype(jnp.bfloat16)
        product = jnp.dot(values_at[mixed, :], weights, preferred_element_type=jnp.float32)
        miss = fine[pl.ds(pl.multiple_of(8 * h, 8), 1), pl.ds(pl.multiple_of(w, HD), HD)] < 0.5
        mass = product[HD : HD + 1] + stat[total, at] * keep
        acc[cols, at] = jnp.where(miss, product[:HD] + acc[cols, at] * keep, acc[cols, at])
        stat[total, at] = jnp.where(miss, mass, stat[total, at])
        stat[refer, at] = jnp.where(miss, peak, before)

    def visit(b, c):
        place, stride = jnp.int32(0), jnp.int32(0)
        for number, (_, (first, second)) in enumerate(blocks):
            place = jnp.where(b == number, first, place)
            stride = jnp.where(b == number, second, stride)
        place = base + place

        @pl.when(plan[place] + plan[place + stride] > 0)
        def _():
            for number, (start, _) in enumerate(blocks):
                @pl.when(b == number)
                def _(start=start, number=number):
                    part = pl.ds(start, STRETCH)
                    keys_at[...] = block_refs[number][0][part, :]
                    for h in range(heads):
                        values_at[pl.ds(h * wide, HD), :] = block_refs[number][1][pl.ds(h * HD, HD), part]

            def stretch(t, c):
                times = plan[place + t * stride]

                @pl.when(times > 0)
                def _():
                    step(t * STRETCH, jnp.where(times > 1, 1.0, 0.0))

                return c

            lax.fori_loop(0, rows // STRETCH, stretch, 0)

        return c

    lax.fori_loop(0, len(blocks), visit, 0)


def attend(plan, row, queries, blocks, state):
    columns, rows = queries.shape[0] // 2, queries.shape[1]
    acc = jax.ShapeDtypeStruct((columns, rows), jnp.float32)
    stat = jax.ShapeDtypeStruct((16 * (columns // HD), rows), jnp.float32)
    scratch = [
        pltpu.VMEM((STRETCH, columns), queries.dtype),
        pltpu.VMEM((columns // HD * (HD + ONES), STRETCH), queries.dtype),
        pltpu.VMEM((8 * (columns // HD), STRETCH), jnp.float32),
    ]
    operands = [plan] + ([] if row is None else [row])
    smem = len(operands)
    operands.append(queries)
    for b in blocks:
        operands += [b[0], b[1]]
    operands += list(state)
    keys = len(blocks) * STRETCH
    return pl.pallas_call(
        functools.partial(attend_kernel, [tuple(b[2:]) for b in blocks], row is not None),
        out_shape=[acc, stat],
        in_specs=[SMEM] * smem + [VMEM] * (len(operands) - smem),
        out_specs=[VMEM] * 2,
        scratch_shapes=scratch,
        compiler_params=room(24),
        cost_estimate=pl.CostEstimate(
            flops=4 * rows * columns * keys, bytes_accessed=8 * rows * columns,
            transcendentals=rows * columns // HD * keys,
        ),
        name="attend",
    )(*operands)


def weigh_kernel(row, plan, queries, *refs):
    *key_refs, acc_in, stat_in, kept, acc, stat, keys_at, fine = refs
    columns, rows = acc.shape
    heads = columns // HD
    base = HEADER + row * ROW + 2
    acc[...] = acc_in[...]
    stat[...] = stat_in[...]

    def rows_of(d, h):
        return pl.ds(pl.multiple_of((d * heads + h) * STRETCH, STRETCH), STRETCH)

    def step(d, t, twice):
        start = t * STRETCH
        at = pl.ds(pl.multiple_of(start, STRETCH), STRETCH)
        lowest = jnp.ones((1, STRETCH), jnp.float32)
        scores = score(keys_at[:, head(0)[0]], queries[head(0)[1], at])
        for h in range(heads):
            _, _, _, refer, total = head(h)
            following = None
            if h + 1 < heads:
                following = score(keys_at[:, head(h + 1)[0]], queries[head(h + 1)[1], at])
            weights = jnp.exp2(scores - (stat[refer, at] - twice))
            kept[rows_of(d, h), at] = weights.astype(jnp.bfloat16)
            mass = jnp.sum(weights, axis=0, keepdims=True)
            fits = mass < GUARD
            stat[total, at] += jnp.where(fits, mass, 0.0)
            fit = jnp.where(fits, 1.0, 0.0)
            fine[pl.ds(8 * h, 1), :] = fit
            lowest = jnp.minimum(lowest, fit)
            scores = following

        @pl.when(jnp.min(lowest) < 0.5)
        def _():
            parts = STRETCH // HD
            lax.fori_loop(
                0, heads * parts, lambda i, c: (again(d, t, i // parts, i % parts * HD, twice), c)[1], 0
            )

    def again(d, t, h, w, twice):
        at = pl.ds(pl.multiple_of(t * STRETCH + w, HD), HD)
        cols, both, _, refer, total = head(h)
        scores = score(keys_at[:, cols], queries[both, at])
        before = stat[refer, at]
        peak = jnp.maximum(jnp.max(scores, axis=0, keepdims=True), before)
        miss = fine[pl.ds(pl.multiple_of(8 * h, 8), 1), pl.ds(pl.multiple_of(w, HD), HD)] < 0.5
        keep = jnp.where(miss, jnp.exp2(before - peak), 1.0)
        weights = jnp.exp2(scores - (peak - twice))
        mass = stat[total, at] * keep + jnp.where(miss, jnp.sum(weights, axis=0, keepdims=True), 0.0)
        acc[cols, at] = acc[cols, at] * keep
        stat[total, at] = mass
        stat[refer, at] = jnp.where(miss, peak, before)
        old = kept[rows_of(d, h), at].astype(jnp.float32)
        kept[rows_of(d, h), at] = jnp.where(miss, weights, old).astype(jnp.bfloat16)

        @pl.when((d > 0) & (plan[base + t] > 0))
        def _():
            earlier = kept[rows_of(0, h), at].astype(jnp.float32)
            kept[rows_of(0, h), at] = (earlier * keep).astype(jnp.bfloat16)

    def visit(d, c):
        @pl.when(plan[base + 2 * d] + plan[base + 2 * d + 1] > 0)
        def _():
            for number, ref in enumerate(key_refs):
                @pl.when(d == number)
                def _(ref=ref):
                    keys_at[...] = ref[...]

            def stretch(t, c):
                times = plan[base + 2 * d + t]

                @pl.when(times > 0)
                def _():
                    step(d, t, jnp.where(times > 1, 1.0, 0.0))

                return c

            lax.fori_loop(0, rows // STRETCH, stretch, 0)

        return c

    lax.fori_loop(0, len(key_refs), visit, 0)


def weigh(plan, row, queries, key_came, state):
    columns, rows = queries.shape[0] // 2, queries.shape[1]
    acc, stat = state
    heads = columns // HD
    keys = len(key_came) * STRETCH
    return pl.pallas_call(
        functools.partial(weigh_kernel, row),
        out_shape=[
            jax.ShapeDtypeStruct((heads * keys, rows), queries.dtype),
            jax.ShapeDtypeStruct(acc.shape, acc.dtype),
            jax.ShapeDtypeStruct(stat.shape, stat.dtype),
        ],
        in_specs=[SMEM] + [VMEM] * (3 + len(key_came)),
        out_specs=[VMEM] * 3,
        scratch_shapes=[
            pltpu.VMEM((STRETCH, columns), queries.dtype),
            pltpu.VMEM((8 * heads, STRETCH), jnp.float32),
        ],
        compiler_params=room(24),
        cost_estimate=pl.CostEstimate(
            flops=2 * rows * columns * keys, bytes_accessed=8 * rows * columns,
            transcendentals=rows * heads * keys,
        ),
        name="weigh",
    )(plan, queries, *key_came, acc, stat)


def finish_kernel(row, plan, kept, *refs):
    *value_refs, acc_in, stat, out, acc = refs
    columns, rows = acc.shape
    heads = columns // HD
    base = HEADER + row * ROW + 2

    def write(source, t):
        for h in range(heads):
            cols = pl.ds(h * HD, HD)
            for w in range(STRETCH // TURN):
                at = pl.ds(pl.multiple_of(t * STRETCH + w * TURN, TURN), TURN)
                share = 1.0 / stat[16 * h + 8 : 16 * h + 9, at]
                out[at, cols] = jnp.transpose((source[cols, at] * share).astype(out.dtype))

    def stretch(t, c):
        at = pl.ds(pl.multiple_of(t * STRETCH, STRETCH), STRETCH)
        live = sum(plan[base + 2 * d + t] for d in range(len(value_refs)))

        @pl.when(live == 0)
        def _():
            write(acc_in, t)

        @pl.when(live > 0)
        def _():
            acc[:, at] = acc_in[:, at]
            for d, values in enumerate(value_refs):
                @pl.when(plan[base + 2 * d + t] > 0)
                def _(d=d, values=values):
                    for h in range(heads):
                        cols = pl.ds(h * HD, HD)
                        acc[cols, at] += jnp.dot(
                            values[cols, :], kept[pl.ds((d * heads + h) * STRETCH, STRETCH), at],
                            preferred_element_type=jnp.float32,
                        )
            write(acc, t)

        return c

    lax.fori_loop(0, rows // STRETCH, stretch, 0)


def finish(plan, row, kept, value_came, state):
    acc, stat = state
    columns, rows = acc.shape
    return pl.pallas_call(
        functools.partial(finish_kernel, row),
        out_shape=jax.ShapeDtypeStruct((rows, columns), kept.dtype),
        in_specs=[SMEM] + [VMEM] * (3 + len(value_came)),
        out_specs=VMEM,
        scratch_shapes=[pltpu.VMEM(acc.shape, acc.dtype)],
        compiler_params=room(24),
        cost_estimate=pl.CostEstimate(
            flops=2 * columns * rows * STRETCH * len(value_came), bytes_accessed=8 * rows * columns, transcendentals=0
        ),
        name="finish",
    )(plan, kept, *value_came, acc, stat)


def own_blocks(keys, values):
    return [(keys, values, j * STRETCH, (1 + j, 2)) for j in range(STRETCH_DEV)]


def came_blocks(base, key_came, value_came):
    return [(key_came[d], value_came[d], 0, (base + 2 + 2 * d, 1)) for d in range(2)]


def send(down, up):
    last = lax.axis_size("seq") - 1
    from_above = lax.ppermute(down, "seq", [(i + 1, i) for i in range(last)])
    from_below = lax.ppermute(up, "seq", [(i, i + 1) for i in range(last)])
    return from_above, from_below


def exchange(rounds, plan, queries, keys, values, text_keys, text_values, key_first):
    key_here = send(*key_first)
    values, text_values, *value_first = turn_values(plan, values, text_values)
    queries = turn_queries(queries)
    value_first, queries = lax.optimization_barrier((value_first, queries))
    value_here = send(*value_first)
    state = attend_text(queries, text_keys, text_values)
    first_own, second_own = own_blocks(keys, values)
    key_came, value_came = ([], []), ([], [])

    def before(blocks):
        nonlocal state
        blocks, state = lax.optimization_barrier((blocks, state))
        return blocks

    for r in range(rounds - 1):
        key_here = before(key_here)
        for d in range(2):
            key_came[d].append(key_here[d])
        key_next = send(*before(choose(plan, r + 1, keys, 0, *key_came)))
        if r == 1:
            state = attend(plan, None, queries, [first_own], state)
        value_here = before(value_here)
        for d in range(2):
            value_came[d].append(value_here[d])
        came = came_blocks(HEADER + r * ROW, key_here, value_here)
        key_here, value_here = key_next, send(*before(choose(plan, r + 1, values, 1, *value_came)))
        blocks = came if r + 2 < rounds else [second_own] + came
        state = attend(plan, None, queries, blocks, state)
    kept, *state = weigh(plan, rounds - 1, queries, key_here, state)
    value_here, kept, state = lax.optimization_barrier((value_here, kept, state))
    return finish(plan, rounds - 1, kept, value_here, state)


def long_exchange(plan, queries, keys, values, text_keys, text_values, key_first):
    values, text_values, *value_first = turn_values(plan, values, text_values)
    queries = turn_queries(queries)
    state = attend_text(queries, text_keys, text_values)
    state = attend(plan, None, queries, own_blocks(keys, values), state)

    def body(carry):
        r, key_here, value_here, state = carry
        row = r.reshape(1)
        key_here = send(*choose(plan, row, keys, 0, [key_here[0]], [key_here[1]]))
        value_here = send(*choose(plan, row, values, 1, [value_here[0]], [value_here[1]]))
        state = attend(plan, row, queries, came_blocks(0, key_here, value_here), state)
        return (r + 1, key_here, value_here, state)

    carry = (jnp.int32(0), tuple(key_first), tuple(value_first), state)
    _, _, _, (acc, stat) = lax.while_loop(lambda c: c[0] < plan[5], body, carry)
    share = jnp.repeat(1.0 / stat[8::16], HD, axis=0)
    return jnp.transpose(acc * share).astype(queries.dtype)


def shards(
    queries, key_rows, value_rows, text_keys, text_values,
    shot_of_stretch, anchor_stretch, context_count, context_ids,
):
    groups = lax.axis_size("seq")
    tables = (shot_of_stretch, anchor_stretch, context_count, context_ids.T)
    plan, branch, key_down, key_up = make_plan(groups, tables, key_rows)
    branches = [functools.partial(exchange, rounds) for rounds in ROUNDS] + [long_exchange]
    return lax.switch(
        branch[0], branches, plan, queries, key_rows, value_rows, text_keys, text_values,
        (key_down, key_up),
    )


def solution(mesh):
    return jax.shard_map(
        shards,
        mesh=mesh,
        in_specs=(
            P(("rep", "seq"), "shot"),
            P(("rep", "seq"), "shot"),
            P(("rep", "seq"), "shot"),
            P("rep", "shot"),
            P("rep", "shot"),
            P("rep"),
            P("rep"),
            P("rep"),
            P("rep", None),
        ),
        out_specs=P(("rep", "seq"), "shot"),
        check_vma=False,
    )
```
